32 devices in a mesh: groups: 1, chan: 16 (over z, y, x), quarter: 2 (over core).
Axes of the slice: x: 2, y: 2, z: 4, core: 2. Of those that a mesh axis runs over, the one named last changes fastest.
Arguments:
- pair: bfloat16 [384, 384, 128], P(('groups', 'chan', 'quarter')), may hold values from -6 to 6
- norm_gain: float32 [128], replicated, may hold values from 0.25 to 1.75
- norm_shift: float32 [128], replicated, may hold values from -3 to 3
- factor_weight: bfloat16 [128, 512], replicated, may hold values from -0.5 to 0.5
- factor_bias: float32 [512], replicated, may hold values from -3 to 3
- gate_weight: bfloat16 [128, 128], replicated, may hold values from -0.5 to 0.5
- gate_bias: float32 [128], replicated, may hold values from -3 to 3
- center_gain: float32 [128], replicated, may hold values from 0.25 to 1.75
- center_shift: float32 [128], replicated, may hold values from -3 to 3
- out_weight: bfloat16 [128, 128], replicated, may hold values from -0.5 to 0.5
- out_bias: float32 [128], replicated, may hold values from -3 to 3
Outputs:
- update: bfloat16 [384, 384, 128], P(('groups', 'chan', 'quarter'))
The draws below stay inside these ranges and needn't reach their ends.
All inputs are finite; a program needn't handle non-finite values.
Results may differ from the reference program's by a relative error of at most 0.0057.
Values may be sent and summed in bfloat16 or wider, within the bound.
No kernel may reach another device: no remote copies, remote signals or barrier semaphores. Data moves between devices by JAX's collectives and lax.ppermute only.
A program may use at most 128 MiB of HBM per device.

```python
import jax
import jax.numpy as jnp
from jax import lax

PAIR = 128
HIDDEN_SIZE = 128
RESIDUES = 384


def levels(own_key, shape, split, smallest, high):
    def one(position, parts):
        steps = jax.random.uniform(jax.random.fold_in(jax.random.fold_in(own_key, 6), position), (parts,), jnp.float32, smallest / len(split), high / len(split))
        return jnp.repeat(jnp.exp(steps), shape[position] // parts).reshape((-1,) + (1,) * (len(shape) - position - 1))

    level = one(*split[0])
    for cut in split[1:]:
        level = level * one(*cut)
    return level


def scatter_about(rng, dims, spread, reach, split=(), held_as=jnp.bfloat16):
    level = levels(rng, dims, split, -0.22, 0.18) if split else 1.0
    entries = jax.random.normal(rng, dims, jnp.float32) * spread * level
    return jnp.minimum(jnp.maximum(entries, -reach), reach).astype(held_as)


def setup_inputs(seed: int = 0, part: int = 0) -> dict:
    arg_keys = jax.random.split(jax.random.key(seed), 12)
    part_keys = jax.random.split(jax.random.fold_in(arg_keys[11], part), 12)
    return {
        "pair": scatter_about(part_keys[0], (RESIDUES, RESIDUES, PAIR), 1.0, 6.0, ((0, 32),)),
        "norm_gain": jnp.clip(1.0 + 0.15 * jax.random.normal(arg_keys[1], (PAIR,), jnp.float32), 0.25, 1.75),
        "norm_shift": scatter_about(arg_keys[2], (PAIR,), 0.5, 3.0, (), jnp.float32),
        "factor_weight": scatter_about(arg_keys[3], (PAIR, 4 * HIDDEN_SIZE), PAIR ** -0.5, 0.5),
        "factor_bias": scatter_about(arg_keys[4], (4 * HIDDEN_SIZE,), 0.5, 3.0, (), jnp.float32),
        "gate_weight": scatter_about(arg_keys[5], (PAIR, PAIR), PAIR ** -0.5, 0.5),
        "gate_bias": scatter_about(arg_keys[6], (PAIR,), 0.5, 3.0, (), jnp.float32),
        "center_gain": jnp.clip(1.0 + 0.15 * jax.random.normal(arg_keys[7], (HIDDEN_SIZE,), jnp.float32), 0.25, 1.75),
        "center_shift": scatter_about(arg_keys[8], (HIDDEN_SIZE,), 0.5, 3.0, (), jnp.float32),
        "out_weight": scatter_about(arg_keys[9], (HIDDEN_SIZE, PAIR), HIDDEN_SIZE ** -0.5, 0.5),
        "out_bias": scatter_about(arg_keys[10], (PAIR,), 0.5, 3.0, (), jnp.float32),
    }


epsilon = 1e-05

def normalize(values, gain, shift, axis):
    average = lax.optimization_barrier(jnp.mean(values, axis=axis, keepdims=True))
    centered = values - average
    variance = lax.optimization_barrier(jnp.mean(centered * centered, axis=axis, keepdims=True))
    return centered * lax.rsqrt(variance + epsilon) * gain + shift

def reference(pair, norm_gain, norm_shift, factor_weight, factor_bias, gate_weight, gate_bias, center_gain, center_shift, out_weight, out_bias):

    def factor_row(row):
        normed = normalize(row.astype(jnp.float32), norm_gain, norm_shift, 1).astype(jnp.bfloat16)
        projected = jnp.dot(normed, factor_weight, preferred_element_type=jnp.float32) + factor_bias
        left = jax.nn.sigmoid(projected[:, :HIDDEN_SIZE]) * projected[:, HIDDEN_SIZE:2 * HIDDEN_SIZE]
        right = jax.nn.sigmoid(projected[:, 2 * HIDDEN_SIZE:3 * HIDDEN_SIZE]) * projected[:, 3 * HIDDEN_SIZE:]
        return (left.astype(jnp.bfloat16), right.astype(jnp.bfloat16))
    left_rows, right_rows = lax.map(factor_row, pair)
    left = jnp.transpose(left_rows, (2, 0, 1))
    right = jnp.transpose(right_rows, (2, 0, 1))

    def channel_product(operands):
        one_left, one_right = operands
        result = jnp.dot(one_left.astype(jnp.float32), one_right.astype(jnp.float32).T, precision=lax.Precision.HIGHEST, preferred_element_type=jnp.float32)
        return result.astype(jnp.bfloat16)
    product = lax.map(channel_product, (left, right))

    def output_row(operands):
        row, column = operands
        normed = normalize(row.astype(jnp.float32), norm_gain, norm_shift, 1).astype(jnp.bfloat16)
        gate = jax.nn.sigmoid(jnp.dot(normed, gate_weight, preferred_element_type=jnp.float32) + gate_bias)
        centered = normalize(column.astype(jnp.float32), center_gain[:, None], center_shift[:, None], 0).astype(jnp.bfloat16)
        projected = jnp.dot(centered.T, out_weight, preferred_element_type=jnp.float32) + out_bias
        return (gate * projected).astype(jnp.bfloat16)
    return lax.map(output_row, (pair, jnp.transpose(product, (1, 0, 2))))
```

```python
import functools

import jax
import jax.numpy as jnp
from jax import lax
from jax.experimental import pallas as pl
from jax.experimental.pallas import tpu as pltpu
from jax.sharding import Mesh
from jax.sharding import PartitionSpec as P

epsilon = 1e-05
BLOCK = 8
PAIRED = 2
LANES = 128
VMEM = 48 * 1024 * 1024

f32, bf16 = jnp.float32, jnp.bfloat16


def sigmoid(x):
    return 0.5 * jnp.tanh(0.5 * x) + 0.5


def dot(a, b):
    return jnp.dot(a, b, preferred_element_type=f32)


def dot_nt(a, b):
    return lax.dot_general(a, b, (((1,), (1,)), ((), ())), preferred_element_type=f32)


def column(row):
    blocks = [
        jnp.broadcast_to(row[:, k : k + LANES], (LANES, LANES)).T
        for k in range(0, row.shape[1], LANES)
    ]
    return jnp.concatenate(blocks, axis=0) if len(blocks) > 1 else blocks[0]


def widen(col, width):
    return jnp.concatenate([col] * (width // LANES), axis=1)


def shuffle(groups, size):
    n = groups * size
    out = lax.broadcasted_iota(jnp.int32, (n, n), 0)
    row = lax.broadcasted_iota(jnp.int32, (n, n), 1)
    want = (out % size) * groups + out // size
    return jnp.where(want == row, 1.0, 0.0).astype(bf16)


def factor(normed, wt, bias):
    width = wt.shape[0] // 2
    lanes = normed.shape[0]
    gate = dot_nt(wt[:width], normed) + widen(bias[:width], lanes)
    value = dot_nt(wt[width:], normed) + widen(bias[width:], lanes)
    return sigmoid(gate) * value


def as_rows(values, k):
    hosts = values.shape[0] // BLOCK
    return jnp.concatenate(
        [values[:, r * k : (r + 1) * k].reshape(hosts, BLOCK, k) for r in range(PAIRED)], axis=1
    )


def right_kernel(pair_ref, gain_ref, shift_ref, w_ref, b_ref, right_ref, normed_ref, wt, bt):
    @pl.when(pl.program_id(0) == 0)
    def _():
        wt[...] = w_ref[...].T
        bt[...] = column(b_ref[...])

    k, width = pair_ref.shape[1:]
    x = pair_ref[...].astype(f32).reshape(PAIRED * k, width)
    centered = x - jnp.mean(x, axis=1, keepdims=True)
    variance = jnp.mean(centered * centered, axis=1, keepdims=True)
    normed = centered * lax.rsqrt(variance + epsilon) * gain_ref[...] + shift_ref[...]
    normed = normed.astype(bf16)
    normed_ref[...] = normed.reshape(PAIRED, k, width)
    out = as_rows(factor(normed, wt[...], bt[...]), k).astype(bf16)
    for p in range(right_ref.shape[0]):
        right_ref[p] = out


def left_kernel(normed_ref, w_ref, b_ref, gw_ref, gb_ref, left_ref, gate_ref, wt, bt):
    @pl.when(pl.program_id(0) == 0)
    def _():
        wt[...] = w_ref[...].T
        bt[...] = column(b_ref[...])

    k, width = normed_ref.shape[1:]
    normed = normed_ref[...].reshape(PAIRED * k, width)
    left_ref[...] = as_rows(factor(normed, wt[...], bt[...]), k).astype(bf16)
    gate = sigmoid(dot(normed, gw_ref[...]) + gb_ref[...])
    gate_ref[...] = gate.reshape(gate_ref.shape).astype(gate_ref.dtype)


def regroup(source, target, matrix, size):
    for s in range(source.shape[0] // (BLOCK * size)):
        rows = source[s * BLOCK * size : (s + 1) * BLOCK * size, :]
        moved = dot(matrix, rows).astype(bf16)
        for c in range(BLOCK):
            target[c, s * size : (s + 1) * size, :] = moved[c * size : (c + 1) * size]


def product_kernel(left_ref, right_ref, out_ref, left, right, held):
    size = 32
    matrix = shuffle(BLOCK, size)
    back = shuffle(size, BLOCK)

    @pl.when(pl.program_id(0) == 0)
    def _():
        regroup(left_ref, left, matrix, size)

    regroup(right_ref, right, matrix, size)
    for c in range(BLOCK):
        held[c] = dot_nt(left[c], right[c]).astype(bf16)
    for s in range(left.shape[1] // size):
        rows = jnp.concatenate([held[c, s * size : (s + 1) * size, :] for c in range(BLOCK)], axis=0)
        out_ref[s * BLOCK * size : (s + 1) * BLOCK * size, :] = dot(back, rows).astype(bf16)


def final_kernel(x_ref, gate_ref, g_ref, s_ref, w_ref, b_ref, out_ref, gt, st):
    @pl.when(pl.program_id(0) == 0)
    def _():
        gt[...] = column(g_ref[...])
        st[...] = column(s_ref[...])

    hosts, _, j = x_ref.shape
    width = hosts * BLOCK
    for r in range(PAIRED):
        x = x_ref[...].astype(f32)[:, r * BLOCK : (r + 1) * BLOCK].reshape(width, j)
        centered = x - jnp.mean(x, axis=0, keepdims=True)
        variance = jnp.mean(centered * centered, axis=0, keepdims=True)
        normed = centered * lax.rsqrt(variance + epsilon) * widen(gt[...], j) + widen(st[...], j)
        outward = dot(normed.T.astype(bf16), w_ref[...]) + b_ref[...]
        out_ref[r] = (gate_ref[r].astype(f32) * outward).astype(bf16)


def whole(shape):
    return pl.BlockSpec(shape, lambda s: (0,) * len(shape))


def params():
    return pltpu.CompilerParams(vmem_limit_bytes=VMEM)


def shards(parts, pair, norm_gain, norm_shift, factor_weight, factor_bias, gate_weight, gate_bias,
           center_gain, center_shift, out_weight, out_bias):
    rows, k, width = pair.shape
    hidden = out_weight.shape[0]
    hosts = hidden // BLOCK
    steps = rows // PAIRED
    tall = PAIRED * BLOCK
    in_part = ("chan", "quarter")
    row = lambda v: v.reshape(1, -1)
    row_block = pl.BlockSpec((PAIRED, k, width), lambda s: (s, 0, 0))

    right, normed = pl.pallas_call(
        right_kernel,
        grid=(steps,),
        in_specs=[
            row_block,
            whole((1, width)),
            whole((1, width)),
            pl.BlockSpec((width, 2 * hidden), lambda s: (0, 1)),
            pl.BlockSpec((1, 2 * hidden), lambda s: (0, 1)),
        ],
        out_specs=[
            pl.BlockSpec((parts, hosts, tall, k), lambda s: (0, 0, s, 0)),
            row_block,
        ],
        out_shape=[
            jax.ShapeDtypeStruct((parts, hosts, rows * BLOCK, k), bf16),
            jax.ShapeDtypeStruct(pair.shape, bf16),
        ],
        scratch_shapes=[pltpu.VMEM((2 * hidden, width), bf16), pltpu.VMEM((2 * hidden, LANES), f32)],
        compiler_params=params(),
        name="right_factor",
    )(pair, row(norm_gain), row(norm_shift), factor_weight, row(factor_bias))
    right = lax.all_to_all(
        right.reshape(parts * hosts, rows * BLOCK, k), ("part",) + in_part, 0, 0, tiled=True
    )

    left, gate = pl.pallas_call(
        left_kernel,
        grid=(steps,),
        in_specs=[
            row_block,
            pl.BlockSpec((width, 2 * hidden), lambda s: (0, 0)),
            pl.BlockSpec((1, 2 * hidden), lambda s: (0, 0)),
            whole((width, width)),
            whole((1, width)),
        ],
        out_specs=[pl.BlockSpec((hosts, tall, k), lambda s: (0, s, 0)), row_block],
        out_shape=[
            jax.ShapeDtypeStruct((hosts, rows * BLOCK, k), bf16),
            jax.ShapeDtypeStruct(pair.shape, bf16),
        ],
        scratch_shapes=[pltpu.VMEM((2 * hidden, width), bf16), pltpu.VMEM((2 * hidden, LANES), f32)],
        compiler_params=params(),
        name="left_factor",
    )(normed, factor_weight, row(factor_bias), gate_weight, row(gate_bias))
    left = lax.all_to_all(left, in_part, 0, 0, tiled=True)

    mine = hosts * rows
    full = parts * mine
    product = pl.pallas_call(
        product_kernel,
        grid=(full // LANES,),
        in_specs=[
            whole((mine * BLOCK, k)),
            pl.BlockSpec((LANES * BLOCK, k), lambda s: (s, 0)),
        ],
        out_specs=pl.BlockSpec((mine * BLOCK, LANES), lambda s: (0, s)),
        out_shape=jax.ShapeDtypeStruct((mine * BLOCK, full), bf16),
        scratch_shapes=[
            pltpu.VMEM((BLOCK, mine, k), bf16),
            pltpu.VMEM((BLOCK, LANES, k), bf16),
            pltpu.VMEM((BLOCK, mine, LANES), bf16),
        ],
        compiler_params=params(),
        name="products",
    )(left.reshape(mine * BLOCK, k), right.reshape(full * BLOCK, k))
    product = lax.all_to_all(product.reshape(hosts, rows * BLOCK, full), in_part, 0, 0, tiled=True)

    return pl.pallas_call(
        final_kernel,
        grid=(steps,),
        in_specs=[
            pl.BlockSpec((hosts, tall, full), lambda s: (0, s, 0)),
            row_block,
            whole((1, hidden)),
            whole((1, hidden)),
            whole((hidden, width)),
            whole((1, width)),
        ],
        out_specs=row_block,
        out_shape=jax.ShapeDtypeStruct(pair.shape, bf16),
        scratch_shapes=[pltpu.VMEM((hidden, LANES), f32), pltpu.VMEM((hidden, LANES), f32)],
        compiler_params=params(),
        name="update",
    )(product, gate, row(center_gain), row(center_shift), out_weight, row(out_bias))


def solution(mesh):
    groups, chan, quarter = (mesh.shape[a] for a in ("groups", "chan", "quarter"))
    near = 128 // BLOCK // quarter
    parts = chan // near
    split = Mesh(
        mesh.devices.reshape(groups, parts, near, quarter), ("groups", "part", "chan", "quarter")
    )
    rows = P(("groups", "part", "chan", "quarter"), None, None)
    return jax.shard_map(
        functools.partial(shards, parts),
        mesh=split,
        in_specs=(rows,) + (P(),) * 10,
        out_specs=rows,
        check_vma=False,
    )
```

```python
import functools

import jax
import jax.numpy as jnp
from jax import lax
from jax.experimental import pallas as pl
from jax.experimental.pallas import tpu as pltpu
from jax.sharding import Mesh
from jax.sharding import PartitionSpec as P

epsilon = 1e-05
CHANNELS = 128
BLOCK = 8
STEP = 4
SIZE = 32
LANES = 128
TAIL = 64
MIB = 1024 * 1024

f32, bf16 = jnp.float32, jnp.bfloat16


def sigmoid(x):
    return 0.5 * jnp.tanh(0.5 * x) + 0.5


def dot(a, b):
    return jnp.dot(a, b, preferred_element_type=f32)


def dot_nt(a, b):
    return lax.dot_general(a, b, (((1,), (1,)), ((), ())), preferred_element_type=f32)


def column(row):
    blocks = [
        jnp.broadcast_to(row[:, k : k + LANES], (LANES, LANES)).T
        for k in range(0, row.shape[1], LANES)
    ]
    return jnp.concatenate(blocks, axis=0)


def widen(col, width):
    return jnp.concatenate([col] * (width // LANES), axis=1)


def shuffle(groups, size):
    n = groups * size
    out = lax.broadcasted_iota(jnp.int32, (n, n), 0)
    row = lax.broadcasted_iota(jnp.int32, (n, n), 1)
    want = (out % size) * groups + out // size
    return jnp.where(want == row, 1.0, 0.0).astype(bf16)


def normalize(x, gain, shift):
    centered = x - jnp.mean(x, axis=1, keepdims=True)
    variance = jnp.mean(centered * centered, axis=1, keepdims=True)
    return (centered * lax.rsqrt(variance + epsilon) * gain + shift).astype(bf16)


def factor(normed, wt, bias):
    width = wt.shape[0] // 2
    lanes = normed.shape[0]
    gate = dot_nt(wt[:width], normed) + widen(bias[:width], lanes)
    value = dot_nt(wt[width:], normed) + widen(bias[width:], lanes)
    return sigmoid(gate) * value


def as_rows(values, k):
    hosts = values.shape[0] // BLOCK
    return jnp.concatenate(
        [values[:, r * k : (r + 1) * k].reshape(hosts, BLOCK, k) for r in range(STEP)], axis=1
    )


def right_kernel(pair_ref, gain_ref, shift_ref, w_ref, b_ref, *refs):
    wf, bf, wt, bt = refs[-4:]
    normed_ref = refs[-5]
    outs = refs[:-5]
    k, width = pair_ref.shape[1:]
    hidden = w_ref.shape[1] // 2

    @pl.when(pl.program_id(0) == 0)
    def _():
        wf[...] = w_ref[...].astype(f32).T
        bf[...] = column(b_ref[...])
        host = lax.axis_index(("chan", "quarter"))
        for half in range(2):
            for b in range(0, len(outs), 2):
                source = [
                    pl.ds(pl.multiple_of(half * hidden + (host ^ (b + n)) * BLOCK, BLOCK), BLOCK)
                    for n in range(2)
                ]
                target = slice(half * hidden + b * BLOCK, half * hidden + (b + 2) * BLOCK)
                wt[target] = jnp.concatenate([wf[s] for s in source], axis=0).astype(bf16)
                bt[target] = jnp.concatenate([bf[s] for s in source], axis=0)

    x = pair_ref[...].astype(f32).reshape(STEP * k, width)
    normed = normalize(x, gain_ref[...], shift_ref[...])
    normed_ref[...] = normed.reshape(STEP, k, width)
    rows = as_rows(factor(normed, wt[...], bt[...]), k).astype(bf16)
    for b, out in enumerate(outs):
        out[...] = rows[b]


def left_kernel(normed_ref, w_ref, b_ref, left_ref, wt, bt):
    @pl.when(pl.program_id(0) == 0)
    def _():
        wt[...] = w_ref[...].astype(f32).T.astype(bf16)
        bt[...] = column(b_ref[...])

    k, width = normed_ref.shape[1:]
    normed = normed_ref[...].reshape(STEP * k, width)
    left_ref[...] = as_rows(factor(normed, wt[...], bt[...]), k).astype(bf16)


def gate_kernel(normed_ref, gw_ref, gb_ref, gate_ref):
    k, width = normed_ref.shape[1:]
    normed = normed_ref[...].reshape(STEP * k, width)
    gate = sigmoid(dot(normed, gw_ref[...]) + gb_ref[...])
    gate_ref[...] = gate.reshape(gate_ref.shape).astype(gate_ref.dtype)


def regroup(source, target, matrix):
    for s in range(source.shape[0] // (BLOCK * SIZE)):
        rows = source[s * BLOCK * SIZE : (s + 1) * BLOCK * SIZE, :]
        moved = dot(matrix, rows).astype(bf16)
        for c in range(BLOCK):
            target[c, s * SIZE : (s + 1) * SIZE, :] = moved[c * SIZE : (c + 1) * SIZE]


def product_kernel(hosts, left_ref, *refs):
    rights = refs[:hosts]
    out_ref, arrived, left, right, held, sems = refs[hosts:]
    tall = rights[0].shape[0]
    rows = tall // BLOCK
    host = lax.axis_index(("chan", "quarter"))
    copies = []
    for b, ref in enumerate(rights):
        start = pl.multiple_of((host ^ b) * tall, 16)
        copies.append(pltpu.make_async_copy(ref, arrived.at[pl.ds(start, tall)], sems.at[b]))
        copies[-1].start()
    matrix = shuffle(BLOCK, SIZE)
    back = shuffle(SIZE, BLOCK)
    regroup(left_ref, left, matrix)
    for copy in copies:
        copy.wait()
    regroup(arrived, right, matrix)
    for c in range(BLOCK):
        held[c] = dot_nt(left[c], right[c]).astype(bf16)
    span = held.shape[2]
    main = span - TAIL
    for s in range(left.shape[1] // SIZE):
        parts = jnp.concatenate([held[c, s * SIZE : (s + 1) * SIZE, :] for c in range(BLOCK)], axis=0)
        moved = dot(back, parts)
        ends = moved[:, main:].reshape(SIZE // 2, 2, BLOCK, TAIL)
        ends = jnp.concatenate([ends[:, 0], ends[:, 1]], axis=2).reshape(SIZE * BLOCK // 2, LANES)
        moved, ends = moved[:, :main].astype(bf16), ends.astype(bf16)
        for i in range(0, SIZE, STEP):
            to, at = divmod(s * SIZE + i, rows)
            out_ref[to, at * BLOCK : (at + STEP) * BLOCK, :] = moved[i * BLOCK : (i + STEP) * BLOCK]
            low = tall + at * BLOCK // 2
            out_ref[to, low : low + STEP * BLOCK // 2, :] = ends[
                i * BLOCK // 2 : (i + STEP) * BLOCK // 2
            ]


def final_kernel(parts, *refs):
    products = refs[:parts]
    gate_ref, g_ref, s_ref, w_ref, b_ref, out_ref, gt, st = refs[parts:]
    step = pl.program_id(0)

    @pl.when(step == 0)
    def _():
        gt[...] = column(g_ref[...])
        st[...] = column(s_ref[...])

    part = lax.axis_index("part")
    hosts, tall, _ = products[0].shape
    tall = tall * 2 // 3
    span = gate_ref.shape[1] // parts
    main = span - TAIL
    width = hosts * BLOCK
    for a, ref in enumerate(products):
        first = pl.multiple_of(lax.rem(part + parts - a, parts) * span, 16)
        whole = ref[:, pl.ds(pl.multiple_of(step * STEP * BLOCK, 16), STEP * BLOCK), :].astype(f32)
        low = pl.multiple_of(tall + step * (STEP * BLOCK // 2), 16)
        ends = ref[:, pl.ds(low, STEP * BLOCK // 2), :].astype(f32)
        blocks = [whole[:, r * BLOCK : (r + 1) * BLOCK].reshape(width, LANES) for r in range(STEP)]
        blocks += [
            ends[:, r * BLOCK : (r + 1) * BLOCK].reshape(width, LANES) for r in range(STEP // 2)
        ]
        x = jnp.concatenate(blocks, axis=1)
        centered = x - jnp.mean(x, axis=0, keepdims=True)
        variance = jnp.mean(centered * centered, axis=0, keepdims=True)
        normed = centered * lax.rsqrt(variance + epsilon)
        normed = normed * widen(gt[...], x.shape[1]) + widen(st[...], x.shape[1])
        outward = dot(normed.T.astype(bf16), w_ref[...]) + b_ref[...]
        for r in range(STEP):
            at = pl.ds(first, main)
            value = outward[r * LANES : (r + 1) * LANES]
            out_ref[r, at, :] = (gate_ref[r, at, :].astype(f32) * value).astype(bf16)
            at = pl.ds(pl.multiple_of(first + main, 16), TAIL)
            low = STEP * LANES + r * TAIL
            value = outward[low : low + TAIL]
            out_ref[r, at, :] = (gate_ref[r, at, :].astype(f32) * value).astype(bf16)


def whole(shape):
    return pl.BlockSpec(shape, lambda s: (0,) * len(shape))


def cost(flops, size):
    return pl.CostEstimate(flops=flops, bytes_accessed=size, transcendentals=0)


def params(mib=32):
    return pltpu.CompilerParams(vmem_limit_bytes=mib * MIB)


def shards(parts, pair, norm_gain, norm_shift, factor_weight, factor_bias, gate_weight, gate_bias,
           center_gain, center_shift, out_weight, out_bias):
    rows, k, width = pair.shape
    hidden = out_weight.shape[0]
    hosts = hidden // BLOCK
    steps = rows // STEP
    tall = rows * BLOCK
    mine = hosts * rows
    in_part = ("chan", "quarter")
    everywhere = ("part",) + in_part
    row = lambda v: v.reshape(1, -1)
    row_block = pl.BlockSpec((STEP, k, width), lambda s: (s, 0, 0))
    factor_block = lambda n: [
        pl.BlockSpec((width, 2 * hidden), lambda s: (0, n)),
        pl.BlockSpec((1, 2 * hidden), lambda s: (0, n)),
    ]
    work = rows * k * width

    *rights, normed = pl.pallas_call(
        right_kernel,
        grid=(steps,),
        in_specs=[row_block, whole((1, width)), whole((1, width))] + factor_block(1),
        out_specs=[pl.BlockSpec((STEP * BLOCK, k), lambda s: (s, 0))] * hosts + [row_block],
        out_shape=[jax.ShapeDtypeStruct((tall, k), bf16)] * hosts
        + [jax.ShapeDtypeStruct(pair.shape, bf16)],
        scratch_shapes=[
            pltpu.VMEM((2 * hidden, width), f32),
            pltpu.VMEM((2 * hidden, LANES), f32),
            pltpu.VMEM((2 * hidden, width), bf16),
            pltpu.VMEM((2 * hidden, LANES), f32),
        ],
        compiler_params=params(60),
        cost_estimate=cost(4 * work * hidden, 6 * work),
        name="right_factor",
    )(pair, row(norm_gain), row(norm_shift), factor_weight, row(factor_bias))

    def send(a, b):
        if a == 0 and b == 0:
            return rights[0]
        pairs = [
            (p * hosts + h, (p + a) % parts * hosts + (h ^ b))
            for p in range(parts)
            for h in range(hosts)
        ]
        return lax.ppermute(rights[b], everywhere, pairs)

    arrived = {}
    order = [(a, b) for b in range(hosts) for a in range(parts)]
    for a, b in order:
        arrived[a, b] = send(a, b)

    left = pl.pallas_call(
        left_kernel,
        grid=(steps,),
        in_specs=[row_block] + factor_block(0),
        out_specs=pl.BlockSpec((hosts, STEP * BLOCK, k), lambda s: (0, s, 0)),
        out_shape=jax.ShapeDtypeStruct((hosts, tall, k), bf16),
        scratch_shapes=[pltpu.VMEM((2 * hidden, width), bf16), pltpu.VMEM((2 * hidden, LANES), f32)],
        compiler_params=params(),
        cost_estimate=cost(4 * work * hidden, 4 * work),
        name="left_factor",
    )(normed, factor_weight, row(factor_bias))
    left = lax.all_to_all(left, in_part, 0, 0, tiled=True).reshape(mine * BLOCK, k)

    gate = pl.pallas_call(
        gate_kernel,
        grid=(steps,),
        in_specs=[row_block, whole((width, width)), whole((1, width))],
        out_specs=row_block,
        out_shape=jax.ShapeDtypeStruct(pair.shape, bf16),
        compiler_params=params(),
        cost_estimate=cost(2 * work * width, 4 * work),
        name="gate",
    )(normed, gate_weight, row(gate_bias))

    products = []
    for a in range(parts):
        product = pl.pallas_call(
            functools.partial(product_kernel, hosts),
            in_specs=[pl.BlockSpec(memory_space=pltpu.VMEM)]
            + [pl.BlockSpec(memory_space=pl.ANY)] * hosts,
            out_specs=pl.BlockSpec(memory_space=pltpu.VMEM),
            out_shape=jax.ShapeDtypeStruct((hosts, tall * 3 // 2, LANES), bf16),
            scratch_shapes=[
                pltpu.VMEM((mine * BLOCK, k), bf16),
                pltpu.VMEM((BLOCK, mine, k), bf16),
                pltpu.VMEM((BLOCK, mine, k), bf16),
                pltpu.VMEM((BLOCK, mine, mine), bf16),
                pltpu.SemaphoreType.DMA((hosts,)),
            ],
            compiler_params=params(),
            cost_estimate=cost(2 * BLOCK * mine * mine * k, 6 * BLOCK * mine * k),
            name="products",
        )(left, *[arrived[a, b] for b in range(hosts)])
        products.append(lax.all_to_all(product, in_part, 0, 0, tiled=True))

    return pl.pallas_call(
        functools.partial(final_kernel, parts),
        grid=(steps,),
        in_specs=[whole(products[0].shape)] * parts
        + [row_block, whole((1, hidden)), whole((1, hidden)), whole((hidden, width)), whole((1, width))],
        out_specs=row_block,
        out_shape=jax.ShapeDtypeStruct(pair.shape, bf16),
        scratch_shapes=[pltpu.VMEM((hidden, LANES), f32), pltpu.VMEM((hidden, LANES), f32)],
        compiler_params=params(),
        cost_estimate=cost(2 * work * width, 6 * work),
        name="update",
    )(*products, gate, row(center_gain), row(center_shift), out_weight, row(out_bias))


def solution(mesh):
    groups, chan, quarter = (mesh.shape[a] for a in ("groups", "chan", "quarter"))
    near = CHANNELS // BLOCK // quarter
    parts = chan // near
    split = Mesh(
        mesh.devices.reshape(groups, parts, near, quarter), ("groups", "part", "chan", "quarter")
    )
    rows = P(("groups", "part", "chan", "quarter"), None, None)
    return jax.shard_map(
        functools.partial(shards, parts),
        mesh=split,
        in_specs=(rows,) + (P(),) * 10,
        out_specs=rows,
        check_vma=False,
    )
```

```python
import functools

import jax
import jax.numpy as jnp
from jax import lax
from jax.experimental import pallas as pl
from jax.experimental.pallas import tpu as pltpu
from jax.sharding import Mesh
from jax.sharding import PartitionSpec as P

epsilon = 1e-05
CHANNELS = 128
BLOCK = 8
STEP = 4
SIZE = 32
LANES = 128
EARLY = 8
GATHER = 32
MIB = 1024 * 1024

f32, bf16 = jnp.float32, jnp.bfloat16


def sigmoid(x):
    return 0.5 * jnp.tanh(0.5 * x) + 0.5


def dot(a, b):
    return jnp.dot(a, b, preferred_element_type=f32)


def dot_nt(a, b):
    return lax.dot_general(a, b, (((1,), (1,)), ((), ())), preferred_element_type=f32)


def column(row):
    blocks = [
        jnp.broadcast_to(row[:, k : k + LANES], (LANES, LANES)).T
        for k in range(0, row.shape[1], LANES)
    ]
    return jnp.concatenate(blocks, axis=0)


def widen(col, width):
    return jnp.concatenate([col] * (width // LANES), axis=1)


def shuffle(groups, size):
    n = groups * size
    out = lax.broadcasted_iota(jnp.int32, (n, n), 0)
    row = lax.broadcasted_iota(jnp.int32, (n, n), 1)
    want = (out % size) * groups + out // size
    return jnp.where(want == row, 1.0, 0.0).astype(bf16)


def normalize(x, gain, shift):
    centered = x - jnp.mean(x, axis=1, keepdims=True)
    variance = jnp.mean(centered * centered, axis=1, keepdims=True)
    return (centered * lax.rsqrt(variance + epsilon) * gain + shift).astype(bf16)


def factor(normed, wt, bias):
    width = wt.shape[0] // 2
    lanes = normed.shape[0]
    gate = dot_nt(wt[:width], normed) + widen(bias[:width], lanes)
    value = dot_nt(wt[width:], normed) + widen(bias[width:], lanes)
    return sigmoid(gate) * value


def as_rows(values, k):
    hosts = values.shape[0] // BLOCK
    return jnp.concatenate(
        [values[:, r * k : (r + 1) * k].reshape(hosts, BLOCK, k) for r in range(STEP)], axis=1
    )


def early_kernel(pair_ref, gain_ref, shift_ref, w_ref, b_ref, out_ref, wt, bt):
    @pl.when(pl.program_id(0) == 0)
    def _():
        wt[...] = w_ref[...].astype(f32).T.astype(bf16)
        bt[...] = column(b_ref[...])

    k, width = pair_ref.shape[1:]
    x = pair_ref[...].astype(f32).reshape(STEP * k, width)
    normed = normalize(x, gain_ref[...], shift_ref[...])
    out = as_rows(factor(normed, wt[...], bt[...]), k).astype(bf16)
    for p in range(out_ref.shape[0]):
        out_ref[p] = out


def left_kernel(pair_ref, gain_ref, shift_ref, w_ref, b_ref, *refs):
    wf, bf, wt, bt = refs[-4:]
    normed_ref = refs[-5]
    outs = refs[:-5]
    k, width = pair_ref.shape[1:]
    hidden = w_ref.shape[1] // 2

    @pl.when(pl.program_id(0) == 0)
    def _():
        wf[...] = w_ref[...].astype(f32).T
        bf[...] = column(b_ref[...])
        host = lax.axis_index(("chan", "quarter"))
        for half in range(2):
            for b in range(0, len(outs), 2):
                source = [
                    pl.ds(pl.multiple_of(half * hidden + (host ^ (b + n)) * BLOCK, BLOCK), BLOCK)
                    for n in range(2)
                ]
                target = slice(half * hidden + b * BLOCK, half * hidden + (b + 2) * BLOCK)
                wt[target] = jnp.concatenate([wf[s] for s in source], axis=0).astype(bf16)
                bt[target] = jnp.concatenate([bf[s] for s in source], axis=0)

    x = pair_ref[...].astype(f32).reshape(STEP * k, width)
    normed = normalize(x, gain_ref[...], shift_ref[...])
    normed_ref[...] = normed.reshape(STEP, k, width)
    rows = as_rows(factor(normed, wt[...], bt[...]), k).astype(bf16)
    for b, out in enumerate(outs):
        out[...] = rows[b]


def late_kernel(normed_ref, w_ref, b_ref, *refs):
    out_ref = refs[-1]
    k, width = normed_ref.shape[1:]
    normed = normed_ref[...].reshape(STEP * k, width)
    wt = w_ref[...].astype(f32).T.astype(bf16)
    out = as_rows(factor(normed, wt, column(b_ref[...])), k).astype(bf16)
    for p in range(out_ref.shape[0]):
        out_ref[p] = out


def gate_kernel(normed_ref, gw_ref, gb_ref, gate_ref):
    k, width = normed_ref.shape[1:]
    normed = normed_ref[...].reshape(STEP * k, width)
    gate = sigmoid(dot(normed, gw_ref[...]) + gb_ref[...])
    gate_ref[...] = gate.reshape(gate_ref.shape).astype(gate_ref.dtype)


def regroup(pieces, target, matrix):
    many = SIZE // STEP
    for s in range(len(pieces) // many):
        rows = jnp.concatenate([piece() for piece in pieces[s * many : (s + 1) * many]], axis=0)
        moved = dot(matrix, rows).astype(bf16)
        for c in range(BLOCK):
            target[c, s * SIZE : (s + 1) * SIZE, :] = moved[c * SIZE : (c + 1) * SIZE]


def slices(refs):
    tall = STEP * BLOCK
    return [
        functools.partial(lambda ref, at: ref[at : at + tall, :], ref, at)
        for ref in refs
        for at in range(0, ref.shape[0], tall)
    ]


def multiply(left, right_ref, right, held, store):
    regroup(slices([right_ref]), right, shuffle(BLOCK, SIZE))
    back = shuffle(SIZE, BLOCK)
    for c in range(BLOCK):
        held[c] = dot_nt(left[c], right[c]).astype(bf16)
    for s in range(left.shape[1] // SIZE):
        parts = jnp.concatenate([held[c, s * SIZE : (s + 1) * SIZE, :] for c in range(BLOCK)], axis=0)
        moved = dot(back, parts).astype(bf16)
        for i in range(0, SIZE, STEP):
            store(s * SIZE + i, moved[i * BLOCK : (i + STEP) * BLOCK])


def first_kernel(hosts, right_ref, *refs):
    lefts, outs = refs[:hosts], refs[hosts : 2 * hosts]
    left, right, held = refs[2 * hosts :]

    @pl.when(pl.program_id(0) == 0)
    def _():
        regroup(slices(lefts), left, shuffle(BLOCK, SIZE))

    rows = left.shape[1] // hosts

    def store(i, values):
        to, at = divmod(i, rows)
        outs[to][at * BLOCK : (at + STEP) * BLOCK, :] = values

    multiply(left, right_ref, right, held, store)


def second_kernel(right_ref, left, *refs):
    out_ref, right, held = refs[-3:]
    rows = left.shape[1] // out_ref.shape[0]
    host = lax.axis_index(("chan", "quarter"))

    def store(i, values):
        to, at = divmod(i, rows)
        out_ref[host ^ to, at * BLOCK : (at + STEP) * BLOCK, :] = values

    multiply(left, right_ref, right, held, store)


def collect_kernel(*refs):
    host = lax.axis_index(("chan", "quarter"))
    for b, ref in enumerate(refs[:-1]):
        refs[-1][host ^ b] = ref[...]


def final_kernel(first_ref, second_ref, gate_ref, g_ref, s_ref, w_ref, b_ref, out_ref, gt, st, order):
    rows = out_ref.shape[1] * GATHER // (first_ref.shape[2] // EARLY)
    early = GATHER * EARLY

    @pl.when(pl.program_id(0) == 0)
    def _():
        gt[...] = column(g_ref[...])
        st[...] = column(s_ref[...])
        each = rows // GATHER
        out = lax.broadcasted_iota(jnp.int32, (rows, rows), 0)
        lane = lax.broadcasted_iota(jnp.int32, (rows, rows), 1)
        device, at = out // each, out % each
        want = jnp.where(
            at < EARLY, device * EARLY + at, early + device * (each - EARLY) + at - EARLY
        )
        order[...] = jnp.where(want == lane, 1.0, 0.0).astype(bf16)

    width = w_ref.shape[0]
    late = rows - early
    for g in range(out_ref.shape[1] // rows):
        x = jnp.concatenate(
            [
                first_ref[:, :, g * early : (g + 1) * early].astype(f32),
                second_ref[:, :, g * late : (g + 1) * late].astype(f32),
            ],
            axis=2,
        )
        for r in range(STEP):
            one = x[:, r * BLOCK : (r + 1) * BLOCK].reshape(width, rows)
            centered = one - jnp.mean(one, axis=0, keepdims=True)
            variance = jnp.mean(centered * centered, axis=0, keepdims=True)
            normed = centered * lax.rsqrt(variance + epsilon)
            normed = normed * widen(gt[...], rows) + widen(st[...], rows)
            turned = dot_nt(order[...], normed.astype(bf16)).astype(bf16)
            outward = dot(turned, w_ref[...]) + b_ref[...]
            at = slice(g * rows, (g + 1) * rows)
            out_ref[r, at, :] = (gate_ref[r, at, :].astype(f32) * outward).astype(bf16)


def whole(shape):
    return pl.BlockSpec(shape, lambda s: (0,) * len(shape))


def cost(flops, size):
    return pl.CostEstimate(flops=flops, bytes_accessed=size, transcendentals=0)


def params(mib=32):
    return pltpu.CompilerParams(vmem_limit_bytes=mib * MIB)


def shards(parts, pair, norm_gain, norm_shift, factor_weight, factor_bias, gate_weight, gate_bias,
           center_gain, center_shift, out_weight, out_bias):
    rows, k, width = pair.shape
    hidden = out_weight.shape[0]
    hosts = hidden // BLOCK
    steps = rows // STEP
    late = rows - EARLY
    tall = rows * BLOCK
    mine = hosts * rows
    devices = parts * hosts
    gathers = devices // GATHER
    in_part = ("chan", "quarter")
    everywhere = ("part",) + in_part
    row = lambda v: v.reshape(1, -1)
    row_block = pl.BlockSpec((STEP, k, width), lambda s: (s, 0, 0))
    work = rows * k * width
    bfloat = lambda *shape: jax.ShapeDtypeStruct(shape, bf16)

    early_right = pl.pallas_call(
        early_kernel,
        grid=(EARLY // STEP,),
        in_specs=[
            row_block,
            whole((1, width)),
            whole((1, width)),
            pl.BlockSpec((width, 2 * hidden), lambda s: (0, 1)),
            pl.BlockSpec((1, 2 * hidden), lambda s: (0, 1)),
        ],
        out_specs=pl.BlockSpec((parts, hosts, STEP * BLOCK, k), lambda s: (0, 0, s, 0)),
        out_shape=bfloat(parts, hosts, EARLY * BLOCK, k),
        scratch_shapes=[pltpu.VMEM((2 * hidden, width), bf16), pltpu.VMEM((2 * hidden, LANES), f32)],
        compiler_params=params(60),
        cost_estimate=cost(4 * work * hidden, 6 * work),
        name="early_right",
    )(pair, row(norm_gain), row(norm_shift), factor_weight, row(factor_bias))
    early_right = lax.all_to_all(
        early_right.reshape(devices, EARLY * BLOCK, k), everywhere, 0, 0, tiled=True
    )

    def send(values, b):
        if b == 0:
            return values
        pairs = [(p * hosts + h, p * hosts + (h ^ b)) for p in range(parts) for h in range(hosts)]
        return lax.ppermute(values, everywhere, pairs)

    *lefts, normed = pl.pallas_call(
        left_kernel,
        grid=(steps,),
        in_specs=[
            row_block,
            whole((1, width)),
            whole((1, width)),
            whole((width, 2 * hidden)),
            whole((1, 2 * hidden)),
        ],
        out_specs=[pl.BlockSpec((STEP * BLOCK, k), lambda s: (s, 0))] * hosts + [row_block],
        out_shape=[bfloat(tall, k)] * hosts + [bfloat(*pair.shape)],
        scratch_shapes=[
            pltpu.VMEM((2 * hidden, width), f32),
            pltpu.VMEM((2 * hidden, LANES), f32),
            pltpu.VMEM((2 * hidden, width), bf16),
            pltpu.VMEM((2 * hidden, LANES), f32),
        ],
        compiler_params=params(60),
        cost_estimate=cost(4 * work * hidden, 6 * work),
        name="left_factor",
    )(pair, row(norm_gain), row(norm_shift), factor_weight, row(factor_bias))
    lefts = [send(values, b) for b, values in enumerate(lefts)]

    late_right = pl.pallas_call(
        late_kernel,
        grid=(late // STEP,),
        in_specs=[
            pl.BlockSpec((STEP, k, width), lambda s: (s + EARLY // STEP, 0, 0)),
            pl.BlockSpec((width, 2 * hidden), lambda s: (0, 1)),
            pl.BlockSpec((1, 2 * hidden), lambda s: (0, 1)),
        ]
        + [pl.BlockSpec(memory_space=pl.ANY)] * (hosts - 1),
        out_specs=pl.BlockSpec((parts, hosts, STEP * BLOCK, k), lambda s: (0, 0, s, 0)),
        out_shape=bfloat(parts, hosts, late * BLOCK, k),
        compiler_params=params(60),
        cost_estimate=cost(2 * work * hidden, 2 * work),
        name="late_right",
    )(normed, factor_weight, row(factor_bias), *lefts[1:])
    late_right = lax.all_to_all(
        late_right.reshape(devices, late * BLOCK, k), everywhere, 0, 0, tiled=True
    )

    gate = pl.pallas_call(
        gate_kernel,
        grid=(steps,),
        in_specs=[row_block, whole((width, width)), whole((1, width))],
        out_specs=row_block,
        out_shape=bfloat(*pair.shape),
        compiler_params=params(60),
        cost_estimate=cost(2 * work * width, 4 * work),
        name="gate",
    )(normed, gate_weight, row(gate_bias))

    first = GATHER * EARLY
    second = GATHER * late
    spent = cost(2 * BLOCK * mine * mine * k, 6 * BLOCK * mine * k)
    *firsts, left = pl.pallas_call(
        functools.partial(first_kernel, hosts),
        grid=(gathers,),
        in_specs=[pl.BlockSpec((first * BLOCK, k), lambda s: (s, 0))] + [whole((tall, k))] * hosts,
        out_specs=[pl.BlockSpec((tall, first), lambda s: (0, s))] * hosts + [whole((BLOCK, mine, k))],
        out_shape=[bfloat(tall, gathers * first)] * hosts + [bfloat(BLOCK, mine, k)],
        scratch_shapes=[pltpu.VMEM((BLOCK, first, k), bf16), pltpu.VMEM((BLOCK, mine, first), bf16)],
        compiler_params=params(),
        cost_estimate=spent,
        name="first_products",
    )(early_right.reshape(devices * EARLY * BLOCK, k), *lefts)
    firsts = [send(values, b) for b, values in enumerate(firsts)]

    forced = firsts[1 : 1 + hosts * 3 // 4]
    seconds = pl.pallas_call(
        second_kernel,
        grid=(gathers,),
        in_specs=[pl.BlockSpec((second * BLOCK, k), lambda s: (s, 0)), whole((BLOCK, mine, k))]
        + [pl.BlockSpec(memory_space=pl.ANY)] * len(forced),
        out_specs=pl.BlockSpec((hosts, tall, second), lambda s: (0, 0, s)),
        out_shape=bfloat(hosts, tall, gathers * second),
        scratch_shapes=[pltpu.VMEM((BLOCK, second, k), bf16), pltpu.VMEM((BLOCK, mine, second), bf16)],
        compiler_params=params(),
        cost_estimate=spent,
        name="second_products",
    )(late_right.reshape(devices * late * BLOCK, k), left, *forced)
    seconds = lax.all_to_all(seconds, in_part, 0, 0, tiled=True)

    vmem = pl.BlockSpec(memory_space=pltpu.VMEM)
    firsts = pl.pallas_call(
        collect_kernel,
        in_specs=[vmem] * hosts,
        out_specs=vmem,
        out_shape=bfloat(hosts, tall, gathers * first),
        compiler_params=params(),
        cost_estimate=cost(0, 4 * work),
        name="collect",
    )(*firsts)

    return pl.pallas_call(
        final_kernel,
        grid=(steps,),
        in_specs=[
            pl.BlockSpec((hosts, STEP * BLOCK, gathers * first), lambda s: (0, s, 0)),
            pl.BlockSpec((hosts, STEP * BLOCK, gathers * second), lambda s: (0, s, 0)),
            row_block,
            whole((1, hidden)),
            whole((1, hidden)),
            whole((hidden, width)),
            whole((1, width)),
        ],
        out_specs=row_block,
        out_shape=bfloat(*pair.shape),
        scratch_shapes=[
            pltpu.VMEM((hidden, LANES), f32),
            pltpu.VMEM((hidden, LANES), f32),
            pltpu.VMEM((GATHER * rows, GATHER * rows), bf16),
        ],
        compiler_params=params(),
        cost_estimate=cost(2 * work * width, 6 * work),
        name="update",
    )(firsts, seconds, gate, row(center_gain), row(center_shift), out_weight, row(out_bias))


def solution(mesh):
    groups, chan, quarter = (mesh.shape[a] for a in ("groups", "chan", "quarter"))
    near = CHANNELS // BLOCK // quarter
    parts = chan // near
    split = Mesh(
        mesh.devices.reshape(groups, parts, near, quarter), ("groups", "part", "chan", "quarter")
    )
    rows = P(("groups", "part", "chan", "quarter"), None, None)
    return jax.shard_map(
        functools.partial(shards, parts),
        mesh=split,
        in_specs=(rows,) + (P(),) * 10,
        out_specs=rows,
        check_vma=False,
    )
```

```python
import functools

import jax
import jax.numpy as jnp
from jax import lax
from jax.experimental import pallas as pl
from jax.experimental.pallas import tpu as pltpu
from jax.sharding import Mesh
from jax.sharding import PartitionSpec as P

epsilon = 1e-05
CHANNELS = 128
BLOCK = 8
STEP = 4
SIZE = 32
LANES = 128
GATHER = 32
MIB = 1024 * 1024

f32, bf16 = jnp.float32, jnp.bfloat16


def sigmoid(x):
    return 0.5 * jnp.tanh(0.5 * x) + 0.5


def dot(a, b):
    return jnp.dot(a, b, preferred_element_type=f32)


def dot_nt(a, b):
    return lax.dot_general(a, b, (((1,), (1,)), ((), ())), preferred_element_type=f32)


def column(row):
    blocks = [
        jnp.broadcast_to(row[:, k : k + LANES], (LANES, LANES)).T
        for k in range(0, row.shape[1], LANES)
    ]
    return jnp.concatenate(blocks, axis=0)


def widen(col, width):
    return jnp.concatenate([col] * (width // LANES), axis=1)


def shuffle(groups, size):
    n = groups * size
    out = lax.broadcasted_iota(jnp.int32, (n, n), 0)
    row = lax.broadcasted_iota(jnp.int32, (n, n), 1)
    want = (out % size) * groups + out // size
    return jnp.where(want == row, 1.0, 0.0).astype(bf16)


def normalize(x, gain, shift):
    centered = x - jnp.mean(x, axis=1, keepdims=True)
    variance = jnp.mean(centered * centered, axis=1, keepdims=True)
    return (centered * lax.rsqrt(variance + epsilon) * gain + shift).astype(bf16)


def factor(normed, wt, bias):
    width = wt.shape[0] // 2
    lanes = normed.shape[0]
    gate = dot_nt(wt[:width], normed) + widen(bias[:width], lanes)
    value = dot_nt(wt[width:], normed) + widen(bias[width:], lanes)
    return sigmoid(gate) * value


def as_rows(values, k):
    hosts = values.shape[0] // BLOCK
    return jnp.concatenate(
        [values[:, r * k : (r + 1) * k].reshape(hosts, BLOCK, k) for r in range(STEP)], axis=1
    )


def right_kernel(pair_ref, gain_ref, shift_ref, w_ref, b_ref, out_ref, wt, bt):
    @pl.when(pl.program_id(0) == 0)
    def _():
        wt[...] = w_ref[...].astype(f32).T.astype(bf16)
        bt[...] = column(b_ref[...])

    k, width = pair_ref.shape[1:]
    x = pair_ref[...].astype(f32).reshape(STEP * k, width)
    normed = normalize(x, gain_ref[...], shift_ref[...])
    out = as_rows(factor(normed, wt[...], bt[...]), k).astype(bf16)
    for p in range(out_ref.shape[0]):
        out_ref[p] = out


def left_kernel(pair_ref, gain_ref, shift_ref, w_ref, b_ref, *refs):
    wf, bf, wt, bt = refs[-4:]
    normed_ref = refs[-5]
    outs = refs[:-5]
    k, width = pair_ref.shape[1:]
    hidden = w_ref.shape[1] // 2

    @pl.when(pl.program_id(0) == 0)
    def _():
        wf[...] = w_ref[...].astype(f32).T
        bf[...] = column(b_ref[...])
        host = lax.axis_index(("chan", "quarter"))
        for half in range(2):
            for b in range(0, len(outs), 2):
                source = [
                    pl.ds(pl.multiple_of(half * hidden + (host ^ (b + n)) * BLOCK, BLOCK), BLOCK)
                    for n in range(2)
                ]
                target = slice(half * hidden + b * BLOCK, half * hidden + (b + 2) * BLOCK)
                wt[target] = jnp.concatenate([wf[s] for s in source], axis=0).astype(bf16)
                bt[target] = jnp.concatenate([bf[s] for s in source], axis=0)

    x = pair_ref[...].astype(f32).reshape(STEP * k, width)
    normed = normalize(x, gain_ref[...], shift_ref[...])
    normed_ref[...] = normed.reshape(STEP, k, width)
    rows = as_rows(factor(normed, wt[...], bt[...]), k).astype(bf16)
    for b, out in enumerate(outs):
        out[...] = rows[b]


def gate_kernel(normed_ref, gw_ref, gb_ref, gate_ref):
    k, width = normed_ref.shape[1:]
    normed = normed_ref[...].reshape(STEP * k, width)
    gate = sigmoid(dot(normed, gw_ref[...]) + gb_ref[...])
    gate_ref[...] = gate.reshape(gate_ref.shape).astype(gate_ref.dtype)


def regroup(pieces, target, matrix):
    many = SIZE // STEP
    for s in range(len(pieces) // many):
        rows = jnp.concatenate([piece() for piece in pieces[s * many : (s + 1) * many]], axis=0)
        moved = dot(matrix, rows).astype(bf16)
        for c in range(BLOCK):
            target[c, s * SIZE : (s + 1) * SIZE, :] = moved[c * SIZE : (c + 1) * SIZE]


def slices(refs):
    tall = STEP * BLOCK
    return [
        functools.partial(lambda ref, at: ref[at : at + tall, :], ref, at)
        for ref in refs
        for at in range(0, ref.shape[0], tall)
    ]


def multiply(left, right_ref, right, held, store):
    regroup(slices([right_ref]), right, shuffle(BLOCK, SIZE))
    back = shuffle(SIZE, BLOCK)
    for c in range(BLOCK):
        held[c] = dot_nt(left[c], right[c]).astype(bf16)
    for s in range(left.shape[1] // SIZE):
        parts = jnp.concatenate([held[c, s * SIZE : (s + 1) * SIZE, :] for c in range(BLOCK)], axis=0)
        moved = dot(back, parts).astype(bf16)
        for i in range(0, SIZE, STEP):
            store(s * SIZE + i, moved[i * BLOCK : (i + STEP) * BLOCK])


def gather_kernel(*refs):
    regroup(slices(refs[:-1]), refs[-1], shuffle(BLOCK, SIZE))


def product_kernel(right_ref, left, out_ref, right, held):
    rows = left.shape[1] // out_ref.shape[0]
    host = lax.axis_index(("chan", "quarter"))

    def store(i, values):
        to, at = divmod(i, rows)
        out_ref[host ^ to, at * BLOCK : (at + STEP) * BLOCK, :] = values

    multiply(left, right_ref, right, held, store)


def final_kernel(x_ref, gate_ref, g_ref, s_ref, w_ref, b_ref, out_ref, gt, st):
    @pl.when(pl.program_id(0) == 0)
    def _():
        gt[...] = column(g_ref[...])
        st[...] = column(s_ref[...])

    hosts, _, j = x_ref.shape
    width = hosts * BLOCK
    for r in range(0, STEP, 2):
        pair = x_ref[:, r * BLOCK : (r + 2) * BLOCK].astype(f32)
        for n in range(2):
            x = pair[:, n * BLOCK : (n + 1) * BLOCK].reshape(width, j)
            centered = x - jnp.mean(x, axis=0, keepdims=True)
            variance = jnp.mean(centered * centered, axis=0, keepdims=True)
            normed = centered * lax.rsqrt(variance + epsilon)
            normed = normed * widen(gt[...], j) + widen(st[...], j)
            outward = dot(normed.T.astype(bf16), w_ref[...]) + b_ref[...]
            out_ref[r + n] = (gate_ref[r + n].astype(f32) * outward).astype(bf16)


def whole(shape):
    return pl.BlockSpec(shape, lambda s: (0,) * len(shape))


def cost(flops, size):
    return pl.CostEstimate(flops=flops, bytes_accessed=size, transcendentals=0)


def params(mib=32):
    return pltpu.CompilerParams(vmem_limit_bytes=mib * MIB)


def shards(parts, pair, norm_gain, norm_shift, factor_weight, factor_bias, gate_weight, gate_bias,
           center_gain, center_shift, out_weight, out_bias):
    rows, k, width = pair.shape
    hidden = out_weight.shape[0]
    hosts = hidden // BLOCK
    steps = rows // STEP
    tall = rows * BLOCK
    mine = hosts * rows
    devices = parts * hosts
    in_part = ("chan", "quarter")
    everywhere = ("part",) + in_part
    row = lambda v: v.reshape(1, -1)
    row_block = pl.BlockSpec((STEP, k, width), lambda s: (s, 0, 0))
    work = rows * k * width
    bfloat = lambda *shape: jax.ShapeDtypeStruct(shape, bf16)

    right = pl.pallas_call(
        right_kernel,
        grid=(steps,),
        in_specs=[
            row_block,
            whole((1, width)),
            whole((1, width)),
            pl.BlockSpec((width, 2 * hidden), lambda s: (0, 1)),
            pl.BlockSpec((1, 2 * hidden), lambda s: (0, 1)),
        ],
        out_specs=pl.BlockSpec((parts, hosts, STEP * BLOCK, k), lambda s: (0, 0, s, 0)),
        out_shape=bfloat(parts, hosts, tall, k),
        scratch_shapes=[pltpu.VMEM((2 * hidden, width), bf16), pltpu.VMEM((2 * hidden, LANES), f32)],
        compiler_params=params(60),
        cost_estimate=cost(4 * work * hidden, 6 * work),
        name="right_factor",
    )(pair, row(norm_gain), row(norm_shift), factor_weight, row(factor_bias))
    right = lax.all_to_all(right.reshape(devices, tall, k), everywhere, 0, 0, tiled=True)

    def send(values, b):
        if b == 0:
            return values
        pairs = [(p * hosts + h, p * hosts + (h ^ b)) for p in range(parts) for h in range(hosts)]
        return lax.ppermute(values, everywhere, pairs)

    *lefts, normed = pl.pallas_call(
        left_kernel,
        grid=(steps,),
        in_specs=[
            row_block,
            whole((1, width)),
            whole((1, width)),
            whole((width, 2 * hidden)),
            whole((1, 2 * hidden)),
        ],
        out_specs=[pl.BlockSpec((STEP * BLOCK, k), lambda s: (s, 0))] * hosts + [row_block],
        out_shape=[bfloat(tall, k)] * hosts + [bfloat(*pair.shape)],
        scratch_shapes=[
            pltpu.VMEM((2 * hidden, width), f32),
            pltpu.VMEM((2 * hidden, LANES), f32),
            pltpu.VMEM((2 * hidden, width), bf16),
            pltpu.VMEM((2 * hidden, LANES), f32),
        ],
        compiler_params=params(),
        cost_estimate=cost(4 * work * hidden, 6 * work),
        name="left_factor",
    )(pair, row(norm_gain), row(norm_shift), factor_weight, row(factor_bias))
    lefts = [send(values, b) for b, values in enumerate(lefts)]

    vmem = pl.BlockSpec(memory_space=pltpu.VMEM)
    left = pl.pallas_call(
        gather_kernel,
        in_specs=[vmem] * hosts,
        out_specs=vmem,
        out_shape=bfloat(BLOCK, mine, k),
        compiler_params=params(),
        cost_estimate=cost(2 * work * BLOCK * SIZE, 4 * work),
        name="gather_left",
    )(*lefts)

    gate = pl.pallas_call(
        gate_kernel,
        grid=(steps,),
        in_specs=[row_block, whole((width, width)), whole((1, width))],
        out_specs=row_block,
        out_shape=bfloat(*pair.shape),
        compiler_params=params(),
        cost_estimate=cost(2 * work * width, 4 * work),
        name="gate",
    )(normed, gate_weight, row(gate_bias))

    span = GATHER * rows
    product = pl.pallas_call(
        product_kernel,
        grid=(devices // GATHER,),
        in_specs=[pl.BlockSpec((span * BLOCK, k), lambda s: (s, 0)), whole((BLOCK, mine, k))],
        out_specs=pl.BlockSpec((hosts, tall, span), lambda s: (0, 0, s)),
        out_shape=bfloat(hosts, tall, devices * rows),
        scratch_shapes=[pltpu.VMEM((BLOCK, span, k), bf16), pltpu.VMEM((BLOCK, mine, span), bf16)],
        compiler_params=params(40),
        cost_estimate=cost(2 * BLOCK * mine * mine * k, 6 * BLOCK * mine * k),
        name="products",
    )(right.reshape(devices * tall, k), left)
    product = lax.all_to_all(product, in_part, 0, 0, tiled=True)

    return pl.pallas_call(
        final_kernel,
        grid=(steps,),
        in_specs=[
            pl.BlockSpec((hosts, STEP * BLOCK, devices * rows), lambda s: (0, s, 0)),
            row_block,
            whole((1, hidden)),
            whole((1, hidden)),
            whole((hidden, width)),
            whole((1, width)),
        ],
        out_specs=row_block,
        out_shape=bfloat(*pair.shape),
        scratch_shapes=[pltpu.VMEM((hidden, LANES), f32), pltpu.VMEM((hidden, LANES), f32)],
        compiler_params=params(),
        cost_estimate=cost(2 * work * width, 6 * work),
        name="update",
    )(product, gate, row(center_gain), row(center_shift), out_weight, row(out_bias))


def solution(mesh):
    groups, chan, quarter = (mesh.shape[a] for a in ("groups", "chan", "quarter"))
    near = CHANNELS // BLOCK // quarter
    parts = chan // near
    split = Mesh(
        mesh.devices.reshape(groups, parts, near, quarter), ("groups", "part", "chan", "quarter")
    )
    rows = P(("groups", "part", "chan", "quarter"), None, None)
    return jax.shard_map(
        functools.partial(shards, parts),
        mesh=split,
        in_specs=(rows,) + (P(),) * 10,
        out_specs=rows,
        check_vma=False,
    )
```

```python
import functools

import jax
import jax.numpy as jnp
from jax import lax
from jax.experimental import pallas as pl
from jax.experimental.pallas import tpu as pltpu
from jax.sharding import Mesh
from jax.sharding import PartitionSpec as P

epsilon = 1e-05
CHANNELS = 128
BLOCK = 8
STEP = 4
SIZE = 32
LANES = 128
GATHER = 32
MIB = 1024 * 1024

f32, bf16 = jnp.float32, jnp.bfloat16


def sigmoid(x):
    return 0.5 * jnp.tanh(0.5 * x) + 0.5


def dot(a, b):
    return jnp.dot(a, b, preferred_element_type=f32)


def dot_nt(a, b):
    return lax.dot_general(a, b, (((1,), (1,)), ((), ())), preferred_element_type=f32)


def column(row):
    blocks = [
        jnp.broadcast_to(row[:, k : k + LANES], (LANES, LANES)).T
        for k in range(0, row.shape[1], LANES)
    ]
    return jnp.concatenate(blocks, axis=0)


def widen(col, width):
    return jnp.concatenate([col] * (width // LANES), axis=1)


def shuffle(groups, size):
    n = groups * size
    out = lax.broadcasted_iota(jnp.int32, (n, n), 0)
    row = lax.broadcasted_iota(jnp.int32, (n, n), 1)
    want = (out % size) * groups + out // size
    return jnp.where(want == row, 1.0, 0.0).astype(bf16)


def normalize(x, gain, shift):
    centered = x - jnp.mean(x, axis=1, keepdims=True)
    variance = jnp.mean(centered * centered, axis=1, keepdims=True)
    return (centered * lax.rsqrt(variance + epsilon) * gain + shift).astype(bf16)


def factor(normed, wt, bias):
    width = wt.shape[0] // 2
    lanes = normed.shape[0]
    gate = dot_nt(wt[:width], normed) + widen(bias[:width], lanes)
    value = dot_nt(wt[width:], normed) + widen(bias[width:], lanes)
    return sigmoid(gate) * value


def as_rows(values, k):
    hosts = values.shape[0] // BLOCK
    return jnp.concatenate(
        [values[:, r * k : (r + 1) * k].reshape(hosts, BLOCK, k) for r in range(STEP)], axis=1
    )


def right_kernel(pair_ref, gain_ref, shift_ref, w_ref, b_ref, out_ref, wt, bt):
    @pl.when(pl.program_id(0) == 0)
    def _():
        wt[...] = w_ref[...].astype(f32).T.astype(bf16)
        bt[...] = column(b_ref[...])

    k, width = pair_ref.shape[1:]
    x = pair_ref[...].astype(f32).reshape(STEP * k, width)
    normed = normalize(x, gain_ref[...], shift_ref[...])
    out = as_rows(factor(normed, wt[...], bt[...]), k).astype(bf16)
    for p in range(out_ref.shape[0]):
        out_ref[p] = out


def left_kernel(own_ref, other_ref, gain_ref, shift_ref, w_ref, b_ref, *refs):
    wf, bf, wt, bt = refs[-4:]
    outs = refs[:-4]
    k, width = own_ref.shape[1:]
    hidden = w_ref.shape[1] // 2
    near = len(outs) * BLOCK
    step = pl.program_id(0)

    @pl.when(step == 0)
    def _():
        wf[...] = w_ref[...].astype(f32).T
        bf[...] = column(b_ref[...])
        host = lax.axis_index(("chan", "quarter"))
        for half in range(2):
            for m in range(0, len(outs), 2):
                source = [
                    pl.ds(
                        pl.multiple_of(half * hidden + (host ^ (2 * (m + n))) * BLOCK, BLOCK), BLOCK
                    )
                    for n in range(2)
                ]
                target = slice(half * near + m * BLOCK, half * near + (m + 2) * BLOCK)
                wt[target] = jnp.concatenate([wf[s] for s in source], axis=0).astype(bf16)
                bt[target] = jnp.concatenate([bf[s] for s in source], axis=0)

    pair = jnp.where(step < pl.num_programs(0) // 2, own_ref[...], other_ref[...])
    normed = normalize(pair.astype(f32).reshape(STEP * k, width), gain_ref[...], shift_ref[...])
    rows = as_rows(factor(normed, wt[...], bt[...]), k).astype(bf16)
    for m, out in enumerate(outs):
        out[...] = rows[m]


def gate_kernel(pair_ref, gain_ref, shift_ref, gw_ref, gb_ref, gate_ref):
    k, width = pair_ref.shape[1:]
    x = pair_ref[...].astype(f32).reshape(STEP * k, width)
    normed = normalize(x, gain_ref[...], shift_ref[...])
    gate = sigmoid(dot(normed, gw_ref[...]) + gb_ref[...])
    gate_ref[...] = gate.reshape(gate_ref.shape).astype(gate_ref.dtype)


def regroup(pieces, target, matrix):
    many = SIZE // STEP
    for s in range(len(pieces) // many):
        rows = jnp.concatenate([piece() for piece in pieces[s * many : (s + 1) * many]], axis=0)
        moved = dot(matrix, rows).astype(bf16)
        for c in range(BLOCK):
            target[c, s * SIZE : (s + 1) * SIZE, :] = moved[c * SIZE : (c + 1) * SIZE]


def slices(refs):
    tall = STEP * BLOCK
    return [
        functools.partial(lambda ref, at: ref[at : at + tall, :], ref, at)
        for ref in refs
        for at in range(0, ref.shape[0], tall)
    ]


def multiply(left, right_ref, right, held, arrive, store):
    regroup(slices([right_ref]), right, shuffle(BLOCK, SIZE))
    back = shuffle(SIZE, BLOCK)
    arrive()
    for c in range(BLOCK):
        held[c] = dot_nt(left[c], right[c]).astype(bf16)
    for s in range(left.shape[1] // SIZE):
        parts = jnp.concatenate([held[c, s * SIZE : (s + 1) * SIZE, :] for c in range(BLOCK)], axis=0)
        moved = dot(back, parts).astype(bf16)
        for i in range(0, SIZE, STEP):
            store(s * SIZE + i, moved[i * BLOCK : (i + STEP) * BLOCK])


def gather_kernel(*refs):
    regroup(slices(refs[:-1]), refs[-1], shuffle(BLOCK, SIZE))


def product_kernel(right_ref, left_ref, out_ref, left, right, held, made, sems, sem):
    copy = pltpu.make_async_copy(left_ref, left, sem)

    @pl.when(pl.program_id(0) == 0)
    def _():
        copy.start()

    def arrive():
        @pl.when(pl.program_id(0) == 0)
        def _():
            copy.wait()

    hosts = out_ref.shape[0]
    rows = left.shape[1] // hosts
    span = made.shape[2]
    host = lax.axis_index(("chan", "quarter"))
    lanes = pl.ds(pl.multiple_of(pl.program_id(0) * span, LANES), span)
    copies = [
        pltpu.make_async_copy(made.at[b], out_ref.at[host ^ b, :, lanes], sems.at[b])
        for b in range(hosts)
    ]

    def store(i, values):
        to, at = divmod(i, rows)
        made[to, at * BLOCK : (at + STEP) * BLOCK, :] = values
        if at + STEP == rows:
            copies[to].start()

    multiply(left, right_ref, right, held, arrive, store)
    for copy in copies:
        copy.wait()


def final_kernel(x_ref, gate_ref, g_ref, s_ref, w_ref, b_ref, out_ref, gt, st, wt, sem):
    copy = pltpu.make_async_copy(w_ref, wt, sem)

    @pl.when(pl.program_id(0) == 0)
    def _():
        copy.start()
        gt[...] = column(g_ref[...])
        st[...] = column(s_ref[...])
        copy.wait()

    hosts, _, j = x_ref.shape
    width = hosts * BLOCK
    for r in range(0, STEP, 2):
        pair = x_ref[:, r * BLOCK : (r + 2) * BLOCK].astype(f32)
        for n in range(2):
            x = pair[:, n * BLOCK : (n + 1) * BLOCK].reshape(width, j)
            centered = x - jnp.mean(x, axis=0, keepdims=True)
            variance = jnp.mean(centered * centered, axis=0, keepdims=True)
            normed = centered * lax.rsqrt(variance + epsilon)
            normed = normed * widen(gt[...], j) + widen(st[...], j)
            outward = dot(normed.astype(bf16).T, wt[...]) + b_ref[...]
            out_ref[r + n] = (gate_ref[r + n].astype(f32) * outward).astype(bf16)


def whole(shape):
    return pl.BlockSpec(shape, lambda s: (0,) * len(shape))


def cost(flops, size):
    return pl.CostEstimate(flops=flops, bytes_accessed=size, transcendentals=0)


def params(mib=32):
    return pltpu.CompilerParams(vmem_limit_bytes=mib * MIB)


def held_in_hbm(x):
    return pltpu.with_memory_space_constraint(x, pltpu.HBM)


def shards(parts, pair, norm_gain, norm_shift, factor_weight, factor_bias, gate_weight, gate_bias,
           center_gain, center_shift, out_weight, out_bias):
    rows, k, width = pair.shape
    hidden = out_weight.shape[0]
    hosts = hidden // BLOCK
    steps = rows // STEP
    tall = rows * BLOCK
    mine = hosts * rows
    devices = parts * hosts
    in_part = ("chan", "quarter")
    everywhere = ("part",) + in_part
    row = lambda v: held_in_hbm(v.reshape(1, -1))
    row_block = pl.BlockSpec((STEP, k, width), lambda s: (s, 0, 0))
    work = rows * k * width
    bfloat = lambda *shape: pltpu.HBM(shape, bf16)
    factor_weight, gate_weight, out_weight = map(
        held_in_hbm, (factor_weight, gate_weight, out_weight)
    )
    kept = held_in_hbm(pair)

    right = pl.pallas_call(
        right_kernel,
        grid=(steps,),
        in_specs=[
            row_block,
            whole((1, width)),
            whole((1, width)),
            pl.BlockSpec((width, 2 * hidden), lambda s: (0, 1)),
            pl.BlockSpec((1, 2 * hidden), lambda s: (0, 1)),
        ],
        out_specs=pl.BlockSpec((parts, hosts, STEP * BLOCK, k), lambda s: (0, 0, s, 0)),
        out_shape=bfloat(parts, hosts, tall, k),
        scratch_shapes=[pltpu.VMEM((2 * hidden, width), bf16), pltpu.VMEM((2 * hidden, LANES), f32)],
        compiler_params=params(),
        cost_estimate=cost(4 * work * hidden, 6 * work),
        name="right_factor",
    )(kept, row(norm_gain), row(norm_shift), factor_weight, row(factor_bias))
    right = lax.all_to_all(right.reshape(devices, tall, k), everywhere, 0, 0, tiled=True)

    chips = hosts // 2
    other = lax.ppermute(pair, "quarter", [(0, 1), (1, 0)])
    *lefts, = pl.pallas_call(
        left_kernel,
        grid=(2 * steps,),
        in_specs=[
            pl.BlockSpec((STEP, k, width), lambda s: (jnp.minimum(s, steps - 1), 0, 0)),
            pl.BlockSpec((STEP, k, width), lambda s: (jnp.maximum(s - steps, 0), 0, 0)),
            whole((1, width)),
            whole((1, width)),
            whole((width, 2 * hidden)),
            whole((1, 2 * hidden)),
        ],
        out_specs=[pl.BlockSpec((STEP * BLOCK, k), lambda s: (s, 0))] * chips,
        out_shape=[bfloat(2 * tall, k)] * chips,
        scratch_shapes=[
            pltpu.VMEM((2 * hidden, width), f32),
            pltpu.VMEM((2 * hidden, LANES), f32),
            pltpu.VMEM((hidden, width), bf16),
            pltpu.VMEM((hidden, LANES), f32),
        ],
        compiler_params=params(),
        cost_estimate=cost(4 * work * hidden, 6 * work),
        name="left_factor",
    )(kept, other, row(norm_gain), row(norm_shift), factor_weight, row(factor_bias))

    def send(values, m):
        pairs = [
            (p * hosts + h, p * hosts + (h ^ (2 * m))) for p in range(parts) for h in range(hosts)
        ]
        return lax.ppermute(values, everywhere, pairs)

    for m in reversed(range(1, chips)):
        lefts[m] = send(lefts[m], m)

    vmem = pl.BlockSpec(memory_space=pltpu.VMEM)
    left = pl.pallas_call(
        gather_kernel,
        in_specs=[vmem] * chips,
        out_specs=vmem,
        out_shape=bfloat(BLOCK, mine, k),
        compiler_params=params(),
        cost_estimate=cost(2 * work * BLOCK * SIZE, 4 * work),
        name="gather_left",
    )(*lefts)

    gate = pl.pallas_call(
        gate_kernel,
        grid=(steps,),
        in_specs=[
            row_block,
            whole((1, width)),
            whole((1, width)),
            whole((width, width)),
            whole((1, width)),
        ],
        out_specs=row_block,
        out_shape=bfloat(*pair.shape),
        compiler_params=params(),
        cost_estimate=cost(2 * work * width, 4 * work),
        name="gate",
    )(kept, row(norm_gain), row(norm_shift), gate_weight, row(gate_bias))

    span = GATHER * rows
    hbm = pl.BlockSpec(memory_space=pltpu.HBM)
    product = pl.pallas_call(
        product_kernel,
        grid=(devices // GATHER,),
        in_specs=[pl.BlockSpec((span * BLOCK, k), lambda s: (s, 0)), hbm],
        out_specs=hbm,
        out_shape=bfloat(hosts, tall, devices * rows),
        scratch_shapes=[
            pltpu.VMEM((BLOCK, mine, k), bf16),
            pltpu.VMEM((BLOCK, span, k), bf16),
            pltpu.VMEM((BLOCK, mine, span), bf16),
            pltpu.VMEM((hosts, tall, span), bf16),
            pltpu.SemaphoreType.DMA((hosts,)),
            pltpu.SemaphoreType.DMA,
        ],
        compiler_params=params(40),
        cost_estimate=cost(2 * BLOCK * mine * mine * k, 6 * BLOCK * mine * k),
        name="products",
    )(right.reshape(devices * tall, k), held_in_hbm(left))
    product = lax.all_to_all(product, in_part, 0, 0, tiled=True)

    return pl.pallas_call(
        final_kernel,
        grid=(steps,),
        in_specs=[
            pl.BlockSpec((hosts, STEP * BLOCK, devices * rows), lambda s: (0, s, 0)),
            row_block,
            whole((1, hidden)),
            whole((1, hidden)),
            hbm,
            whole((1, width)),
        ],
        out_specs=row_block,
        out_shape=bfloat(*pair.shape),
        scratch_shapes=[
            pltpu.VMEM((hidden, LANES), f32),
            pltpu.VMEM((hidden, LANES), f32),
            pltpu.VMEM((hidden, width), bf16),
            pltpu.SemaphoreType.DMA,
        ],
        compiler_params=params(),
        cost_estimate=cost(2 * work * width, 6 * work),
        name="update",
    )(product, held_in_hbm(gate), row(center_gain), row(center_shift), out_weight, row(out_bias))


def solution(mesh):
    groups, chan, quarter = (mesh.shape[a] for a in ("groups", "chan", "quarter"))
    near = CHANNELS // BLOCK // quarter
    parts = chan // near
    split = Mesh(
        mesh.devices.reshape(groups, parts, near, quarter), ("groups", "part", "chan", "quarter")
    )
    rows = P(("groups", "part", "chan", "quarter"), None, None)
    return jax.shard_map(
        functools.partial(shards, parts),
        mesh=split,
        in_specs=(rows,) + (P(),) * 10,
        out_specs=rows,
        check_vma=False,
    )
```

```python
import functools

import jax
import jax.numpy as jnp
from jax import lax
from jax.experimental import pallas as pl
from jax.experimental.pallas import tpu as pltpu
from jax.sharding import Mesh
from jax.sharding import PartitionSpec as P

epsilon = 1e-05
CHANNELS = 128
BLOCK = 8
STEP = 4
SIZE = 32
LANES = 128
TAIL = 64
MIB = 1024 * 1024

f32, bf16 = jnp.float32, jnp.bfloat16


def sigmoid(x):
    return 0.5 * jnp.tanh(0.5 * x) + 0.5


def dot(a, b):
    return jnp.dot(a, b, preferred_element_type=f32)


def dot_nt(a, b):
    return lax.dot_general(a, b, (((1,), (1,)), ((), ())), preferred_element_type=f32)


def column(row):
    blocks = [
        jnp.broadcast_to(row[:, k : k + LANES], (LANES, LANES)).T
        for k in range(0, row.shape[1], LANES)
    ]
    return jnp.concatenate(blocks, axis=0)


def widen(col, width):
    return jnp.concatenate([col] * (width // LANES), axis=1)


def shuffle(groups, size):
    n = groups * size
    out = lax.broadcasted_iota(jnp.int32, (n, n), 0)
    row = lax.broadcasted_iota(jnp.int32, (n, n), 1)
    want = (out % size) * groups + out // size
    return jnp.where(want == row, 1.0, 0.0).astype(bf16)


def normalize(x, gain, shift):
    centered = x - jnp.mean(x, axis=1, keepdims=True)
    variance = jnp.mean(centered * centered, axis=1, keepdims=True)
    return (centered * lax.rsqrt(variance + epsilon) * gain + shift).astype(bf16)


def factor(normed, wt, bias):
    width = wt.shape[0] // 2
    lanes = normed.shape[0]
    gate = dot_nt(wt[:width], normed) + widen(bias[:width], lanes)
    value = dot_nt(wt[width:], normed) + widen(bias[width:], lanes)
    return sigmoid(gate) * value


def as_rows(values, k):
    hosts = values.shape[0] // BLOCK
    return jnp.concatenate(
        [values[:, r * k : (r + 1) * k].reshape(hosts, BLOCK, k) for r in range(STEP)], axis=1
    )


def factor_kernel(pair_ref, gain_ref, shift_ref, w_ref, b_ref, out_ref, *refs):
    wt, bt = refs[-2:]
    rights = refs[:-2]

    @pl.when(pl.program_id(0) == 0)
    def _():
        wt[...] = w_ref[...].astype(f32).T.astype(bf16)
        bt[...] = column(b_ref[...])

    k, width = pair_ref.shape[1:]
    half = wt.shape[0] // 2
    x = pair_ref[...].astype(f32).reshape(STEP * k, width)
    normed = normalize(x, gain_ref[...], shift_ref[...])
    for n in range(2):
        rows = slice((1 - n) * half, (2 - n) * half)
        values = factor(normed, wt[rows], bt[rows])
        out_ref[:, n] = as_rows(values, k).astype(bf16)
    host = lax.axis_index(("chan", "quarter"))
    for b, right in enumerate(rights):
        right[...] = out_ref[host ^ b, 0]


def gate_kernel(pair_ref, gain_ref, shift_ref, gw_ref, gb_ref, gate_ref):
    k, width = pair_ref.shape[1:]
    x = pair_ref[...].astype(f32).reshape(STEP * k, width)
    normed = normalize(x, gain_ref[...], shift_ref[...])
    gate = sigmoid(dot(normed, gw_ref[...]) + gb_ref[...])
    gate_ref[...] = gate.reshape(gate_ref.shape).astype(gate_ref.dtype)


def regroup(pieces, target, matrix):
    many = SIZE // STEP
    for s in range(len(pieces) // many):
        rows = jnp.concatenate([piece() for piece in pieces[s * many : (s + 1) * many]], axis=0)
        moved = dot(matrix, rows).astype(bf16)
        for c in range(BLOCK):
            target[c, s * SIZE : (s + 1) * SIZE, :] = moved[c * SIZE : (c + 1) * SIZE]


def multiply(left, right, held, out_ref):
    rows = left.shape[1] // out_ref.shape[0]
    tall = rows * BLOCK
    back = shuffle(SIZE, BLOCK)
    for c in range(BLOCK):
        held[c] = dot_nt(left[c], right[c]).astype(bf16)
    main = held.shape[2] - TAIL
    for s in range(left.shape[1] // SIZE):
        parts = jnp.concatenate([held[c, s * SIZE : (s + 1) * SIZE, :] for c in range(BLOCK)], axis=0)
        moved = dot(back, parts)
        ends = moved[:, main:].reshape(SIZE // 2, 2, BLOCK, TAIL)
        ends = jnp.concatenate([ends[:, 0], ends[:, 1]], axis=2).reshape(SIZE * BLOCK // 2, LANES)
        moved, ends = moved[:, :main].astype(bf16), ends.astype(bf16)
        for i in range(0, SIZE, STEP):
            to, at = divmod(s * SIZE + i, rows)
            out_ref[to, at * BLOCK : (at + STEP) * BLOCK, :] = moved[i * BLOCK : (i + STEP) * BLOCK]
            low = tall + at * BLOCK // 2
            out_ref[to, low : low + STEP * BLOCK // 2, :] = ends[
                i * BLOCK // 2 : (i + STEP) * BLOCK // 2
            ]


def near_kernel(factors_ref, left, out_ref, right, held):
    matrix = shuffle(BLOCK, SIZE)
    tall = factors_ref.shape[1] // 2
    step = STEP * BLOCK

    def pieces(n):
        return [
            functools.partial(lambda h, at: factors_ref[h, at : at + step, :], h, at)
            for h in range(factors_ref.shape[0])
            for at in range(n * tall, (n + 1) * tall, step)
        ]

    regroup(pieces(0), right, matrix)
    regroup(pieces(1), left, matrix)
    multiply(left, right, held, out_ref)


def far_kernel(hosts, left_ref, *refs):
    rights = refs[:hosts]
    out_ref, left, arrived, right, held, sems = refs[-6:]
    tall = rights[0].shape[0]
    host = lax.axis_index(("chan", "quarter"))
    copies = []
    for b, ref in enumerate(rights):
        to = arrived.at[pl.ds(pl.multiple_of((host ^ b) * tall, 16), tall)]
        copies.append(pltpu.make_async_copy(ref, to, sems.at[b]))
    copies.append(pltpu.make_async_copy(left_ref, left, sems.at[hosts]))
    for copy in copies:
        copy.start()
    for copy in copies[:-1]:
        copy.wait()
    step = STEP * BLOCK
    pieces = [
        functools.partial(lambda at: arrived[at : at + step, :], at)
        for at in range(0, arrived.shape[0], step)
    ]
    regroup(pieces, right, shuffle(BLOCK, SIZE))
    copies[-1].wait()
    multiply(left, right, held, out_ref)


def final_kernel(parts, *refs):
    products = refs[:parts]
    gate_ref, g_ref, s_ref, w_ref, b_ref, out_ref, gt, st = refs[parts:]
    step = pl.program_id(0)

    @pl.when(step == 0)
    def _():
        gt[...] = column(g_ref[...])
        st[...] = column(s_ref[...])

    part = lax.axis_index("part")
    hosts, tall, _ = products[0].shape
    tall = tall * 2 // 3
    span = gate_ref.shape[1] // parts
    main = span - TAIL
    width = hosts * BLOCK
    for a, ref in enumerate(products):
        first = pl.multiple_of(lax.rem(part + parts - a, parts) * span, 16)
        whole = ref[:, pl.ds(pl.multiple_of(step * STEP * BLOCK, 16), STEP * BLOCK), :].astype(f32)
        low = pl.multiple_of(tall + step * (STEP * BLOCK // 2), 16)
        ends = ref[:, pl.ds(low, STEP * BLOCK // 2), :].astype(f32)
        blocks = [whole[:, r * BLOCK : (r + 1) * BLOCK].reshape(width, LANES) for r in range(STEP)]
        blocks += [
            ends[:, r * BLOCK : (r + 1) * BLOCK].reshape(width, LANES) for r in range(STEP // 2)
        ]
        x = jnp.concatenate(blocks, axis=1)
        centered = x - jnp.mean(x, axis=0, keepdims=True)
        variance = jnp.mean(centered * centered, axis=0, keepdims=True)
        normed = centered * lax.rsqrt(variance + epsilon)
        normed = normed * widen(gt[...], x.shape[1]) + widen(st[...], x.shape[1])
        outward = dot(normed.T.astype(bf16), w_ref[...]) + b_ref[...]
        for r in range(STEP):
            at = pl.ds(first, main)
            value = outward[r * LANES : (r + 1) * LANES]
            out_ref[r, at, :] = (gate_ref[r, at, :].astype(f32) * value).astype(bf16)
            at = pl.ds(pl.multiple_of(first + main, 16), TAIL)
            low = STEP * LANES + r * TAIL
            value = outward[low : low + TAIL]
            out_ref[r, at, :] = (gate_ref[r, at, :].astype(f32) * value).astype(bf16)


def whole(shape):
    return pl.BlockSpec(shape, lambda s: (0,) * len(shape))


def cost(flops, size):
    return pl.CostEstimate(flops=flops, bytes_accessed=size, transcendentals=0)


def params(mib=32):
    return pltpu.CompilerParams(vmem_limit_bytes=mib * MIB)


def in_hbm(x):
    return pltpu.with_memory_space_constraint(x, pltpu.HBM)


def shards(parts, pair, norm_gain, norm_shift, factor_weight, factor_bias, gate_weight, gate_bias,
           center_gain, center_shift, out_weight, out_bias):
    rows, k, width = pair.shape
    hidden = out_weight.shape[0]
    hosts = hidden // BLOCK
    steps = rows // STEP
    tall = rows * BLOCK
    mine = hosts * rows
    in_part = ("chan", "quarter")
    everywhere = ("part",) + in_part
    row = lambda v: in_hbm(v.reshape(1, -1))
    row_block = pl.BlockSpec((STEP, k, width), lambda s: (s, 0, 0))
    work = rows * k * width

    anywhere = pl.BlockSpec(memory_space=pl.ANY)
    bfloat = lambda *shape: jax.ShapeDtypeStruct(shape, bf16)
    bfloat_hbm = lambda *shape: pltpu.HBM(shape, bf16)
    kept = in_hbm(pair)
    factors, *rights = pl.pallas_call(
        factor_kernel,
        grid=(steps,),
        in_specs=[
            row_block,
            whole((1, width)),
            whole((1, width)),
            whole((width, 4 * hidden)),
            whole((1, 4 * hidden)),
        ],
        out_specs=[pl.BlockSpec((hosts, 2, STEP * BLOCK, k), lambda s: (0, 0, s, 0))]
        + [pl.BlockSpec((STEP * BLOCK, k), lambda s: (s, 0))] * hosts,
        out_shape=[bfloat_hbm(hosts, 2, tall, k)] + [bfloat_hbm(tall, k)] * hosts,
        scratch_shapes=[pltpu.VMEM((4 * hidden, width), bf16), pltpu.VMEM((4 * hidden, LANES), f32)],
        compiler_params=params(60),
        cost_estimate=cost(8 * work * hidden, 8 * work),
        name="factors",
    )(kept, row(norm_gain), row(norm_shift), factor_weight, row(factor_bias))

    def send(a, b):
        pairs = [
            (p * hosts + h, (p + a) % parts * hosts + (h ^ b))
            for p in range(parts)
            for h in range(hosts)
        ]
        return lax.ppermute(rights[b], everywhere, pairs)

    arrived = [[send(a, b) for b in range(hosts)] for a in range(1, parts)]

    factors = factors.reshape(hosts, 2 * tall, k)
    factors = lax.all_to_all(factors, in_part, 0, 0, tiled=True)

    gate = pl.pallas_call(
        gate_kernel,
        grid=(steps,),
        in_specs=[
            row_block,
            whole((1, width)),
            whole((1, width)),
            whole((width, width)),
            whole((1, width)),
        ],
        out_specs=row_block,
        out_shape=bfloat_hbm(*pair.shape),
        compiler_params=params(),
        cost_estimate=cost(1 << 37, 4 * work),
        name="gate",
    )(kept, row(norm_gain), row(norm_shift), in_hbm(gate_weight), row(gate_bias))

    vmem = pl.BlockSpec(memory_space=pltpu.VMEM)
    anywhere = pl.BlockSpec(memory_space=pl.ANY)
    grouped = (BLOCK, mine, k)
    spent = cost(2 * BLOCK * mine * mine * k, 6 * BLOCK * mine * k)
    left, product = pl.pallas_call(
        near_kernel,
        in_specs=[vmem],
        out_specs=[vmem, vmem],
        out_shape=[bfloat_hbm(*grouped), bfloat_hbm(hosts, tall * 3 // 2, LANES)],
        scratch_shapes=[pltpu.VMEM(grouped, bf16), pltpu.VMEM((BLOCK, mine, mine), bf16)],
        compiler_params=params(),
        cost_estimate=spent,
        name="near_products",
    )(factors)
    products = [lax.all_to_all(product, in_part, 0, 0, tiled=True)]
    for rest in arrived:
        product = pl.pallas_call(
            functools.partial(far_kernel, hosts),
            in_specs=[anywhere] * (3 + hosts),
            out_specs=vmem,
            out_shape=bfloat_hbm(hosts, tall * 3 // 2, LANES),
            scratch_shapes=[
                pltpu.VMEM(grouped, bf16),
                pltpu.VMEM((mine * BLOCK, k), bf16),
                pltpu.VMEM(grouped, bf16),
                pltpu.VMEM((BLOCK, mine, mine), bf16),
                pltpu.SemaphoreType.DMA((1 + hosts,)),
            ],
            compiler_params=params(),
            cost_estimate=spent,
            name="far_products",
        )(in_hbm(left), *map(in_hbm, rest), in_hbm(products[-1]), in_hbm(gate))
        products.append(lax.all_to_all(product, in_part, 0, 0, tiled=True))

    return pl.pallas_call(
        functools.partial(final_kernel, parts),
        grid=(steps,),
        in_specs=[whole(products[0].shape)] * parts
        + [row_block, whole((1, hidden)), whole((1, hidden)), whole((hidden, width)), whole((1, width))],
        out_specs=row_block,
        out_shape=bfloat(*pair.shape),
        scratch_shapes=[pltpu.VMEM((hidden, LANES), f32), pltpu.VMEM((hidden, LANES), f32)],
        compiler_params=params(),
        cost_estimate=cost(2 * work * width, 6 * work),
        name="update",
    )(
        *map(in_hbm, products[:-1]),
        products[-1],
        in_hbm(gate),
        row(center_gain),
        row(center_shift),
        in_hbm(out_weight),
        row(out_bias),
    )


def solution(mesh):
    groups, chan, quarter = (mesh.shape[a] for a in ("groups", "chan", "quarter"))
    near = CHANNELS // BLOCK // quarter
    parts = chan // near
    split = Mesh(
        mesh.devices.reshape(groups, parts, near, quarter), ("groups", "part", "chan", "quarter")
    )
    rows = P(("groups", "part", "chan", "quarter"), None, None)
    return jax.shard_map(
        functools.partial(shards, parts),
        mesh=split,
        in_specs=(rows,) + (P(),) * 10,
        out_specs=rows,
        check_vma=False,
    )
```

```python
import functools

import jax
import jax.numpy as jnp
from jax import lax
from jax.experimental import pallas as pl
from jax.experimental.pallas import tpu as pltpu
from jax.sharding import Mesh
from jax.sharding import PartitionSpec as P

epsilon = 1e-05
CHANNELS = 128
BLOCK = 8
STEP = 4
SIZE = 32
LANES = 128
GATHER = 32
MIB = 1024 * 1024

f32, bf16 = jnp.float32, jnp.bfloat16


def sigmoid(x):
    return 0.5 * jnp.tanh(0.5 * x) + 0.5


def dot(a, b):
    return jnp.dot(a, b, preferred_element_type=f32)


def dot_nt(a, b):
    return lax.dot_general(a, b, (((1,), (1,)), ((), ())), preferred_element_type=f32)


def column(row):
    blocks = [
        jnp.broadcast_to(row[:, k : k + LANES], (LANES, LANES)).T
        for k in range(0, row.shape[1], LANES)
    ]
    return jnp.concatenate(blocks, axis=0)


def widen(col, width):
    return jnp.concatenate([col] * (width // LANES), axis=1)


def shuffle(groups, size):
    n = groups * size
    out = lax.broadcasted_iota(jnp.int32, (n, n), 0)
    row = lax.broadcasted_iota(jnp.int32, (n, n), 1)
    want = (out % size) * groups + out // size
    return jnp.where(want == row, 1.0, 0.0).astype(bf16)


def normalize(x, gain, shift):
    centered = x - jnp.mean(x, axis=1, keepdims=True)
    variance = jnp.mean(centered * centered, axis=1, keepdims=True)
    return (centered * lax.rsqrt(variance + epsilon) * gain + shift).astype(bf16)


def factor(normed, wt, bias):
    width = wt.shape[0] // 2
    lanes = normed.shape[0]
    gate = dot_nt(wt[:width], normed) + widen(bias[:width], lanes)
    value = dot_nt(wt[width:], normed) + widen(bias[width:], lanes)
    return sigmoid(gate) * value


def as_rows(values, k):
    hosts = values.shape[0] // BLOCK
    return jnp.concatenate(
        [values[:, r * k : (r + 1) * k].reshape(hosts, BLOCK, k) for r in range(STEP)], axis=1
    )


def right_kernel(pair_ref, gain_ref, shift_ref, w_ref, b_ref, out_ref, pair, made, arrive, leave):
    rows, k, width = pair.shape
    starts = range(0, rows, STEP)
    loads = [
        pltpu.make_async_copy(pair_ref.at[pl.ds(r, STEP)], pair.at[pl.ds(r, STEP)], arrive.at[n])
        for n, r in enumerate(starts)
    ]
    for load in loads:
        load.start()
    wt = w_ref[...].astype(f32).T.astype(bf16)
    bt = column(b_ref[...])
    stores = []
    for n, r in enumerate(starts):
        loads[n].wait()
        x = pair[r : r + STEP].astype(f32).reshape(STEP * k, width)
        normed = normalize(x, gain_ref[...], shift_ref[...])
        at = pl.ds(r * BLOCK, STEP * BLOCK)
        made[:, at, :] = as_rows(factor(normed, wt, bt), k).astype(bf16)
        for p in range(out_ref.shape[0]):
            stores.append(
                pltpu.make_async_copy(made.at[:, at, :], out_ref.at[p, :, at, :], leave.at[p, n])
            )
            stores[-1].start()
    for store in stores:
        store.wait()


def left_kernel(pair_ref, gain_ref, shift_ref, w_ref, b_ref, gw_ref, gb_ref, *refs):
    wf, bf, wt, bt = refs[-4:]
    gate_ref = refs[-5]
    outs = refs[:-5]
    k, width = pair_ref.shape[1:]
    hidden = w_ref.shape[1] // 2

    @pl.when(pl.program_id(0) == 0)
    def _():
        wf[...] = w_ref[...].astype(f32).T
        bf[...] = column(b_ref[...])
        host = lax.axis_index(("chan", "quarter"))
        for half in range(2):
            for b in range(0, len(outs), 2):
                source = [
                    pl.ds(pl.multiple_of(half * hidden + (host ^ (b + n)) * BLOCK, BLOCK), BLOCK)
                    for n in range(2)
                ]
                target = slice(half * hidden + b * BLOCK, half * hidden + (b + 2) * BLOCK)
                wt[target] = jnp.concatenate([wf[s] for s in source], axis=0).astype(bf16)
                bt[target] = jnp.concatenate([bf[s] for s in source], axis=0)

    x = pair_ref[...].astype(f32).reshape(STEP * k, width)
    normed = normalize(x, gain_ref[...], shift_ref[...])
    gate = sigmoid(dot(normed, gw_ref[...]) + gb_ref[...])
    gate_ref[...] = gate.reshape(STEP, k, width).astype(bf16)
    rows = as_rows(factor(normed, wt[...], bt[...]), k).astype(bf16)
    for b, out in enumerate(outs):
        out[...] = rows[b]


def regroup(pieces, target, matrix):
    many = SIZE // STEP
    for s in range(len(pieces) // many):
        rows = jnp.concatenate([piece() for piece in pieces[s * many : (s + 1) * many]], axis=0)
        moved = dot(matrix, rows).astype(bf16)
        for c in range(BLOCK):
            target[c, s * SIZE : (s + 1) * SIZE, :] = moved[c * SIZE : (c + 1) * SIZE]


def slices(refs):
    tall = STEP * BLOCK
    return [
        functools.partial(lambda ref, at: ref[at : at + tall, :], ref, at)
        for ref in refs
        for at in range(0, ref.shape[0], tall)
    ]


def multiply(left, right_ref, right, held, store):
    regroup(slices([right_ref]), right, shuffle(BLOCK, SIZE))
    back = shuffle(SIZE, BLOCK)
    for c in range(BLOCK):
        held[c] = dot_nt(left[c], right[c]).astype(bf16)
    for s in range(left.shape[1] // SIZE):
        parts = jnp.concatenate([held[c, s * SIZE : (s + 1) * SIZE, :] for c in range(BLOCK)], axis=0)
        moved = dot(back, parts).astype(bf16)
        for i in range(0, SIZE, STEP):
            store(s * SIZE + i, moved[i * BLOCK : (i + STEP) * BLOCK])


def gather_kernel(*refs):
    regroup(slices(refs[:-1]), refs[-1], shuffle(BLOCK, SIZE))


def product_kernel(right_ref, left, out_ref, right, held):
    rows = left.shape[1] // out_ref.shape[0]
    host = lax.axis_index(("chan", "quarter"))

    def store(i, values):
        to, at = divmod(i, rows)
        out_ref[host ^ to, at * BLOCK : (at + STEP) * BLOCK, :] = values

    multiply(left, right_ref, right, held, store)


def final_kernel(x_ref, gate_ref, g_ref, s_ref, w_ref, b_ref, out_ref, made, leave):
    hosts, _, j = x_ref.shape
    rows = gate_ref.shape[0]
    width = hosts * BLOCK
    gain, shift = widen(column(g_ref[...]), j), widen(column(s_ref[...]), j)
    stores = []
    for r in range(0, rows, 2):
        pair = x_ref[:, r * BLOCK : (r + 2) * BLOCK].astype(f32)
        for n in range(2):
            x = pair[:, n * BLOCK : (n + 1) * BLOCK].reshape(width, j)
            centered = x - jnp.mean(x, axis=0, keepdims=True)
            variance = jnp.mean(centered * centered, axis=0, keepdims=True)
            normed = centered * lax.rsqrt(variance + epsilon) * gain + shift
            outward = dot(normed.astype(bf16).T, w_ref[...]) + b_ref[...]
            made[r + n] = (gate_ref[r + n].astype(f32) * outward).astype(bf16)
        at = pl.ds(r, 2)
        stores.append(pltpu.make_async_copy(made.at[at], out_ref.at[at], leave.at[r // 2]))
        stores[-1].start()
    for store in stores:
        store.wait()


def whole(shape):
    return pl.BlockSpec(shape, lambda s: (0,) * len(shape))


def cost(flops, size):
    return pl.CostEstimate(flops=flops, bytes_accessed=size, transcendentals=0)


def params(mib=32):
    return pltpu.CompilerParams(vmem_limit_bytes=mib * MIB)


def shards(parts, pair, norm_gain, norm_shift, factor_weight, factor_bias, gate_weight, gate_bias,
           center_gain, center_shift, out_weight, out_bias):
    rows, k, width = pair.shape
    hidden = out_weight.shape[0]
    hosts = hidden // BLOCK
    steps = rows // STEP
    tall = rows * BLOCK
    mine = hosts * rows
    devices = parts * hosts
    in_part = ("chan", "quarter")
    everywhere = ("part",) + in_part
    row = lambda v: v.reshape(1, -1)
    row_block = pl.BlockSpec((STEP, k, width), lambda s: (s, 0, 0))
    work = rows * k * width
    bfloat = lambda *shape: jax.ShapeDtypeStruct(shape, bf16)

    vmem = pl.BlockSpec(memory_space=pltpu.VMEM)
    anywhere = pl.BlockSpec(memory_space=pl.ANY)
    right = pl.pallas_call(
        right_kernel,
        grid=(1,),
        in_specs=[
            anywhere,
            whole((1, width)),
            whole((1, width)),
            pl.BlockSpec((width, 2 * hidden), lambda s: (0, 1)),
            pl.BlockSpec((1, 2 * hidden), lambda s: (0, 1)),
        ],
        out_specs=anywhere,
        out_shape=bfloat(parts, hosts, tall, k),
        scratch_shapes=[
            pltpu.VMEM((rows, k, width), bf16),
            pltpu.VMEM((hosts, tall, k), bf16),
            pltpu.SemaphoreType.DMA((steps,)),
            pltpu.SemaphoreType.DMA((parts, steps)),
        ],
        compiler_params=params(60),
        cost_estimate=cost(4 * work * hidden, 6 * work),
        name="right_factor",
    )(pair, row(norm_gain), row(norm_shift), factor_weight, row(factor_bias))
    right = lax.all_to_all(right.reshape(devices, tall, k), everywhere, 0, 0, tiled=True)

    def send(values, b):
        pairs = [(p * hosts + h, p * hosts + (h ^ b)) for p in range(parts) for h in range(hosts)]
        return lax.ppermute(values, everywhere, pairs)

    *lefts, gate = pl.pallas_call(
        left_kernel,
        grid=(steps,),
        in_specs=[
            row_block,
            whole((1, width)),
            whole((1, width)),
            whole((width, 2 * hidden)),
            whole((1, 2 * hidden)),
            whole((width, width)),
            whole((1, width)),
        ],
        out_specs=[pl.BlockSpec((STEP * BLOCK, k), lambda s: (s, 0))] * hosts + [row_block],
        out_shape=[bfloat(tall, k)] * hosts + [bfloat(*pair.shape)],
        scratch_shapes=[
            pltpu.VMEM((2 * hidden, width), f32),
            pltpu.VMEM((2 * hidden, LANES), f32),
            pltpu.VMEM((2 * hidden, width), bf16),
            pltpu.VMEM((2 * hidden, LANES), f32),
        ],
        compiler_params=params(),
        cost_estimate=cost(4 * work * hidden, 6 * work),
        name="left_factor",
    )(
        pair,
        row(norm_gain),
        row(norm_shift),
        factor_weight,
        row(factor_bias),
        gate_weight,
        row(gate_bias),
    )
    lefts = [lefts[0]] + [send(lefts[b], b) for b in reversed(range(1, hosts))][::-1]

    left = pl.pallas_call(
        gather_kernel,
        in_specs=[vmem] * hosts,
        out_specs=vmem,
        out_shape=bfloat(BLOCK, mine, k),
        compiler_params=params(),
        cost_estimate=cost(2 * work * BLOCK * SIZE, 4 * work),
        name="gather_left",
    )(*lefts)

    span = GATHER * rows
    product = pl.pallas_call(
        product_kernel,
        grid=(devices // GATHER,),
        in_specs=[pl.BlockSpec((span * BLOCK, k), lambda s: (s, 0)), whole((BLOCK, mine, k))],
        out_specs=pl.BlockSpec((hosts, tall, span), lambda s: (0, 0, s)),
        out_shape=bfloat(hosts, tall, devices * rows),
        scratch_shapes=[pltpu.VMEM((BLOCK, span, k), bf16), pltpu.VMEM((BLOCK, mine, span), bf16)],
        compiler_params=params(40),
        cost_estimate=cost(2 * BLOCK * mine * mine * k, 6 * BLOCK * mine * k),
        name="products",
    )(right.reshape(devices * tall, k), left)
    product = lax.all_to_all(product, in_part, 0, 0, tiled=True)

    return pl.pallas_call(
        final_kernel,
        in_specs=[vmem] * 6,
        out_specs=anywhere,
        out_shape=bfloat(*pair.shape),
        scratch_shapes=[pltpu.VMEM(pair.shape, bf16), pltpu.SemaphoreType.DMA((rows // 2,))],
        compiler_params=params(),
        cost_estimate=cost(2 * work * width, 6 * work),
        name="update",
    )(product, gate, row(center_gain), row(center_shift), out_weight, row(out_bias))


def solution(mesh):
    groups, chan, quarter = (mesh.shape[a] for a in ("groups", "chan", "quarter"))
    near = CHANNELS // BLOCK // quarter
    parts = chan // near
    split = Mesh(
        mesh.devices.reshape(groups, parts, near, quarter), ("groups", "part", "chan", "quarter")
    )
    rows = P(("groups", "part", "chan", "quarter"), None, None)
    return jax.shard_map(
        functools.partial(shards, parts),
        mesh=split,
        in_specs=(rows,) + (P(),) * 10,
        out_specs=rows,
        check_vma=False,
    )
```

```python
import functools

import jax
import jax.numpy as jnp
from jax import lax
from jax.experimental import pallas as pl
from jax.experimental.pallas import tpu as pltpu
from jax.sharding import Mesh
from jax.sharding import PartitionSpec as P

epsilon = 1e-05
CHANNELS = 128
BLOCK = 8
STEP = 4
PAIRED = 2
SIZE = 32
LANES = 128
GATHER = 32
MIB = 1024 * 1024

f32, bf16 = jnp.float32, jnp.bfloat16


def sigmoid(x):
    return 0.5 * jnp.tanh(0.5 * x) + 0.5


def dot(a, b):
    return jnp.dot(a, b, preferred_element_type=f32)


def dot_nt(a, b):
    return lax.dot_general(a, b, (((1,), (1,)), ((), ())), preferred_element_type=f32)


def column(row):
    blocks = [
        jnp.broadcast_to(row[:, k : k + LANES], (LANES, LANES)).T
        for k in range(0, row.shape[1], LANES)
    ]
    return jnp.concatenate(blocks, axis=0)


def widen(col, width):
    return jnp.concatenate([col] * (width // LANES), axis=1)


def shuffle(groups, size):
    n = groups * size
    out = lax.broadcasted_iota(jnp.int32, (n, n), 0)
    row = lax.broadcasted_iota(jnp.int32, (n, n), 1)
    want = (out % size) * groups + out // size
    return jnp.where(want == row, 1.0, 0.0).astype(bf16)


def normalize(x, gain, shift):
    centered = x - jnp.mean(x, axis=1, keepdims=True)
    variance = jnp.mean(centered * centered, axis=1, keepdims=True)
    return (centered * lax.rsqrt(variance + epsilon) * gain + shift).astype(bf16)


def factor(normed, wt, bias):
    width = wt.shape[0] // 2
    lanes = normed.shape[0]
    gate = dot_nt(wt[:width], normed) + widen(bias[:width], lanes)
    value = dot_nt(wt[width:], normed) + widen(bias[width:], lanes)
    return sigmoid(gate) * value


def as_rows(values, k, step=STEP):
    hosts = values.shape[0] // BLOCK
    return jnp.concatenate(
        [values[:, r * k : (r + 1) * k].reshape(hosts, BLOCK, k) for r in range(step)], axis=1
    )


def right_kernel(
    pair_ref, gain_ref, shift_ref, w_ref, b_ref, out_ref, pair, gain, shift, w, bias, wt, bt, made,
    arrive, leave, sems,
):
    rows, k, width = pair.shape
    parts, hosts = out_ref.shape[:2]
    half = w.shape[1]
    loads = [
        pltpu.make_async_copy(ref, to, sems.at[n])
        for n, (ref, to) in enumerate(
            [
                (w_ref.at[:, pl.ds(half, half)], w),
                (b_ref.at[:, pl.ds(half, half)], bias),
                (gain_ref, gain),
                (shift_ref, shift),
            ]
        )
    ]

    def load(n):
        at = pl.ds(n * PAIRED, PAIRED)
        return pltpu.make_async_copy(pair_ref.at[at], pair.at[at], arrive.at[n])

    def store(p, n):
        at = pl.ds(pl.multiple_of(n * PAIRED * BLOCK, 16), PAIRED * BLOCK)
        return pltpu.make_async_copy(made.at[:, at, :], out_ref.at[p, :, at, :], leave.at[p, n])

    load(0).start()
    for copy in loads:
        copy.start()
    for n in range(1, rows // PAIRED):
        load(n).start()
    for copy in loads:
        copy.wait()
    wt[...] = w[...].astype(f32).T.astype(bf16)
    bt[...] = column(bias[...])

    @pl.loop(0, rows // PAIRED)
    def _(n):
        load(n).wait()
        x = pair[pl.ds(n * PAIRED, PAIRED)].astype(f32).reshape(PAIRED * k, width)
        normed = normalize(x, gain[...], shift[...])
        values = as_rows(factor(normed, wt[...], bt[...]), k, PAIRED).astype(bf16)
        made[:, pl.ds(pl.multiple_of(n * PAIRED * BLOCK, 16), PAIRED * BLOCK), :] = values
        for p in range(parts):
            store(p, n).start()

    @pl.loop(0, rows // PAIRED)
    def _(n):
        for p in range(parts):
            store(p, n).wait()


def left_kernel(pair_ref, gain_ref, shift_ref, w_ref, b_ref, gw_ref, gb_ref, *refs):
    wf, bf, wt, bt = refs[-4:]
    gate_ref = refs[-5]
    outs = refs[:-5]
    k, width = pair_ref.shape[1:]
    hidden = w_ref.shape[1] // 2

    @pl.when(pl.program_id(0) == 0)
    def _():
        wf[...] = w_ref[...].astype(f32).T
        bf[...] = column(b_ref[...])
        host = lax.axis_index(("chan", "quarter"))
        for half in range(2):
            for b in range(0, len(outs), 2):
                source = [
                    pl.ds(pl.multiple_of(half * hidden + (host ^ (b + n)) * BLOCK, BLOCK), BLOCK)
                    for n in range(2)
                ]
                target = slice(half * hidden + b * BLOCK, half * hidden + (b + 2) * BLOCK)
                wt[target] = jnp.concatenate([wf[s] for s in source], axis=0).astype(bf16)
                bt[target] = jnp.concatenate([bf[s] for s in source], axis=0)

    x = pair_ref[...].astype(f32).reshape(STEP * k, width)
    normed = normalize(x, gain_ref[...], shift_ref[...])
    gate = sigmoid(dot(normed, gw_ref[...]) + gb_ref[...])
    gate_ref[...] = gate.reshape(STEP, k, width).astype(bf16)
    rows = as_rows(factor(normed, wt[...], bt[...]), k).astype(bf16)
    for b, out in enumerate(outs):
        out[...] = rows[b]


def regroup(pieces, target, matrix):
    many = SIZE // STEP
    for s in range(len(pieces) // many):
        rows = jnp.concatenate([piece() for piece in pieces[s * many : (s + 1) * many]], axis=0)
        moved = dot(matrix, rows).astype(bf16)
        for c in range(BLOCK):
            target[c, s * SIZE : (s + 1) * SIZE, :] = moved[c * SIZE : (c + 1) * SIZE]


def slices(refs):
    tall = STEP * BLOCK
    return [
        functools.partial(lambda ref, at: ref[at : at + tall, :], ref, at)
        for ref in refs
        for at in range(0, ref.shape[0], tall)
    ]


def multiply(left, right_ref, right, held, store):
    regroup(slices([right_ref]), right, shuffle(BLOCK, SIZE))
    back = shuffle(SIZE, BLOCK)
    for c in range(BLOCK):
        held[c] = dot_nt(left[c], right[c]).astype(bf16)
    for s in range(left.shape[1] // SIZE):
        parts = jnp.concatenate([held[c, s * SIZE : (s + 1) * SIZE, :] for c in range(BLOCK)], axis=0)
        moved = dot(back, parts).astype(bf16)
        for i in range(0, SIZE, STEP):
            store(s * SIZE + i, moved[i * BLOCK : (i + STEP) * BLOCK])


def gather_kernel(*refs):
    regroup(slices(refs[:-1]), refs[-1], shuffle(BLOCK, SIZE))


def product_kernel(right_ref, left, out_ref, right, held):
    rows = left.shape[1] // out_ref.shape[0]
    host = lax.axis_index(("chan", "quarter"))

    def store(i, values):
        to, at = divmod(i, rows)
        out_ref[host ^ to, at * BLOCK : (at + STEP) * BLOCK, :] = values

    multiply(left, right_ref, right, held, store)


def final_kernel(x_ref, gate_ref, g_ref, s_ref, w_ref, b_ref, out_ref, gain, shift, made, leave):
    hosts, _, j = x_ref.shape
    rows = gate_ref.shape[0]
    width = hosts * BLOCK
    gain[...] = column(g_ref[...])
    shift[...] = column(s_ref[...])

    def store(n):
        at = pl.ds(n * PAIRED, PAIRED)
        return pltpu.make_async_copy(made.at[at], out_ref.at[at], leave.at[n])

    @pl.loop(0, rows // PAIRED)
    def _(n):
        at = pl.ds(pl.multiple_of(n * PAIRED * BLOCK, 16), PAIRED * BLOCK)
        pair = x_ref[:, at].astype(f32)
        for m in range(PAIRED):
            x = pair[:, m * BLOCK : (m + 1) * BLOCK].reshape(width, j)
            centered = x - jnp.mean(x, axis=0, keepdims=True)
            variance = jnp.mean(centered * centered, axis=0, keepdims=True)
            normed = centered * lax.rsqrt(variance + epsilon)
            normed = normed * widen(gain[...], j) + widen(shift[...], j)
            outward = dot(normed.astype(bf16).T, w_ref[...]) + b_ref[...]
            row = n * PAIRED + m
            made[row] = (gate_ref[row].astype(f32) * outward).astype(bf16)
        store(n).start()

    @pl.loop(0, rows // PAIRED)
    def _(n):
        store(n).wait()


def whole(shape):
    return pl.BlockSpec(shape, lambda s: (0,) * len(shape))


def cost(flops, size):
    return pl.CostEstimate(flops=flops, bytes_accessed=size, transcendentals=0)


def params(mib=32):
    return pltpu.CompilerParams(vmem_limit_bytes=mib * MIB)


def shards(parts, pair, norm_gain, norm_shift, factor_weight, factor_bias, gate_weight, gate_bias,
           center_gain, center_shift, out_weight, out_bias):
    rows, k, width = pair.shape
    hidden = out_weight.shape[0]
    hosts = hidden // BLOCK
    steps = rows // STEP
    tall = rows * BLOCK
    mine = hosts * rows
    devices = parts * hosts
    in_part = ("chan", "quarter")
    everywhere = ("part",) + in_part
    row = lambda v: v.reshape(1, -1)
    row_block = pl.BlockSpec((STEP, k, width), lambda s: (s, 0, 0))
    work = rows * k * width
    bfloat = lambda *shape: jax.ShapeDtypeStruct(shape, bf16)

    vmem = pl.BlockSpec(memory_space=pltpu.VMEM)
    anywhere = pl.BlockSpec(memory_space=pl.ANY)
    turns = rows // PAIRED
    right = pl.pallas_call(
        right_kernel,
        in_specs=[anywhere] * 5,
        out_specs=anywhere,
        out_shape=bfloat(parts, hosts, tall, k),
        scratch_shapes=[
            pltpu.VMEM((rows, k, width), bf16),
            pltpu.VMEM((1, width), f32),
            pltpu.VMEM((1, width), f32),
            pltpu.VMEM((width, 2 * hidden), bf16),
            pltpu.VMEM((1, 2 * hidden), f32),
            pltpu.VMEM((2 * hidden, width), bf16),
            pltpu.VMEM((2 * hidden, LANES), f32),
            pltpu.VMEM((hosts, tall, k), bf16),
            pltpu.SemaphoreType.DMA((turns,)),
            pltpu.SemaphoreType.DMA((parts, turns)),
            pltpu.SemaphoreType.DMA((4,)),
        ],
        compiler_params=params(60),
        cost_estimate=cost(4 * work * hidden, 6 * work),
        name="right_factor",
    )(pair, row(norm_gain), row(norm_shift), factor_weight, row(factor_bias))
    right = lax.all_to_all(right.reshape(devices, tall, k), everywhere, 0, 0, tiled=True)

    def send(values, b):
        pairs = [(p * hosts + h, p * hosts + (h ^ b)) for p in range(parts) for h in range(hosts)]
        return lax.ppermute(values, everywhere, pairs)

    *lefts, gate = pl.pallas_call(
        left_kernel,
        grid=(steps,),
        in_specs=[
            row_block,
            whole((1, width)),
            whole((1, width)),
            whole((width, 2 * hidden)),
            whole((1, 2 * hidden)),
            whole((width, width)),
            whole((1, width)),
        ],
        out_specs=[pl.BlockSpec((STEP * BLOCK, k), lambda s: (s, 0))] * hosts + [row_block],
        out_shape=[bfloat(tall, k)] * hosts + [bfloat(*pair.shape)],
        scratch_shapes=[
            pltpu.VMEM((2 * hidden, width), f32),
            pltpu.VMEM((2 * hidden, LANES), f32),
            pltpu.VMEM((2 * hidden, width), bf16),
            pltpu.VMEM((2 * hidden, LANES), f32),
        ],
        compiler_params=params(),
        cost_estimate=cost(4 * work * hidden, 6 * work),
        name="left_factor",
    )(
        pair,
        row(norm_gain),
        row(norm_shift),
        factor_weight,
        row(factor_bias),
        gate_weight,
        row(gate_bias),
    )
    lefts = [lefts[0]] + [send(lefts[b], b) for b in reversed(range(1, hosts))][::-1]

    left = pl.pallas_call(
        gather_kernel,
        in_specs=[vmem] * hosts,
        out_specs=vmem,
        out_shape=bfloat(BLOCK, mine, k),
        compiler_params=params(),
        cost_estimate=cost(2 * work * BLOCK * SIZE, 4 * work),
        name="gather_left",
    )(*lefts)

    span = GATHER * rows
    product = pl.pallas_call(
        product_kernel,
        grid=(devices // GATHER,),
        in_specs=[pl.BlockSpec((span * BLOCK, k), lambda s: (s, 0)), whole((BLOCK, mine, k))],
        out_specs=pl.BlockSpec((hosts, tall, span), lambda s: (0, 0, s)),
        out_shape=bfloat(hosts, tall, devices * rows),
        scratch_shapes=[pltpu.VMEM((BLOCK, span, k), bf16), pltpu.VMEM((BLOCK, mine, span), bf16)],
        compiler_params=params(40),
        cost_estimate=cost(2 * BLOCK * mine * mine * k, 6 * BLOCK * mine * k),
        name="products",
    )(right.reshape(devices * tall, k), left)
    product = lax.all_to_all(product, in_part, 0, 0, tiled=True)

    return pl.pallas_call(
        final_kernel,
        in_specs=[vmem] * 6,
        out_specs=anywhere,
        out_shape=bfloat(*pair.shape),
        scratch_shapes=[
            pltpu.VMEM((hidden, LANES), f32),
            pltpu.VMEM((hidden, LANES), f32),
            pltpu.VMEM(pair.shape, bf16),
            pltpu.SemaphoreType.DMA((turns,)),
        ],
        compiler_params=params(),
        cost_estimate=cost(2 * work * width, 6 * work),
        name="update",
    )(product, gate, row(center_gain), row(center_shift), out_weight, row(out_bias))


def solution(mesh):
    groups, chan, quarter = (mesh.shape[a] for a in ("groups", "chan", "quarter"))
    near = CHANNELS // BLOCK // quarter
    parts = chan // near
    split = Mesh(
        mesh.devices.reshape(groups, parts, near, quarter), ("groups", "part", "chan", "quarter")
    )
    rows = P(("groups", "part", "chan", "quarter"), None, None)
    return jax.shard_map(
        functools.partial(shards, parts),
        mesh=split,
        in_specs=(rows,) + (P(),) * 10,
        out_specs=rows,
        check_vma=False,
    )
```

```python
import functools

import jax
import jax.numpy as jnp
from jax import lax
from jax.experimental import pallas as pl
from jax.experimental.pallas import tpu as pltpu
from jax.sharding import Mesh
from jax.sharding import PartitionSpec as P

epsilon = 1e-05
CHANNELS = 128
BLOCK = 8
STEP = 4
SIZE = 32
LANES = 128
GATHER = 32
MIB = 1024 * 1024

f32, bf16 = jnp.float32, jnp.bfloat16


def sigmoid(x):
    return 0.5 * jnp.tanh(0.5 * x) + 0.5


def dot(a, b):
    return jnp.dot(a, b, preferred_element_type=f32)


def dot_nt(a, b):
    return lax.dot_general(a, b, (((1,), (1,)), ((), ())), preferred_element_type=f32)


def column(row):
    blocks = [
        jnp.broadcast_to(row[:, k : k + LANES], (LANES, LANES)).T
        for k in range(0, row.shape[1], LANES)
    ]
    return jnp.concatenate(blocks, axis=0)


def widen(col, width):
    return jnp.concatenate([col] * (width // LANES), axis=1)


def shuffle(groups, size):
    n = groups * size
    out = lax.broadcasted_iota(jnp.int32, (n, n), 0)
    row = lax.broadcasted_iota(jnp.int32, (n, n), 1)
    want = (out % size) * groups + out // size
    return jnp.where(want == row, 1.0, 0.0).astype(bf16)


def normalize(x, gain, shift):
    centered = x - jnp.mean(x, axis=1, keepdims=True)
    variance = jnp.mean(centered * centered, axis=1, keepdims=True)
    return (centered * lax.rsqrt(variance + epsilon) * gain + shift).astype(bf16)


def factor(normed, wt, bias):
    width = wt.shape[0] // 2
    both = dot_nt(wt, normed) + widen(bias, normed.shape[0])
    return sigmoid(both[:width]) * both[width:]


def as_rows(values, k):
    hosts = values.shape[0] // BLOCK
    return jnp.concatenate(
        [values[:, r * k : (r + 1) * k].reshape(hosts, BLOCK, k) for r in range(STEP)], axis=1
    )


def right_kernel(pair_ref, gain_ref, shift_ref, w_ref, b_ref, out_ref, wt, bt):
    @pl.when(pl.program_id(0) == 0)
    def _():
        wt[...] = w_ref[...].astype(f32).T.astype(bf16)
        bt[...] = column(b_ref[...])

    k, width = pair_ref.shape[1:]
    x = pair_ref[...].astype(f32).reshape(STEP * k, width)
    normed = normalize(x, gain_ref[...], shift_ref[...])
    out = as_rows(factor(normed, wt[...], bt[...]), k).astype(bf16)
    for p in range(out_ref.shape[0]):
        out_ref[p] = out


def left_kernel(pair_ref, gain_ref, shift_ref, w_ref, b_ref, gw_ref, gb_ref, *refs):
    wf, bf, wt, bt = refs[-4:]
    gate_ref = refs[-5]
    outs = refs[:-5]
    k, width = pair_ref.shape[1:]
    hidden = w_ref.shape[1] // 2

    @pl.when(pl.program_id(0) == 0)
    def _():
        wf[...] = w_ref[...].astype(f32).T
        bf[...] = column(b_ref[...])
        host = lax.axis_index(("chan", "quarter"))
        for half in range(2):
            for b in range(0, len(outs), 2):
                source = [
                    pl.ds(pl.multiple_of(half * hidden + (host ^ (b + n)) * BLOCK, BLOCK), BLOCK)
                    for n in range(2)
                ]
                target = slice(half * hidden + b * BLOCK, half * hidden + (b + 2) * BLOCK)
                wt[target] = jnp.concatenate([wf[s] for s in source], axis=0).astype(bf16)
                bt[target] = jnp.concatenate([bf[s] for s in source], axis=0)

    x = pair_ref[...].astype(f32).reshape(STEP * k, width)
    normed = normalize(x, gain_ref[...], shift_ref[...])
    gate = sigmoid(dot(normed, gw_ref[...]) + gb_ref[...])
    gate_ref[...] = gate.reshape(STEP, k, width).astype(bf16)
    rows = as_rows(factor(normed, wt[...], bt[...]), k).astype(bf16)
    for b, out in enumerate(outs):
        out[...] = rows[b]


def regroup(pieces, target, matrix):
    many = SIZE // STEP
    for s in range(len(pieces) // many):
        rows = jnp.concatenate([piece() for piece in pieces[s * many : (s + 1) * many]], axis=0)
        moved = dot(matrix, rows).astype(bf16)
        for c in range(BLOCK):
            target[c, s * SIZE : (s + 1) * SIZE, :] = moved[c * SIZE : (c + 1) * SIZE]


def slices(refs):
    tall = STEP * BLOCK
    return [
        functools.partial(lambda ref, at: ref[at : at + tall, :], ref, at)
        for ref in refs
        for at in range(0, ref.shape[0], tall)
    ]


def multiply(left, right_ref, right, held, store):
    regroup(slices([right_ref]), right, shuffle(BLOCK, SIZE))
    back = shuffle(SIZE, BLOCK)
    for c in range(BLOCK):
        held[c] = dot_nt(left[c], right[c]).astype(bf16)
    for s in range(left.shape[1] // SIZE):
        parts = jnp.concatenate([held[c, s * SIZE : (s + 1) * SIZE, :] for c in range(BLOCK)], axis=0)
        moved = dot(back, parts).astype(bf16)
        for i in range(0, SIZE, STEP):
            store(s * SIZE + i, moved[i * BLOCK : (i + STEP) * BLOCK])


def gather_kernel(*refs):
    regroup(slices(refs[:-1]), refs[-1], shuffle(BLOCK, SIZE))


def product_kernel(right_ref, left, out_ref, right, held):
    rows = left.shape[1] // out_ref.shape[0]
    host = lax.axis_index(("chan", "quarter"))

    def store(i, values):
        to, at = divmod(i, rows)
        out_ref[host ^ to, at * BLOCK : (at + STEP) * BLOCK, :] = values

    multiply(left, right_ref, right, held, store)


def final_kernel(x_ref, gate_ref, g_ref, s_ref, w_ref, b_ref, out_ref, made, leave):
    hosts, _, j = x_ref.shape
    rows = gate_ref.shape[0]
    width = hosts * BLOCK
    gain, shift = widen(column(g_ref[...]), j), widen(column(s_ref[...]), j)
    stores = []
    for r in range(0, rows, 2):
        pair = x_ref[:, r * BLOCK : (r + 2) * BLOCK].astype(f32)
        for n in range(2):
            x = pair[:, n * BLOCK : (n + 1) * BLOCK].reshape(width, j)
            centered = x - jnp.mean(x, axis=0, keepdims=True)
            variance = jnp.mean(centered * centered, axis=0, keepdims=True)
            normed = centered * lax.rsqrt(variance + epsilon) * gain + shift
            outward = dot(normed.astype(bf16).T, w_ref[...]) + b_ref[...]
            made[r + n] = (gate_ref[r + n].astype(f32) * outward).astype(bf16)
        at = pl.ds(r, 2)
        stores.append(pltpu.make_async_copy(made.at[at], out_ref.at[at], leave.at[r // 2]))
        stores[-1].start()
    for store in stores:
        store.wait()


def whole(shape):
    return pl.BlockSpec(shape, lambda s: (0,) * len(shape))


def cost(flops, size):
    return pl.CostEstimate(flops=flops, bytes_accessed=size, transcendentals=0)


def params(mib=32):
    return pltpu.CompilerParams(vmem_limit_bytes=mib * MIB)


def shards(parts, pair, norm_gain, norm_shift, factor_weight, factor_bias, gate_weight, gate_bias,
           center_gain, center_shift, out_weight, out_bias):
    rows, k, width = pair.shape
    hidden = out_weight.shape[0]
    hosts = hidden // BLOCK
    steps = rows // STEP
    tall = rows * BLOCK
    mine = hosts * rows
    devices = parts * hosts
    in_part = ("chan", "quarter")
    everywhere = ("part",) + in_part
    row = lambda v: v.reshape(1, -1)
    row_block = pl.BlockSpec((STEP, k, width), lambda s: (s, 0, 0))
    work = rows * k * width
    bfloat = lambda *shape: jax.ShapeDtypeStruct(shape, bf16)

    vmem = pl.BlockSpec(memory_space=pltpu.VMEM)
    anywhere = pl.BlockSpec(memory_space=pl.ANY)
    right = pl.pallas_call(
        right_kernel,
        grid=(steps,),
        in_specs=[
            row_block,
            whole((1, width)),
            whole((1, width)),
            pl.BlockSpec((width, 2 * hidden), lambda s: (0, 1)),
            pl.BlockSpec((1, 2 * hidden), lambda s: (0, 1)),
        ],
        out_specs=pl.BlockSpec((parts, hosts, STEP * BLOCK, k), lambda s: (0, 0, s, 0)),
        out_shape=bfloat(parts, hosts, tall, k),
        scratch_shapes=[pltpu.VMEM((2 * hidden, width), bf16), pltpu.VMEM((2 * hidden, LANES), f32)],
        compiler_params=params(60),
        cost_estimate=cost(4 * work * hidden, 6 * work),
        name="right_factor",
    )(pair, row(norm_gain), row(norm_shift), factor_weight, row(factor_bias))
    right = lax.all_to_all(right.reshape(devices, tall, k), everywhere, 0, 0, tiled=True)

    def send(values, b):
        pairs = [(p * hosts + h, p * hosts + (h ^ b)) for p in range(parts) for h in range(hosts)]
        return lax.ppermute(values, everywhere, pairs)

    *lefts, gate = pl.pallas_call(
        left_kernel,
        grid=(steps,),
        in_specs=[
            row_block,
            whole((1, width)),
            whole((1, width)),
            whole((width, 2 * hidden)),
            whole((1, 2 * hidden)),
            whole((width, width)),
            whole((1, width)),
        ],
        out_specs=[pl.BlockSpec((STEP * BLOCK, k), lambda s: (s, 0))] * hosts + [row_block],
        out_shape=[bfloat(tall, k)] * hosts + [bfloat(*pair.shape)],
        scratch_shapes=[
            pltpu.VMEM((2 * hidden, width), f32),
            pltpu.VMEM((2 * hidden, LANES), f32),
            pltpu.VMEM((2 * hidden, width), bf16),
            pltpu.VMEM((2 * hidden, LANES), f32),
        ],
        compiler_params=params(),
        cost_estimate=cost(4 * work * hidden, 6 * work),
        name="left_factor",
    )(
        pair,
        row(norm_gain),
        row(norm_shift),
        factor_weight,
        row(factor_bias),
        gate_weight,
        row(gate_bias),
    )
    lefts = [lefts[0]] + [send(lefts[b], b) for b in reversed(range(1, hosts))][::-1]

    left = pl.pallas_call(
        gather_kernel,
        in_specs=[vmem] * hosts,
        out_specs=vmem,
        out_shape=bfloat(BLOCK, mine, k),
        compiler_params=params(),
        cost_estimate=cost(2 * work * BLOCK * SIZE, 4 * work),
        name="gather_left",
    )(*lefts)

    span = GATHER * rows
    product = pl.pallas_call(
        product_kernel,
        grid=(devices // GATHER,),
        in_specs=[pl.BlockSpec((span * BLOCK, k), lambda s: (s, 0)), whole((BLOCK, mine, k))],
        out_specs=pl.BlockSpec((hosts, tall, span), lambda s: (0, 0, s)),
        out_shape=bfloat(hosts, tall, devices * rows),
        scratch_shapes=[pltpu.VMEM((BLOCK, span, k), bf16), pltpu.VMEM((BLOCK, mine, span), bf16)],
        compiler_params=params(40),
        cost_estimate=cost(2 * BLOCK * mine * mine * k, 6 * BLOCK * mine * k),
        name="products",
    )(right.reshape(devices * tall, k), left)
    product = lax.all_to_all(product, in_part, 0, 0, tiled=True)

    return pl.pallas_call(
        final_kernel,
        in_specs=[vmem] * 6,
        out_specs=anywhere,
        out_shape=bfloat(*pair.shape),
        scratch_shapes=[pltpu.VMEM(pair.shape, bf16), pltpu.SemaphoreType.DMA((rows // 2,))],
        compiler_params=params(),
        cost_estimate=cost(2 * work * width, 6 * work),
        name="update",
    )(product, gate, row(center_gain), row(center_shift), out_weight, row(out_bias))


def solution(mesh):
    groups, chan, quarter = (mesh.shape[a] for a in ("groups", "chan", "quarter"))
    near = CHANNELS // BLOCK // quarter
    parts = chan // near
    split = Mesh(
        mesh.devices.reshape(groups, parts, near, quarter), ("groups", "part", "chan", "quarter")
    )
    rows = P(("groups", "part", "chan", "quarter"), None, None)
    return jax.shard_map(
        functools.partial(shards, parts),
        mesh=split,
        in_specs=(rows,) + (P(),) * 10,
        out_specs=rows,
        check_vma=False,
    )
```

```python
import functools

import jax
import jax.numpy as jnp
from jax import lax
from jax.experimental import pallas as pl
from jax.experimental.pallas import tpu as pltpu
from jax.sharding import Mesh
from jax.sharding import PartitionSpec as P

epsilon = 1e-05
CHANNELS = 128
BLOCK = 8
STEP = 4
SIZE = 32
LANES = 128
PAIRED = 2
EARLY = 8
GATHER = 32
MIB = 1024 * 1024

f32, bf16 = jnp.float32, jnp.bfloat16


def sigmoid(x):
    return 0.5 * jnp.tanh(0.5 * x) + 0.5


def dot(a, b):
    return jnp.dot(a, b, preferred_element_type=f32)


def dot_nt(a, b):
    return lax.dot_general(a, b, (((1,), (1,)), ((), ())), preferred_element_type=f32)


def column(row):
    blocks = [
        jnp.broadcast_to(row[:, k : k + LANES], (LANES, LANES)).T
        for k in range(0, row.shape[1], LANES)
    ]
    return jnp.concatenate(blocks, axis=0)


def widen(col, width):
    return jnp.concatenate([col] * (width // LANES), axis=1)


def shuffle(groups, size):
    n = groups * size
    out = lax.broadcasted_iota(jnp.int32, (n, n), 0)
    row = lax.broadcasted_iota(jnp.int32, (n, n), 1)
    want = (out % size) * groups + out // size
    return jnp.where(want == row, 1.0, 0.0).astype(bf16)


def normalize(x, gain, shift):
    centered = x - jnp.mean(x, axis=1, keepdims=True)
    variance = jnp.mean(centered * centered, axis=1, keepdims=True)
    return (centered * lax.rsqrt(variance + epsilon) * gain + shift).astype(bf16)


def factor(normed, wt, bias):
    width = wt.shape[0] // 2
    both = dot_nt(wt, normed) + widen(bias, normed.shape[0])
    return sigmoid(both[:width]) * both[width:]


def as_rows(values, k):
    hosts = values.shape[0] // BLOCK
    return jnp.concatenate(
        [values[:, r * k : (r + 1) * k].reshape(hosts, BLOCK, k) for r in range(STEP)], axis=1
    )


def early_kernel(pair_ref, gain_ref, shift_ref, w_ref, b_ref, out_ref, wt, bt):
    @pl.when(pl.program_id(0) == 0)
    def _():
        wt[...] = w_ref[...].astype(f32).T.astype(bf16)
        bt[...] = column(b_ref[...])

    k, width = pair_ref.shape[1:]
    x = pair_ref[...].astype(f32).reshape(STEP * k, width)
    normed = normalize(x, gain_ref[...], shift_ref[...])
    out = as_rows(factor(normed, wt[...], bt[...]), k).astype(bf16)
    for p in range(out_ref.shape[0]):
        out_ref[p] = out


def left_kernel(own_ref, other_ref, gain_ref, shift_ref, w_ref, b_ref, *refs):
    wf, bf, wt, bt = refs[-4:]
    outs = refs[:-4]
    k, width = own_ref.shape[1:]
    hidden = w_ref.shape[1] // 2
    near = len(outs) * BLOCK
    step = pl.program_id(0)

    @pl.when(step == 0)
    def _():
        wf[...] = w_ref[...].astype(f32).T
        bf[...] = column(b_ref[...])
        host = lax.axis_index(("chan", "quarter"))
        for half in range(2):
            for m in range(0, len(outs), 2):
                source = [
                    pl.ds(
                        pl.multiple_of(half * hidden + (host ^ (2 * (m + n))) * BLOCK, BLOCK), BLOCK
                    )
                    for n in range(2)
                ]
                target = slice(half * near + m * BLOCK, half * near + (m + 2) * BLOCK)
                wt[target] = jnp.concatenate([wf[s] for s in source], axis=0).astype(bf16)
                bt[target] = jnp.concatenate([bf[s] for s in source], axis=0)

    pair = jnp.where(step < pl.num_programs(0) // 2, own_ref[...], other_ref[...])
    normed = normalize(pair.astype(f32).reshape(STEP * k, width), gain_ref[...], shift_ref[...])
    rows = as_rows(factor(normed, wt[...], bt[...]), k).astype(bf16)
    for m, out in enumerate(outs):
        out[...] = rows[m]


def late_kernel(pair_ref, gain_ref, shift_ref, w_ref, b_ref, *refs):
    out_ref = refs[-1]
    k, width = pair_ref.shape[1:]
    x = pair_ref[...].astype(f32).reshape(STEP * k, width)
    normed = normalize(x, gain_ref[...], shift_ref[...])
    wt = w_ref[...].astype(f32).T.astype(bf16)
    out = as_rows(factor(normed, wt, column(b_ref[...])), k).astype(bf16)
    for p in range(out_ref.shape[0]):
        out_ref[p] = out


def gate_kernel(pair_ref, gain_ref, shift_ref, gw_ref, gb_ref, gate_ref):
    k, width = pair_ref.shape[1:]
    x = pair_ref[...].astype(f32).reshape(STEP * k, width)
    normed = normalize(x, gain_ref[...], shift_ref[...])
    gate = sigmoid(dot(normed, gw_ref[...]) + gb_ref[...])
    gate_ref[...] = gate.reshape(gate_ref.shape).astype(gate_ref.dtype)


def regroup(pieces, target, matrix):
    many = SIZE // STEP
    for s in range(len(pieces) // many):
        rows = jnp.concatenate([piece() for piece in pieces[s * many : (s + 1) * many]], axis=0)
        moved = dot(matrix, rows).astype(bf16)
        for c in range(BLOCK):
            target[c, s * SIZE : (s + 1) * SIZE, :] = moved[c * SIZE : (c + 1) * SIZE]


def slices(refs):
    tall = STEP * BLOCK
    return [
        functools.partial(lambda ref, at: ref[at : at + tall, :], ref, at)
        for ref in refs
        for at in range(0, ref.shape[0], tall)
    ]


def multiply(left, right_ref, right, held, store):
    regroup(slices([right_ref]), right, shuffle(BLOCK, SIZE))
    back = shuffle(SIZE, BLOCK)
    for c in range(BLOCK):
        held[c] = dot_nt(left[c], right[c]).astype(bf16)
    for s in range(left.shape[1] // SIZE):
        parts = jnp.concatenate([held[c, s * SIZE : (s + 1) * SIZE, :] for c in range(BLOCK)], axis=0)
        moved = dot(back, parts).astype(bf16)
        for i in range(0, SIZE, STEP):
            store(s * SIZE + i, moved[i * BLOCK : (i + STEP) * BLOCK])


def first_kernel(hosts, right_ref, *refs):
    chips = hosts // 2
    lefts, outs = refs[:chips], refs[chips + 1 : chips + 1 + hosts]
    left_ref, arrived, left, right, held, sems, sem = refs[chips + 1 + hosts :]
    loads = [
        pltpu.make_async_copy(ref, arrived.at[m], sems.at[m]) for m, ref in enumerate(lefts)
    ]
    keep = pltpu.make_async_copy(left, left_ref, sem)
    step = pl.program_id(0)

    @pl.when(step == 0)
    def _():
        for load in loads:
            load.start()
        for load in loads:
            load.wait()
        regroup(slices([arrived.at[m] for m in range(chips)]), left, shuffle(BLOCK, SIZE))
        keep.start()

    rows = left.shape[1] // hosts

    def store(i, values):
        to, at = divmod(i, rows)
        outs[to][at * BLOCK : (at + STEP) * BLOCK, :] = values

    multiply(left, right_ref, right, held, store)

    @pl.when(step == 0)
    def _():
        keep.wait()


def second_kernel(right_ref, left_ref, *refs):
    out_ref, left, right, held, sem = refs[-5:]
    load = pltpu.make_async_copy(left_ref, left, sem)

    @pl.when(pl.program_id(0) == 0)
    def _():
        load.start()
        load.wait()

    rows = left.shape[1] // out_ref.shape[0]
    host = lax.axis_index(("chan", "quarter"))

    def store(i, values):
        to, at = divmod(i, rows)
        out_ref[host ^ to, at * BLOCK : (at + STEP) * BLOCK, :] = values

    multiply(left, right_ref, right, held, store)


def collect_kernel(*refs):
    out_ref, sems = refs[-2:]
    host = lax.axis_index(("chan", "quarter"))
    copies = [
        pltpu.make_async_copy(ref, out_ref.at[host ^ b], sems.at[b])
        for b, ref in enumerate(refs[:-2])
    ]
    for copy in copies:
        copy.start()
    for copy in copies:
        copy.wait()


def final_kernel(
    first_ref, second_ref, gate_ref, g_ref, s_ref, w_ref, b_ref, out_ref, gate, weight, made,
    arrive, leave, sem,
):
    hosts, _, lanes = first_ref.shape
    count, j, width = gate.shape
    gathers = lanes // (GATHER * EARLY)
    early = GATHER * EARLY
    span = j // gathers
    late = span - early

    def load(n):
        at = pl.ds(n * PAIRED, PAIRED)
        return pltpu.make_async_copy(gate_ref.at[at], gate.at[at], arrive.at[n])

    def store(n):
        at = pl.ds(n * PAIRED, PAIRED)
        return pltpu.make_async_copy(made.at[at], out_ref.at[at], leave.at[n])

    turns = count // PAIRED
    fetch = pltpu.make_async_copy(w_ref, weight, sem)
    fetch.start()
    for n in range(turns):
        load(n).start()
    gain, shift = widen(column(g_ref[...]), span), widen(column(s_ref[...]), span)
    each = span // GATHER
    out = lax.broadcasted_iota(jnp.int32, (span, span), 0)
    lane = lax.broadcasted_iota(jnp.int32, (span, span), 1)
    device, at = out // each, out % each
    want = jnp.where(at < EARLY, device * EARLY + at, early + device * (each - EARLY) + at - EARLY)
    order = jnp.where(want == lane, 1.0, 0.0).astype(bf16)
    fetch.wait()
    for n in range(turns):
        load(n).wait()
        rows = slice(n * PAIRED * BLOCK, (n + 1) * PAIRED * BLOCK)
        for g in range(gathers):
            x = jnp.concatenate(
                [
                    first_ref[:, rows, g * early : (g + 1) * early].astype(f32),
                    second_ref[:, rows, g * late : (g + 1) * late].astype(f32),
                ],
                axis=2,
            )
            for m in range(PAIRED):
                one = x[:, m * BLOCK : (m + 1) * BLOCK].reshape(hosts * BLOCK, span)
                centered = one - jnp.mean(one, axis=0, keepdims=True)
                variance = jnp.mean(centered * centered, axis=0, keepdims=True)
                normed = centered * lax.rsqrt(variance + epsilon) * gain + shift
                turned = dot_nt(order, normed.astype(bf16)).astype(bf16)
                outward = dot(turned, weight[...]) + b_ref[...]
                at = slice(g * span, (g + 1) * span)
                row = n * PAIRED + m
                made[row, at, :] = (gate[row, at, :].astype(f32) * outward).astype(bf16)
        store(n).start()
    for n in range(turns):
        store(n).wait()


def whole(shape):
    return pl.BlockSpec(shape, lambda s: (0,) * len(shape))


def cost(flops, size):
    return pl.CostEstimate(flops=flops, bytes_accessed=size, transcendentals=0)


def params(mib=32):
    return pltpu.CompilerParams(vmem_limit_bytes=mib * MIB)


def in_hbm(x):
    return pltpu.with_memory_space_constraint(x, pltpu.HBM)


def shards(parts, pair, norm_gain, norm_shift, factor_weight, factor_bias, gate_weight, gate_bias,
           center_gain, center_shift, out_weight, out_bias):
    rows, k, width = pair.shape
    hidden = out_weight.shape[0]
    hosts = hidden // BLOCK
    steps = rows // STEP
    late = rows - EARLY
    tall = rows * BLOCK
    mine = hosts * rows
    devices = parts * hosts
    gathers = devices // GATHER
    in_part = ("chan", "quarter")
    everywhere = ("part",) + in_part
    row = lambda v: v.reshape(1, -1)
    row_block = pl.BlockSpec((STEP, k, width), lambda s: (s, 0, 0))
    work = rows * k * width
    bfloat = lambda *shape: jax.ShapeDtypeStruct(shape, bf16)

    early_right = pl.pallas_call(
        early_kernel,
        grid=(EARLY // STEP,),
        in_specs=[
            row_block,
            whole((1, width)),
            whole((1, width)),
            pl.BlockSpec((width, 2 * hidden), lambda s: (0, 1)),
            pl.BlockSpec((1, 2 * hidden), lambda s: (0, 1)),
        ],
        out_specs=pl.BlockSpec((parts, hosts, STEP * BLOCK, k), lambda s: (0, 0, s, 0)),
        out_shape=bfloat(parts, hosts, EARLY * BLOCK, k),
        scratch_shapes=[pltpu.VMEM((2 * hidden, width), bf16), pltpu.VMEM((2 * hidden, LANES), f32)],
        compiler_params=params(60),
        cost_estimate=cost(4 * work * hidden, 6 * work),
        name="early_right",
    )(pair, row(norm_gain), row(norm_shift), factor_weight, row(factor_bias))
    early_right = lax.all_to_all(
        early_right.reshape(devices, EARLY * BLOCK, k), everywhere, 0, 0, tiled=True
    )

    other = lax.ppermute(pair, "quarter", [(0, 1), (1, 0)])
    chips = hosts // 2
    *lefts, = pl.pallas_call(
        left_kernel,
        grid=(2 * steps,),
        in_specs=[
            pl.BlockSpec((STEP, k, width), lambda s: (jnp.minimum(s, steps - 1), 0, 0)),
            pl.BlockSpec((STEP, k, width), lambda s: (jnp.maximum(s - steps, 0), 0, 0)),
            whole((1, width)),
            whole((1, width)),
            whole((width, 2 * hidden)),
            whole((1, 2 * hidden)),
        ],
        out_specs=[pl.BlockSpec((STEP * BLOCK, k), lambda s: (s, 0))] * chips,
        out_shape=[bfloat(2 * tall, k)] * chips,
        scratch_shapes=[
            pltpu.VMEM((2 * hidden, width), f32),
            pltpu.VMEM((2 * hidden, LANES), f32),
            pltpu.VMEM((hidden, width), bf16),
            pltpu.VMEM((hidden, LANES), f32),
        ],
        compiler_params=params(),
        cost_estimate=cost(4 * work * hidden, 6 * work),
        name="left_factor",
    )(pair, other, row(norm_gain), row(norm_shift), factor_weight, row(factor_bias))

    def send(values, b):
        pairs = [(p * hosts + h, p * hosts + (h ^ b)) for p in range(parts) for h in range(hosts)]
        return lax.ppermute(values, everywhere, pairs)

    lefts = [lefts[0]] + [send(lefts[m], 2 * m) for m in range(1, chips)]

    lefts = [in_hbm(x) for x in lefts]
    soon = lefts[1 : chips // 2]
    late_right = pl.pallas_call(
        late_kernel,
        grid=(late // STEP,),
        in_specs=[
            pl.BlockSpec((STEP, k, width), lambda s: (s + EARLY // STEP, 0, 0)),
            whole((1, width)),
            whole((1, width)),
            pl.BlockSpec((width, 2 * hidden), lambda s: (0, 1)),
            pl.BlockSpec((1, 2 * hidden), lambda s: (0, 1)),
        ]
        + [pl.BlockSpec(memory_space=pl.ANY)] * len(soon),
        out_specs=pl.BlockSpec((parts, hosts, STEP * BLOCK, k), lambda s: (0, 0, s, 0)),
        out_shape=pltpu.HBM((parts, hosts, late * BLOCK, k), bf16),
        compiler_params=params(),
        cost_estimate=cost(2 * work * hidden, 2 * work),
        name="late_right",
    )(pair, row(norm_gain), row(norm_shift), factor_weight, row(factor_bias), *soon)
    late_right = lax.all_to_all(
        late_right.reshape(devices, late * BLOCK, k), everywhere, 0, 0, tiled=True
    )

    gate = pl.pallas_call(
        gate_kernel,
        grid=(steps,),
        in_specs=[
            row_block,
            whole((1, width)),
            whole((1, width)),
            whole((width, width)),
            whole((1, width)),
        ],
        out_specs=row_block,
        out_shape=pltpu.HBM(pair.shape, bf16),
        compiler_params=params(),
        cost_estimate=cost(1 << 37, 4 * work),
        name="gate",
    )(pair, row(norm_gain), row(norm_shift), gate_weight, row(gate_bias))

    first = GATHER * EARLY
    second = GATHER * late
    spent = cost(2 * BLOCK * mine * mine * k, 6 * BLOCK * mine * k)
    vmem = pl.BlockSpec(memory_space=pltpu.VMEM)
    anywhere = pl.BlockSpec(memory_space=pl.ANY)
    grouped = (BLOCK, mine, k)
    *firsts, left = pl.pallas_call(
        functools.partial(first_kernel, hosts),
        grid=(gathers,),
        in_specs=[pl.BlockSpec((first * BLOCK, k), lambda s: (s, 0))] + [anywhere] * (chips + 1),
        out_specs=[pl.BlockSpec((tall, first), lambda s: (0, s))] * hosts + [anywhere],
        out_shape=[bfloat(tall, gathers * first)] * hosts + [pltpu.HBM(grouped, bf16)],
        scratch_shapes=[
            pltpu.VMEM((chips, 2 * tall, k), bf16),
            pltpu.VMEM(grouped, bf16),
            pltpu.VMEM((BLOCK, first, k), bf16),
            pltpu.VMEM((BLOCK, mine, first), bf16),
            pltpu.SemaphoreType.DMA((chips,)),
            pltpu.SemaphoreType.DMA,
        ],
        compiler_params=params(40),
        cost_estimate=spent,
        name="first_products",
    )(early_right.reshape(devices * EARLY * BLOCK, k), *lefts, in_hbm(gate))
    firsts = [firsts[0]] + [send(firsts[b], b) for b in range(1, hosts)]
    firsts = [in_hbm(x) for x in firsts]

    forced = firsts[hosts // 2 :]
    seconds = pl.pallas_call(
        second_kernel,
        grid=(gathers,),
        in_specs=[pl.BlockSpec((second * BLOCK, k), lambda s: (s, 0))]
        + [anywhere] * (1 + len(forced)),
        out_specs=pl.BlockSpec((hosts, tall, second), lambda s: (0, 0, s)),
        out_shape=pltpu.HBM((hosts, tall, gathers * second), bf16),
        scratch_shapes=[
            pltpu.VMEM(grouped, bf16),
            pltpu.VMEM((BLOCK, second, k), bf16),
            pltpu.VMEM((BLOCK, mine, second), bf16),
            pltpu.SemaphoreType.DMA,
        ],
        compiler_params=params(),
        cost_estimate=spent,
        name="second_products",
    )(late_right.reshape(devices * late * BLOCK, k), in_hbm(left), *forced)
    seconds = lax.all_to_all(seconds, in_part, 0, 0, tiled=True)

    firsts = pl.pallas_call(
        collect_kernel,
        in_specs=[anywhere] * hosts,
        out_specs=vmem,
        out_shape=bfloat(hosts, tall, gathers * first),
        scratch_shapes=[pltpu.SemaphoreType.DMA((hosts,))],
        compiler_params=params(),
        cost_estimate=cost(0, 4 * work),
        name="collect",
    )(*firsts)

    turns = rows // PAIRED
    return pl.pallas_call(
        final_kernel,
        in_specs=[vmem] * 2 + [anywhere] + [vmem] * 2 + [anywhere, vmem],
        out_specs=anywhere,
        out_shape=bfloat(*pair.shape),
        scratch_shapes=[
            pltpu.VMEM(pair.shape, bf16),
            pltpu.VMEM(out_weight.shape, bf16),
            pltpu.VMEM(pair.shape, bf16),
            pltpu.SemaphoreType.DMA((turns,)),
            pltpu.SemaphoreType.DMA((turns,)),
            pltpu.SemaphoreType.DMA,
        ],
        compiler_params=params(40),
        cost_estimate=cost(2 * work * width, 6 * work),
        name="update",
    )(
        firsts,
        seconds,
        in_hbm(gate),
        row(center_gain),
        row(center_shift),
        in_hbm(out_weight),
        row(out_bias),
    )


def solution(mesh):
    groups, chan, quarter = (mesh.shape[a] for a in ("groups", "chan", "quarter"))
    near = CHANNELS // BLOCK // quarter
    parts = chan // near
    split = Mesh(
        mesh.devices.reshape(groups, parts, near, quarter), ("groups", "part", "chan", "quarter")
    )
    rows = P(("groups", "part", "chan", "quarter"), None, None)
    return jax.shard_map(
        functools.partial(shards, parts),
        mesh=split,
        in_specs=(rows,) + (P(),) * 10,
        out_specs=rows,
        check_vma=False,
    )
```

```python
import functools

import jax
import jax.numpy as jnp
from jax import lax
from jax.experimental import pallas as pl
from jax.experimental.pallas import tpu as pltpu
from jax.sharding import Mesh
from jax.sharding import PartitionSpec as P

epsilon = 1e-05
CHANNELS = 128
BLOCK = 8
STEP = 4
PAIRED = 2
SIZE = 32
LANES = 128
GATHER = 32
MIB = 1024 * 1024

f32, bf16 = jnp.float32, jnp.bfloat16


def sigmoid(x):
    return 0.5 * jnp.tanh(0.5 * x) + 0.5


def dot(a, b):
    return jnp.dot(a, b, preferred_element_type=f32)


def dot_nt(a, b):
    return lax.dot_general(a, b, (((1,), (1,)), ((), ())), preferred_element_type=f32)


def column(row):
    blocks = [
        jnp.broadcast_to(row[:, k : k + LANES], (LANES, LANES)).T
        for k in range(0, row.shape[1], LANES)
    ]
    return jnp.concatenate(blocks, axis=0)


def widen(col, width):
    return jnp.concatenate([col] * (width // LANES), axis=1)


def shuffle(groups, size):
    n = groups * size
    out = lax.broadcasted_iota(jnp.int32, (n, n), 0)
    row = lax.broadcasted_iota(jnp.int32, (n, n), 1)
    want = (out % size) * groups + out // size
    return jnp.where(want == row, 1.0, 0.0).astype(bf16)


def normalize(x, gain, shift):
    centered = x - jnp.mean(x, axis=1, keepdims=True)
    variance = jnp.mean(centered * centered, axis=1, keepdims=True)
    return (centered * lax.rsqrt(variance + epsilon) * gain + shift).astype(bf16)


def factor(normed, wt, bias):
    width = wt.shape[0] // 2
    both = dot_nt(wt, normed) + widen(bias, normed.shape[0])
    return sigmoid(both[:width]) * both[width:]


def as_rows(values, k, step=STEP):
    hosts = values.shape[0] // BLOCK
    return jnp.concatenate(
        [values[:, r * k : (r + 1) * k].reshape(hosts, BLOCK, k) for r in range(step)], axis=1
    )


def turns_of(rows):
    cuts = [0, PAIRED, *range(PAIRED + STEP, rows - PAIRED + 1, STEP), rows]
    return list(zip(cuts[:-1], (n - m for m, n in zip(cuts[:-1], cuts[1:]))))


def right_kernel(
    pair_ref, gain_ref, shift_ref, w_ref, b_ref, out_ref, pair, gain, shift, w, bias, made,
    arrive, leave, sems,
):
    rows, k, width = pair.shape
    half = w.shape[1]
    turns = turns_of(rows)
    loads = [
        pltpu.make_async_copy(pair_ref.at[pl.ds(r, size)], pair.at[pl.ds(r, size)], arrive.at[n])
        for n, (r, size) in enumerate(turns)
    ]
    small = [
        pltpu.make_async_copy(ref, to, sems.at[n])
        for n, (ref, to) in enumerate(
            [
                (w_ref.at[:, pl.ds(half, half)], w),
                (b_ref.at[:, pl.ds(half, half)], bias),
                (gain_ref, gain),
                (shift_ref, shift),
            ]
        )
    ]
    for copy in loads[:1] + small + loads[1:]:
        copy.start()
    for copy in small:
        copy.wait()
    wt = w[...].astype(f32).T.astype(bf16)
    bt = column(bias[...])
    stores = []
    for n, (r, size) in enumerate(turns):
        loads[n].wait()
        x = pair[r : r + size].astype(f32).reshape(size * k, width)
        normed = normalize(x, gain[...], shift[...])
        at = pl.ds(r * BLOCK, size * BLOCK)
        made[:, at, :] = as_rows(factor(normed, wt, bt), k, size).astype(bf16)
        for p in range(out_ref.shape[0]):
            stores.append(
                pltpu.make_async_copy(made.at[:, at, :], out_ref.at[p, :, at, :], leave.at[p, n])
            )
            stores[-1].start()
    for store in stores:
        store.wait()


def left_kernel(pair_ref, gain_ref, shift_ref, w_ref, b_ref, gw_ref, gb_ref, *refs):
    wf, bf, wt, bt = refs[-4:]
    gate_ref = refs[-5]
    outs = refs[:-5]
    k, width = pair_ref.shape[1:]
    hidden = w_ref.shape[1] // 2

    @pl.when(pl.program_id(0) == 0)
    def _():
        wf[...] = w_ref[...].astype(f32).T
        bf[...] = column(b_ref[...])
        host = lax.axis_index(("chan", "quarter"))
        for half in range(2):
            for b in range(0, len(outs), 2):
                source = [
                    pl.ds(pl.multiple_of(half * hidden + (host ^ (b + n)) * BLOCK, BLOCK), BLOCK)
                    for n in range(2)
                ]
                target = slice(half * hidden + b * BLOCK, half * hidden + (b + 2) * BLOCK)
                wt[target] = jnp.concatenate([wf[s] for s in source], axis=0).astype(bf16)
                bt[target] = jnp.concatenate([bf[s] for s in source], axis=0)

    x = pair_ref[...].astype(f32).reshape(STEP * k, width)
    normed = normalize(x, gain_ref[...], shift_ref[...])
    gate = sigmoid(dot(normed, gw_ref[...]) + gb_ref[...])
    gate_ref[...] = gate.reshape(STEP, k, width).astype(bf16)
    rows = as_rows(factor(normed, wt[...], bt[...]), k).astype(bf16)
    for b, out in enumerate(outs):
        out[...] = rows[b]


def regroup(pieces, target, matrix):
    many = SIZE // STEP
    for s in range(len(pieces) // many):
        rows = jnp.concatenate([piece() for piece in pieces[s * many : (s + 1) * many]], axis=0)
        moved = dot(matrix, rows).astype(bf16)
        for c in range(BLOCK):
            target[c, s * SIZE : (s + 1) * SIZE, :] = moved[c * SIZE : (c + 1) * SIZE]


def slices(refs):
    tall = STEP * BLOCK
    return [
        functools.partial(lambda ref, at: ref[at : at + tall, :], ref, at)
        for ref in refs
        for at in range(0, ref.shape[0], tall)
    ]


def multiply(left, right_ref, right, held, store):
    regroup(slices([right_ref]), right, shuffle(BLOCK, SIZE))
    back = shuffle(SIZE, BLOCK)
    for c in range(BLOCK):
        held[c] = dot_nt(left[c], right[c]).astype(bf16)
    for s in range(left.shape[1] // SIZE):
        parts = jnp.concatenate([held[c, s * SIZE : (s + 1) * SIZE, :] for c in range(BLOCK)], axis=0)
        moved = dot(back, parts).astype(bf16)
        for i in range(0, SIZE, STEP):
            store(s * SIZE + i, moved[i * BLOCK : (i + STEP) * BLOCK])


def gather_kernel(*refs):
    regroup(slices(refs[:-1]), refs[-1], shuffle(BLOCK, SIZE))


def product_kernel(right_ref, left, out_ref, right, held):
    rows = left.shape[1] // out_ref.shape[0]
    host = lax.axis_index(("chan", "quarter"))

    def store(i, values):
        to, at = divmod(i, rows)
        out_ref[host ^ to, at * BLOCK : (at + STEP) * BLOCK, :] = values

    multiply(left, right_ref, right, held, store)


def final_kernel(x_ref, gate_ref, g_ref, s_ref, w_ref, b_ref, out_ref, made, leave):
    hosts, _, j = x_ref.shape
    rows = gate_ref.shape[0]
    width = hosts * BLOCK
    gain, shift = widen(column(g_ref[...]), j), widen(column(s_ref[...]), j)
    stores = []
    for r in range(0, rows, 2):
        pair = x_ref[:, r * BLOCK : (r + 2) * BLOCK].astype(f32)
        for n in range(2):
            x = pair[:, n * BLOCK : (n + 1) * BLOCK].reshape(width, j)
            centered = x - jnp.mean(x, axis=0, keepdims=True)
            variance = jnp.mean(centered * centered, axis=0, keepdims=True)
            normed = centered * lax.rsqrt(variance + epsilon) * gain + shift
            outward = dot(normed.astype(bf16).T, w_ref[...]) + b_ref[...]
            made[r + n] = (gate_ref[r + n].astype(f32) * outward).astype(bf16)
        at = pl.ds(r, 2)
        stores.append(pltpu.make_async_copy(made.at[at], out_ref.at[at], leave.at[r // 2]))
        stores[-1].start()
    for store in stores:
        store.wait()


def whole(shape):
    return pl.BlockSpec(shape, lambda s: (0,) * len(shape))


def cost(flops, size):
    return pl.CostEstimate(flops=flops, bytes_accessed=size, transcendentals=0)


def params(mib=32):
    return pltpu.CompilerParams(vmem_limit_bytes=mib * MIB)


def shards(parts, pair, norm_gain, norm_shift, factor_weight, factor_bias, gate_weight, gate_bias,
           center_gain, center_shift, out_weight, out_bias):
    rows, k, width = pair.shape
    hidden = out_weight.shape[0]
    hosts = hidden // BLOCK
    steps = rows // STEP
    tall = rows * BLOCK
    mine = hosts * rows
    devices = parts * hosts
    in_part = ("chan", "quarter")
    everywhere = ("part",) + in_part
    row = lambda v: v.reshape(1, -1)
    row_block = pl.BlockSpec((STEP, k, width), lambda s: (s, 0, 0))
    work = rows * k * width
    bfloat = lambda *shape: jax.ShapeDtypeStruct(shape, bf16)

    vmem = pl.BlockSpec(memory_space=pltpu.VMEM)
    anywhere = pl.BlockSpec(memory_space=pl.ANY)
    turns = len(turns_of(rows))
    right = pl.pallas_call(
        right_kernel,
        in_specs=[anywhere] * 5,
        out_specs=anywhere,
        out_shape=bfloat(parts, hosts, tall, k),
        scratch_shapes=[
            pltpu.VMEM((rows, k, width), bf16),
            pltpu.VMEM((1, width), f32),
            pltpu.VMEM((1, width), f32),
            pltpu.VMEM((width, 2 * hidden), bf16),
            pltpu.VMEM((1, 2 * hidden), f32),
            pltpu.VMEM((hosts, tall, k), bf16),
            pltpu.SemaphoreType.DMA((turns,)),
            pltpu.SemaphoreType.DMA((parts, turns)),
            pltpu.SemaphoreType.DMA((4,)),
        ],
        compiler_params=params(60),
        cost_estimate=cost(4 * work * hidden, 6 * work),
        name="right_factor",
    )(pair, row(norm_gain), row(norm_shift), factor_weight, row(factor_bias))
    right = lax.all_to_all(right.reshape(devices, tall, k), everywhere, 0, 0, tiled=True)

    def send(values, b):
        pairs = [(p * hosts + h, p * hosts + (h ^ b)) for p in range(parts) for h in range(hosts)]
        return lax.ppermute(values, everywhere, pairs)

    *lefts, gate = pl.pallas_call(
        left_kernel,
        grid=(steps,),
        in_specs=[
            row_block,
            whole((1, width)),
            whole((1, width)),
            whole((width, 2 * hidden)),
            whole((1, 2 * hidden)),
            whole((width, width)),
            whole((1, width)),
        ],
        out_specs=[pl.BlockSpec((STEP * BLOCK, k), lambda s: (s, 0))] * hosts + [row_block],
        out_shape=[bfloat(tall, k)] * hosts + [bfloat(*pair.shape)],
        scratch_shapes=[
            pltpu.VMEM((2 * hidden, width), f32),
            pltpu.VMEM((2 * hidden, LANES), f32),
            pltpu.VMEM((2 * hidden, width), bf16),
            pltpu.VMEM((2 * hidden, LANES), f32),
        ],
        compiler_params=params(),
        cost_estimate=cost(4 * work * hidden, 6 * work),
        name="left_factor",
    )(
        pair,
        row(norm_gain),
        row(norm_shift),
        factor_weight,
        row(factor_bias),
        gate_weight,
        row(gate_bias),
    )
    lefts = [lefts[0]] + [send(lefts[b], b) for b in reversed(range(1, hosts))][::-1]

    left = pl.pallas_call(
        gather_kernel,
        in_specs=[vmem] * hosts,
        out_specs=vmem,
        out_shape=bfloat(BLOCK, mine, k),
        compiler_params=params(),
        cost_estimate=cost(2 * work * BLOCK * SIZE, 4 * work),
        name="gather_left",
    )(*lefts)

    span = GATHER * rows
    gathers = devices // GATHER
    if gathers == 1:
        blocks = dict(in_specs=[vmem] * 2, out_specs=vmem)
    else:
        blocks = dict(
            grid=(gathers,),
            in_specs=[pl.BlockSpec((span * BLOCK, k), lambda s: (s, 0)), whole((BLOCK, mine, k))],
            out_specs=pl.BlockSpec((hosts, tall, span), lambda s: (0, 0, s)),
        )
    product = pl.pallas_call(
        product_kernel,
        **blocks,
        out_shape=bfloat(hosts, tall, devices * rows),
        scratch_shapes=[pltpu.VMEM((BLOCK, span, k), bf16), pltpu.VMEM((BLOCK, mine, span), bf16)],
        compiler_params=params(40),
        cost_estimate=cost(2 * BLOCK * mine * mine * k, 6 * BLOCK * mine * k),
        name="products",
    )(right.reshape(devices * tall, k), left)
    product = lax.all_to_all(product, in_part, 0, 0, tiled=True)

    return pl.pallas_call(
        final_kernel,
        in_specs=[vmem] * 6,
        out_specs=anywhere,
        out_shape=bfloat(*pair.shape),
        scratch_shapes=[pltpu.VMEM(pair.shape, bf16), pltpu.SemaphoreType.DMA((rows // 2,))],
        compiler_params=params(),
        cost_estimate=cost(2 * work * width, 6 * work),
        name="update",
    )(product, gate, row(center_gain), row(center_shift), out_weight, row(out_bias))


def solution(mesh):
    groups, chan, quarter = (mesh.shape[a] for a in ("groups", "chan", "quarter"))
    near = CHANNELS // BLOCK // quarter
    parts = chan // near
    split = Mesh(
        mesh.devices.reshape(groups, parts, near, quarter), ("groups", "part", "chan", "quarter")
    )
    rows = P(("groups", "part", "chan", "quarter"), None, None)
    return jax.shard_map(
        functools.partial(shards, parts),
        mesh=split,
        in_specs=(rows,) + (P(),) * 10,
        out_specs=rows,
        check_vma=False,
    )
```

```python
import functools

import jax
import jax.numpy as jnp
from jax import lax
from jax.experimental import pallas as pl
from jax.experimental.pallas import tpu as pltpu
from jax.sharding import Mesh
from jax.sharding import PartitionSpec as P

epsilon = 1e-05
CHANNELS = 128
BLOCK = 8
STEP = 4
PAIRED = 2
SIZE = 32
LANES = 128
GATHER = 32
MIB = 1024 * 1024

f32, bf16 = jnp.float32, jnp.bfloat16


def sigmoid(x):
    return 0.5 * jnp.tanh(0.5 * x) + 0.5


def dot(a, b):
    return jnp.dot(a, b, preferred_element_type=f32)


def dot_nt(a, b):
    return lax.dot_general(a, b, (((1,), (1,)), ((), ())), preferred_element_type=f32)


def column(row):
    blocks = [
        jnp.broadcast_to(row[:, k : k + LANES], (LANES, LANES)).T
        for k in range(0, row.shape[1], LANES)
    ]
    return jnp.concatenate(blocks, axis=0)


def widen(col, width):
    return jnp.concatenate([col] * (width // LANES), axis=1)


def shuffle(groups, size):
    n = groups * size
    out = lax.broadcasted_iota(jnp.int32, (n, n), 0)
    row = lax.broadcasted_iota(jnp.int32, (n, n), 1)
    want = (out % size) * groups + out // size
    return jnp.where(want == row, 1.0, 0.0).astype(bf16)


def normalize(x, gain, shift):
    centered = x - jnp.mean(x, axis=1, keepdims=True)
    variance = jnp.mean(centered * centered, axis=1, keepdims=True)
    return (centered * lax.rsqrt(variance + epsilon) * gain + shift).astype(bf16)


def factor(normed, wt, bias):
    width = wt.shape[0] // 2
    both = dot_nt(wt, normed) + widen(bias, normed.shape[0])
    return sigmoid(both[:width]) * both[width:]


def as_rows(values, k, step=STEP):
    hosts = values.shape[0] // BLOCK
    return jnp.concatenate(
        [values[:, r * k : (r + 1) * k].reshape(hosts, BLOCK, k) for r in range(step)], axis=1
    )


def turns_of(rows):
    cuts = [0, PAIRED, *range(PAIRED + STEP, rows - PAIRED + 1, STEP), rows]
    return list(zip(cuts[:-1], (n - m for m, n in zip(cuts[:-1], cuts[1:]))))


def right_kernel(
    pair_ref, gain_ref, shift_ref, w_ref, b_ref, out_ref, pair, gain, shift, w, bias, made,
    arrive, leave, sems,
):
    rows, k, width = pair.shape
    half = w.shape[1]
    turns = turns_of(rows)
    loads = [
        pltpu.make_async_copy(pair_ref.at[pl.ds(r, size)], pair.at[pl.ds(r, size)], arrive.at[n])
        for n, (r, size) in enumerate(turns)
    ]
    small = [
        pltpu.make_async_copy(ref, to, sems.at[n])
        for n, (ref, to) in enumerate(
            [
                (w_ref.at[:, pl.ds(half, half)], w),
                (b_ref.at[:, pl.ds(half, half)], bias),
                (gain_ref, gain),
                (shift_ref, shift),
            ]
        )
    ]
    for copy in loads[:1] + small + loads[1:]:
        copy.start()
    for copy in small:
        copy.wait()
    wt = w[...].astype(f32).T.astype(bf16)
    bt = column(bias[...])
    stores = []
    for n, (r, size) in enumerate(turns):
        loads[n].wait()
        x = pair[r : r + size].astype(f32).reshape(size * k, width)
        normed = normalize(x, gain[...], shift[...])
        at = pl.ds(r * BLOCK, size * BLOCK)
        made[:, at, :] = as_rows(factor(normed, wt, bt), k, size).astype(bf16)
        for p in range(out_ref.shape[0]):
            stores.append(
                pltpu.make_async_copy(made.at[:, at, :], out_ref.at[p, :, at, :], leave.at[p, n])
            )
            stores[-1].start()
    for store in stores:
        store.wait()


def left_kernel(pair_ref, gain_ref, shift_ref, w_ref, b_ref, gw_ref, gb_ref, *refs):
    wf, bf, wt, bt = refs[-4:]
    gate_ref = refs[-5]
    outs = refs[:-5]
    k, width = pair_ref.shape[1:]
    hidden = w_ref.shape[1] // 2

    @pl.when(pl.program_id(0) == 0)
    def _():
        wf[...] = w_ref[...].astype(f32).T
        bf[...] = column(b_ref[...])
        host = lax.axis_index(("chan", "quarter"))
        for half in range(2):
            for b in range(0, len(outs), 2):
                source = [
                    pl.ds(pl.multiple_of(half * hidden + (host ^ (b + n)) * BLOCK, BLOCK), BLOCK)
                    for n in range(2)
                ]
                target = slice(half * hidden + b * BLOCK, half * hidden + (b + 2) * BLOCK)
                wt[target] = jnp.concatenate([wf[s] for s in source], axis=0).astype(bf16)
                bt[target] = jnp.concatenate([bf[s] for s in source], axis=0)

    x = pair_ref[...].astype(f32).reshape(STEP * k, width)
    normed = normalize(x, gain_ref[...], shift_ref[...])
    gate = sigmoid(dot(normed, gw_ref[...]) + gb_ref[...])
    gate_ref[...] = gate.reshape(STEP, k, width).astype(bf16)
    rows = as_rows(factor(normed, wt[...], bt[...]), k).astype(bf16)
    for b, out in enumerate(outs):
        out[...] = rows[b]


def regroup(pieces, target, matrix):
    many = SIZE // STEP
    for s in range(len(pieces) // many):
        rows = jnp.concatenate([piece() for piece in pieces[s * many : (s + 1) * many]], axis=0)
        moved = dot(matrix, rows).astype(bf16)
        for c in range(BLOCK):
            target[c, s * SIZE : (s + 1) * SIZE, :] = moved[c * SIZE : (c + 1) * SIZE]


def slices(refs):
    tall = STEP * BLOCK
    return [
        functools.partial(lambda ref, at: ref[at : at + tall, :], ref, at)
        for ref in refs
        for at in range(0, ref.shape[0], tall)
    ]


def multiply(left, right_ref, right, held, store):
    regroup(slices([right_ref]), right, shuffle(BLOCK, SIZE))
    back = shuffle(SIZE, BLOCK)
    for c in range(BLOCK):
        held[c] = dot_nt(left[c], right[c]).astype(bf16)
    for s in range(left.shape[1] // SIZE):
        parts = jnp.concatenate([held[c, s * SIZE : (s + 1) * SIZE, :] for c in range(BLOCK)], axis=0)
        moved = dot(back, parts).astype(bf16)
        for i in range(0, SIZE, STEP):
            store(s * SIZE + i, moved[i * BLOCK : (i + STEP) * BLOCK])


def gather_kernel(*refs):
    regroup(slices(refs[:-1]), refs[-1], shuffle(BLOCK, SIZE))


def sending_order(hosts):
    far, near = list(range(hosts // 2, hosts)), list(range(1, hosts // 2))
    order = [0]
    while far:
        order += far[:2] + near[:1]
        far, near = far[2:], near[1:]
    return order + near


def product_kernel(right_ref, left, *refs):
    outs = refs[:-2]
    right, held = refs[-2:]
    rows = left.shape[1] // len(outs)

    def store(i, values):
        to, at = divmod(i, rows)
        outs[to][at * BLOCK : (at + STEP) * BLOCK, :] = values

    multiply(left, right_ref, right, held, store)


def final_kernel(hosts, *refs):
    products = refs[:hosts]
    gate_ref, g_ref, s_ref, w_ref, b_ref, out_ref, made, plain, mixed, leave = refs[hosts:]
    j = products[0].shape[1]
    rows, _, width = gate_ref.shape
    plain[0] = column(g_ref[...])
    plain[1] = column(s_ref[...])
    plain[2] = w_ref[...].astype(f32)
    host = lax.axis_index(("chan", "quarter"))
    for m, b in enumerate(sending_order(hosts)):
        source = pl.ds(pl.multiple_of((host ^ b) * BLOCK, BLOCK), BLOCK)
        for n in range(3):
            mixed[n, m * BLOCK : (m + 1) * BLOCK] = plain[n, source]
    gain, shift = widen(mixed[0], j), widen(mixed[1], j)
    weight = mixed[2].astype(bf16)
    stores = []
    for r in range(0, rows, 2):
        pair = [ref[r * BLOCK : (r + 2) * BLOCK, :].astype(f32) for ref in products]
        for n in range(2):
            x = jnp.concatenate([one[n * BLOCK : (n + 1) * BLOCK] for one in pair], axis=0)
            centered = x - jnp.mean(x, axis=0, keepdims=True)
            variance = jnp.mean(centered * centered, axis=0, keepdims=True)
            normed = centered * lax.rsqrt(variance + epsilon) * gain + shift
            outward = dot(normed.astype(bf16).T, weight) + b_ref[...]
            made[r + n] = (gate_ref[r + n].astype(f32) * outward).astype(bf16)
        at = pl.ds(r, 2)
        stores.append(pltpu.make_async_copy(made.at[at], out_ref.at[at], leave.at[r // 2]))
        stores[-1].start()
    for store in stores:
        store.wait()


def whole(shape):
    return pl.BlockSpec(shape, lambda s: (0,) * len(shape))


def cost(flops, size):
    return pl.CostEstimate(flops=flops, bytes_accessed=size, transcendentals=0)


def params(mib=32):
    return pltpu.CompilerParams(vmem_limit_bytes=mib * MIB)


def shards(parts, pair, norm_gain, norm_shift, factor_weight, factor_bias, gate_weight, gate_bias,
           center_gain, center_shift, out_weight, out_bias):
    rows, k, width = pair.shape
    hidden = out_weight.shape[0]
    hosts = hidden // BLOCK
    steps = rows // STEP
    tall = rows * BLOCK
    mine = hosts * rows
    devices = parts * hosts
    in_part = ("chan", "quarter")
    everywhere = ("part",) + in_part
    row = lambda v: v.reshape(1, -1)
    row_block = pl.BlockSpec((STEP, k, width), lambda s: (s, 0, 0))
    work = rows * k * width
    bfloat = lambda *shape: jax.ShapeDtypeStruct(shape, bf16)

    vmem = pl.BlockSpec(memory_space=pltpu.VMEM)
    anywhere = pl.BlockSpec(memory_space=pl.ANY)
    turns = len(turns_of(rows))
    right = pl.pallas_call(
        right_kernel,
        in_specs=[anywhere] * 5,
        out_specs=anywhere,
        out_shape=bfloat(parts, hosts, tall, k),
        scratch_shapes=[
            pltpu.VMEM((rows, k, width), bf16),
            pltpu.VMEM((1, width), f32),
            pltpu.VMEM((1, width), f32),
            pltpu.VMEM((width, 2 * hidden), bf16),
            pltpu.VMEM((1, 2 * hidden), f32),
            pltpu.VMEM((hosts, tall, k), bf16),
            pltpu.SemaphoreType.DMA((turns,)),
            pltpu.SemaphoreType.DMA((parts, turns)),
            pltpu.SemaphoreType.DMA((4,)),
        ],
        compiler_params=params(60),
        cost_estimate=cost(4 * work * hidden, 6 * work),
        name="right_factor",
    )(pair, row(norm_gain), row(norm_shift), factor_weight, row(factor_bias))
    right = lax.all_to_all(right.reshape(devices, tall, k), everywhere, 0, 0, tiled=True)

    def send(values, b):
        pairs = [(p * hosts + h, p * hosts + (h ^ b)) for p in range(parts) for h in range(hosts)]
        return lax.ppermute(values, everywhere, pairs)

    *lefts, gate = pl.pallas_call(
        left_kernel,
        grid=(steps,),
        in_specs=[
            row_block,
            whole((1, width)),
            whole((1, width)),
            whole((width, 2 * hidden)),
            whole((1, 2 * hidden)),
            whole((width, width)),
            whole((1, width)),
        ],
        out_specs=[pl.BlockSpec((STEP * BLOCK, k), lambda s: (s, 0))] * hosts + [row_block],
        out_shape=[bfloat(tall, k)] * hosts + [bfloat(*pair.shape)],
        scratch_shapes=[
            pltpu.VMEM((2 * hidden, width), f32),
            pltpu.VMEM((2 * hidden, LANES), f32),
            pltpu.VMEM((2 * hidden, width), bf16),
            pltpu.VMEM((2 * hidden, LANES), f32),
        ],
        compiler_params=params(),
        cost_estimate=cost(4 * work * hidden, 6 * work),
        name="left_factor",
    )(
        pair,
        row(norm_gain),
        row(norm_shift),
        factor_weight,
        row(factor_bias),
        gate_weight,
        row(gate_bias),
    )
    lefts = [lefts[0]] + [send(lefts[b], b) for b in reversed(range(1, hosts))][::-1]

    left = pl.pallas_call(
        gather_kernel,
        in_specs=[vmem] * hosts,
        out_specs=vmem,
        out_shape=bfloat(BLOCK, mine, k),
        compiler_params=params(),
        cost_estimate=cost(2 * work * BLOCK * SIZE, 4 * work),
        name="gather_left",
    )(*lefts)

    span = GATHER * rows
    gathers = devices // GATHER
    if gathers == 1:
        blocks = dict(in_specs=[vmem] * 2, out_specs=[vmem] * hosts)
    else:
        blocks = dict(
            grid=(gathers,),
            in_specs=[pl.BlockSpec((span * BLOCK, k), lambda s: (s, 0)), whole((BLOCK, mine, k))],
            out_specs=[pl.BlockSpec((tall, span), lambda s: (0, s))] * hosts,
        )
    products = pl.pallas_call(
        product_kernel,
        **blocks,
        out_shape=[bfloat(tall, devices * rows)] * hosts,
        scratch_shapes=[pltpu.VMEM((BLOCK, span, k), bf16), pltpu.VMEM((BLOCK, mine, span), bf16)],
        compiler_params=params(40),
        cost_estimate=cost(2 * BLOCK * mine * mine * k, 6 * BLOCK * mine * k),
        name="products",
    )(right.reshape(devices * tall, k), left)
    products = [send(products[b], b) if b else products[b] for b in sending_order(hosts)]

    return pl.pallas_call(
        functools.partial(final_kernel, hosts),
        in_specs=[vmem] * (hosts + 5),
        out_specs=anywhere,
        out_shape=bfloat(*pair.shape),
        scratch_shapes=[
            pltpu.VMEM(pair.shape, bf16),
            pltpu.VMEM((3, hidden, LANES), f32),
            pltpu.VMEM((3, hidden, LANES), f32),
            pltpu.SemaphoreType.DMA((rows // 2,)),
        ],
        compiler_params=params(),
        cost_estimate=cost(2 * work * width, 6 * work),
        name="update",
    )(*products, gate, row(center_gain), row(center_shift), out_weight, row(out_bias))


def solution(mesh):
    groups, chan, quarter = (mesh.shape[a] for a in ("groups", "chan", "quarter"))
    near = CHANNELS // BLOCK // quarter
    parts = chan // near
    split = Mesh(
        mesh.devices.reshape(groups, parts, near, quarter), ("groups", "part", "chan", "quarter")
    )
    rows = P(("groups", "part", "chan", "quarter"), None, None)
    return jax.shard_map(
        functools.partial(shards, parts),
        mesh=split,
        in_specs=(rows,) + (P(),) * 10,
        out_specs=rows,
        check_vma=False,
    )
```

```python
import functools

import jax
import jax.numpy as jnp
from jax import lax
from jax.experimental import pallas as pl
from jax.experimental.pallas import tpu as pltpu
from jax.sharding import Mesh
from jax.sharding import PartitionSpec as P

epsilon = 1e-05
CHANNELS = 128
BLOCK = 8
STEP = 4
SIZE = 32
LANES = 128
GATHER = 32
MIB = 1024 * 1024

f32, bf16 = jnp.float32, jnp.bfloat16


def sigmoid(x):
    return 0.5 * jnp.tanh(0.5 * x) + 0.5


def dot(a, b):
    return jnp.dot(a, b, preferred_element_type=f32)


def dot_nt(a, b):
    return lax.dot_general(a, b, (((1,), (1,)), ((), ())), preferred_element_type=f32)


def column(row):
    blocks = [
        jnp.broadcast_to(row[:, k : k + LANES], (LANES, LANES)).T
        for k in range(0, row.shape[1], LANES)
    ]
    return jnp.concatenate(blocks, axis=0)


def widen(col, width):
    return jnp.concatenate([col] * (width // LANES), axis=1)


def shuffle(groups, size):
    n = groups * size
    out = lax.broadcasted_iota(jnp.int32, (n, n), 0)
    row = lax.broadcasted_iota(jnp.int32, (n, n), 1)
    want = (out % size) * groups + out // size
    return jnp.where(want == row, 1.0, 0.0).astype(bf16)


def normalize(x, gain, shift):
    centered = x - jnp.mean(x, axis=1, keepdims=True)
    variance = jnp.mean(centered * centered, axis=1, keepdims=True)
    return (centered * lax.rsqrt(variance + epsilon) * gain + shift).astype(bf16)


def factor(normed, wt, bias):
    width = wt.shape[0] // 2
    both = dot_nt(wt, normed) + widen(bias, normed.shape[0])
    return sigmoid(both[:width]) * both[width:]


def as_rows(values, k, step=STEP):
    hosts = values.shape[0] // BLOCK
    return jnp.concatenate(
        [values[:, r * k : (r + 1) * k].reshape(hosts, BLOCK, k) for r in range(step)], axis=1
    )


def right_kernel(pair_ref, gain_ref, shift_ref, w_ref, b_ref, out_ref, wt, bt):
    @pl.when(pl.program_id(0) == 0)
    def _():
        wt[...] = w_ref[...].astype(f32).T.astype(bf16)
        bt[...] = column(b_ref[...])

    k, width = pair_ref.shape[1:]
    x = pair_ref[...].astype(f32).reshape(STEP * k, width)
    normed = normalize(x, gain_ref[...], shift_ref[...])
    out = as_rows(factor(normed, wt[...], bt[...]), k).astype(bf16)
    for p in range(out_ref.shape[0]):
        out_ref[p] = out


def left_kernel(pair_ref, gain_ref, shift_ref, w_ref, b_ref, gw_ref, gb_ref, *refs):
    wf, bf, wt, bt = refs[-4:]
    gate_ref = refs[-5]
    outs = refs[:-5]
    k, width = pair_ref.shape[1:]
    hidden = w_ref.shape[1] // 2

    @pl.when(pl.program_id(0) == 0)
    def _():
        wf[...] = w_ref[...].astype(f32).T
        bf[...] = column(b_ref[...])
        host = lax.axis_index(("side", "chan", "quarter"))
        for half in range(2):
            for b in range(0, len(outs), 2):
                source = [
                    pl.ds(pl.multiple_of(half * hidden + (host ^ (b + n)) * BLOCK, BLOCK), BLOCK)
                    for n in range(2)
                ]
                target = slice(half * hidden + b * BLOCK, half * hidden + (b + 2) * BLOCK)
                wt[target] = jnp.concatenate([wf[s] for s in source], axis=0).astype(bf16)
                bt[target] = jnp.concatenate([bf[s] for s in source], axis=0)

    x = pair_ref[...].astype(f32).reshape(STEP * k, width)
    normed = normalize(x, gain_ref[...], shift_ref[...])
    gate = sigmoid(dot(normed, gw_ref[...]) + gb_ref[...])
    gate_ref[...] = gate.reshape(STEP, k, width).astype(bf16)
    rows = as_rows(factor(normed, wt[...], bt[...]), k).astype(bf16)
    for b, out in enumerate(outs):
        out[...] = rows[b]


def regroup(pieces, target, matrix):
    many = SIZE // STEP
    for s in range(len(pieces) // many):
        rows = jnp.concatenate([piece() for piece in pieces[s * many : (s + 1) * many]], axis=0)
        moved = dot(matrix, rows).astype(bf16)
        for c in range(BLOCK):
            target[c, s * SIZE : (s + 1) * SIZE, :] = moved[c * SIZE : (c + 1) * SIZE]


def slices(refs):
    tall = STEP * BLOCK
    return [
        functools.partial(lambda ref, at: ref[at : at + tall, :], ref, at)
        for ref in refs
        for at in range(0, ref.shape[0], tall)
    ]


def multiply(left, right, held, store):
    back = shuffle(SIZE, BLOCK)
    for c in range(BLOCK):
        held[c] = dot_nt(left[c], right[c]).astype(bf16)
    for s in range(left.shape[1] // SIZE):
        parts = jnp.concatenate([held[c, s * SIZE : (s + 1) * SIZE, :] for c in range(BLOCK)], axis=0)
        moved = dot(back, parts).astype(bf16)
        for i in range(0, SIZE, STEP):
            store(s * SIZE + i, moved[i * BLOCK : (i + STEP) * BLOCK])


def gather_kernel(*refs):
    regroup(slices(refs[:-1]), refs[-1], shuffle(BLOCK, SIZE))


def far_kernel(right_ref, left_ref, *refs):
    outs, (right, held) = refs[:-2], refs[-2:]
    count = left_ref.shape[1] // 2
    rows = count // len(outs)
    regroup(slices([right_ref]), right, shuffle(BLOCK, SIZE))

    def store(i, values):
        to, at = divmod(i, rows)
        outs[to][at * BLOCK : (at + STEP) * BLOCK, :] = values

    multiply(left_ref.at[:, count:], right, held, store)


def near_kernel(left_ref, right_ref, out_ref, held):
    near = out_ref.shape[0]
    count = left_ref.shape[1] // 2
    rows = count // near
    host = lax.axis_index(("chan", "quarter"))

    def store(i, values):
        to, at = divmod(i, rows)
        out_ref[host ^ to, at * BLOCK : (at + STEP) * BLOCK, :] = values

    multiply(left_ref.at[:, :count], right_ref, held, store)


def prepare_kernel(near, g_ref, s_ref, w_ref, columns_ref, weight_ref, plain, mixed):
    plain[0] = column(g_ref[...])
    plain[1] = column(s_ref[...])
    plain[2] = w_ref[...].astype(f32)
    host = lax.axis_index(("side", "chan", "quarter"))
    order = [host // near * near + n for n in range(near)]
    order += [host ^ (near + n) for n in range(near)]
    for m, one in enumerate(order):
        source = pl.ds(pl.multiple_of(one * BLOCK, BLOCK), BLOCK)
        for n in range(3):
            mixed[n, m * BLOCK : (m + 1) * BLOCK] = plain[n, source]
    columns_ref[...] = mixed[:2]
    weight_ref[...] = mixed[2].astype(bf16)


def final_kernel(near_ref, *refs):
    near, _, j = near_ref.shape
    fars = refs[:near]
    gate_ref, columns_ref, w_ref, b_ref, out_ref, made, leave = refs[near:]
    rows, _, width = gate_ref.shape
    gain, shift = widen(columns_ref[0], j), widen(columns_ref[1], j)
    stores = []
    for r in range(0, rows, 2):
        pair = [near_ref[h, r * BLOCK : (r + 2) * BLOCK, :].astype(f32) for h in range(near)]
        pair += [ref[r * BLOCK : (r + 2) * BLOCK, :].astype(f32) for ref in fars]
        for n in range(2):
            x = jnp.concatenate([one[n * BLOCK : (n + 1) * BLOCK] for one in pair], axis=0)
            centered = x - jnp.mean(x, axis=0, keepdims=True)
            variance = jnp.mean(centered * centered, axis=0, keepdims=True)
            normed = centered * lax.rsqrt(variance + epsilon) * gain + shift
            outward = dot(normed.astype(bf16).T, w_ref[...]) + b_ref[...]
            made[r + n] = (gate_ref[r + n].astype(f32) * outward).astype(bf16)
        at = pl.ds(r, 2)
        stores.append(pltpu.make_async_copy(made.at[at], out_ref.at[at], leave.at[r // 2]))
        stores[-1].start()
    for store in stores:
        store.wait()


def whole(shape):
    return pl.BlockSpec(shape, lambda s: (0,) * len(shape))


def cost(flops, size):
    return pl.CostEstimate(flops=flops, bytes_accessed=size, transcendentals=0)


def params(mib=32):
    return pltpu.CompilerParams(vmem_limit_bytes=mib * MIB)


def shards(parts, pair, norm_gain, norm_shift, factor_weight, factor_bias, gate_weight, gate_bias,
           center_gain, center_shift, out_weight, out_bias):
    rows, k, width = pair.shape
    hidden = out_weight.shape[0]
    hosts = hidden // BLOCK
    steps = rows // STEP
    tall = rows * BLOCK
    mine = hosts * rows
    devices = parts * hosts
    in_part = ("side", "chan", "quarter")
    everywhere = ("part",) + in_part
    row = lambda v: v.reshape(1, -1)
    row_block = pl.BlockSpec((STEP, k, width), lambda s: (s, 0, 0))
    work = rows * k * width
    bfloat = lambda *shape: jax.ShapeDtypeStruct(shape, bf16)

    vmem = pl.BlockSpec(memory_space=pltpu.VMEM)
    anywhere = pl.BlockSpec(memory_space=pl.ANY)
    right = pl.pallas_call(
        right_kernel,
        grid=(steps,),
        in_specs=[
            row_block,
            whole((1, width)),
            whole((1, width)),
            pl.BlockSpec((width, 2 * hidden), lambda s: (0, 1)),
            pl.BlockSpec((1, 2 * hidden), lambda s: (0, 1)),
        ],
        out_specs=pl.BlockSpec((parts, hosts, STEP * BLOCK, k), lambda s: (0, 0, s, 0)),
        out_shape=bfloat(parts, hosts, tall, k),
        scratch_shapes=[pltpu.VMEM((2 * hidden, width), bf16), pltpu.VMEM((2 * hidden, LANES), f32)],
        compiler_params=params(60),
        cost_estimate=cost(4 * work * hidden, 6 * work),
        name="right_factor",
    )(pair, row(norm_gain), row(norm_shift), factor_weight, row(factor_bias))
    right = lax.all_to_all(right.reshape(devices, tall, k), everywhere, 0, 0, tiled=True)

    def send(values, b):
        pairs = [(p * hosts + h, p * hosts + (h ^ b)) for p in range(parts) for h in range(hosts)]
        return lax.ppermute(values, everywhere, pairs)

    *lefts, gate = pl.pallas_call(
        left_kernel,
        grid=(steps,),
        in_specs=[
            row_block,
            whole((1, width)),
            whole((1, width)),
            whole((width, 2 * hidden)),
            whole((1, 2 * hidden)),
            whole((width, width)),
            whole((1, width)),
        ],
        out_specs=[pl.BlockSpec((STEP * BLOCK, k), lambda s: (s, 0))] * hosts + [row_block],
        out_shape=[bfloat(tall, k)] * hosts + [bfloat(*pair.shape)],
        scratch_shapes=[
            pltpu.VMEM((2 * hidden, width), f32),
            pltpu.VMEM((2 * hidden, LANES), f32),
            pltpu.VMEM((2 * hidden, width), bf16),
            pltpu.VMEM((2 * hidden, LANES), f32),
        ],
        compiler_params=params(),
        cost_estimate=cost(4 * work * hidden, 6 * work),
        name="left_factor",
    )(
        pair,
        row(norm_gain),
        row(norm_shift),
        factor_weight,
        row(factor_bias),
        gate_weight,
        row(gate_bias),
    )
    lefts = [lefts[0]] + [send(lefts[b], b) for b in reversed(range(1, hosts))][::-1]

    left = pl.pallas_call(
        gather_kernel,
        in_specs=[vmem] * hosts,
        out_specs=vmem,
        out_shape=bfloat(BLOCK, mine, k),
        compiler_params=params(),
        cost_estimate=cost(2 * work * BLOCK * SIZE, 4 * work),
        name="gather_left",
    )(*lefts)

    near = hosts // 2
    span = GATHER * rows
    gathers = devices // GATHER
    if gathers == 1:
        blocks = dict(in_specs=[vmem] * 2, out_specs=[vmem] * (near + 1))
        rest = dict(in_specs=[vmem] * 2, out_specs=vmem)
    else:
        grouped = pl.BlockSpec((BLOCK, span, k), lambda s: (0, s, 0))
        blocks = dict(
            grid=(gathers,),
            in_specs=[pl.BlockSpec((span * BLOCK, k), lambda s: (s, 0)), whole((BLOCK, mine, k))],
            out_specs=[pl.BlockSpec((tall, span), lambda s: (0, s))] * near + [grouped],
        )
        rest = dict(
            grid=(gathers,),
            in_specs=[whole((BLOCK, mine, k)), grouped],
            out_specs=pl.BlockSpec((near, tall, span), lambda s: (0, 0, s)),
        )
    spent = BLOCK * mine * mine * k
    *fars, right = pl.pallas_call(
        far_kernel,
        **blocks,
        out_shape=[pltpu.HBM((tall, devices * rows), bf16)] * near + [bfloat(BLOCK, devices * rows, k)],
        scratch_shapes=[pltpu.VMEM((BLOCK, mine // 2, span), bf16)],
        compiler_params=params(40),
        cost_estimate=cost(spent, 6 * BLOCK * mine * k),
        name="far_products",
    )(right.reshape(devices * tall, k), left)
    fars = [send(values, near + b) for b, values in enumerate(fars)]
    nears = pl.pallas_call(
        near_kernel,
        **rest,
        out_shape=bfloat(near, tall, devices * rows),
        scratch_shapes=[pltpu.VMEM((BLOCK, mine // 2, span), bf16)],
        compiler_params=params(),
        cost_estimate=cost(spent, 6 * BLOCK * mine * k),
        name="near_products",
    )(left, right)
    nears = lax.all_to_all(nears, ("chan", "quarter"), 0, 0, tiled=True)

    columns, weight = pl.pallas_call(
        functools.partial(prepare_kernel, near),
        in_specs=[vmem] * 3,
        out_specs=[vmem] * 2,
        out_shape=[jax.ShapeDtypeStruct((2, hidden, LANES), f32), bfloat(hidden, width)],
        scratch_shapes=[pltpu.VMEM((3, hidden, LANES), f32)] * 2,
        compiler_params=params(),
        cost_estimate=cost(1 << 37, 4 * hidden * width),
        name="prepare",
    )(row(center_gain), row(center_shift), out_weight)

    return pl.pallas_call(
        final_kernel,
        in_specs=[vmem] * (near + 5),
        out_specs=anywhere,
        out_shape=bfloat(*pair.shape),
        scratch_shapes=[
            pltpu.VMEM(pair.shape, bf16),
            pltpu.SemaphoreType.DMA((rows // 2,)),
        ],
        compiler_params=params(),
        cost_estimate=cost(2 * work * width, 6 * work),
        name="update",
    )(nears, *fars, gate, columns, weight, row(out_bias))


def solution(mesh):
    groups, chan, quarter = (mesh.shape[a] for a in ("groups", "chan", "quarter"))
    near = CHANNELS // BLOCK // quarter
    parts = chan // near
    split = Mesh(
        mesh.devices.reshape(groups, parts, 2, near // 2, quarter),
        ("groups", "part", "side", "chan", "quarter"),
    )
    rows = P(("groups", "part", "side", "chan", "quarter"), None, None)
    return jax.shard_map(
        functools.partial(shards, parts),
        mesh=split,
        in_specs=(rows,) + (P(),) * 10,
        out_specs=rows,
        check_vma=False,
    )
```

```python
import functools

import jax
import jax.numpy as jnp
from jax import lax
from jax.experimental import pallas as pl
from jax.experimental.pallas import tpu as pltpu
from jax.sharding import Mesh
from jax.sharding import PartitionSpec as P

epsilon = 1e-05
CHANNELS = 128
BLOCK = 8
STEP = 4
SIZE = 32
LANES = 128
GATHER = 32
MIB = 1024 * 1024

f32, bf16 = jnp.float32, jnp.bfloat16


def sigmoid(x):
    return 0.5 * jnp.tanh(0.5 * x) + 0.5


def dot(a, b):
    return jnp.dot(a, b, preferred_element_type=f32)


def dot_nt(a, b):
    return lax.dot_general(a, b, (((1,), (1,)), ((), ())), preferred_element_type=f32)


def column(row):
    blocks = [
        jnp.broadcast_to(row[:, k : k + LANES], (LANES, LANES)).T
        for k in range(0, row.shape[1], LANES)
    ]
    return jnp.concatenate(blocks, axis=0)


def widen(col, width):
    return jnp.concatenate([col] * (width // LANES), axis=1)


def shuffle(groups, size):
    n = groups * size
    out = lax.broadcasted_iota(jnp.int32, (n, n), 0)
    row = lax.broadcasted_iota(jnp.int32, (n, n), 1)
    want = (out % size) * groups + out // size
    return jnp.where(want == row, 1.0, 0.0).astype(bf16)


def normalize(x, gain, shift):
    centered = x - jnp.mean(x, axis=1, keepdims=True)
    variance = jnp.mean(centered * centered, axis=1, keepdims=True)
    return (centered * lax.rsqrt(variance + epsilon) * gain + shift).astype(bf16)


def factor(normed, wt, bias):
    width = wt.shape[0] // 2
    both = dot_nt(wt, normed) + widen(bias, normed.shape[0])
    return sigmoid(both[:width]) * both[width:]


def as_rows(values, k):
    hosts = values.shape[0] // BLOCK
    return jnp.concatenate(
        [values[:, r * k : (r + 1) * k].reshape(hosts, BLOCK, k) for r in range(STEP)], axis=1
    )


def right_kernel(pair_ref, gain_ref, shift_ref, w_ref, b_ref, out_ref, wt, bt):
    @pl.when(pl.program_id(0) == 0)
    def _():
        wt[...] = w_ref[...].astype(f32).T.astype(bf16)
        bt[...] = column(b_ref[...])

    k, width = pair_ref.shape[1:]
    x = pair_ref[...].astype(f32).reshape(STEP * k, width)
    normed = normalize(x, gain_ref[...], shift_ref[...])
    out = as_rows(factor(normed, wt[...], bt[...]), k).astype(bf16)
    for p in range(out_ref.shape[0]):
        out_ref[p] = out


def left_kernel(pair_ref, gain_ref, shift_ref, w_ref, b_ref, gw_ref, gb_ref, *refs):
    wf, bf, wt, bt = refs[-4:]
    gate_ref = refs[-5]
    outs = refs[:-5]
    k, width = pair_ref.shape[1:]
    hidden = w_ref.shape[1] // 2

    @pl.when(pl.program_id(0) == 0)
    def _():
        wf[...] = w_ref[...].astype(f32).T
        bf[...] = column(b_ref[...])
        host = lax.axis_index(("chan", "quarter"))
        for half in range(2):
            for b in range(0, len(outs), 2):
                source = [
                    pl.ds(pl.multiple_of(half * hidden + (host ^ (b + n)) * BLOCK, BLOCK), BLOCK)
                    for n in range(2)
                ]
                target = slice(half * hidden + b * BLOCK, half * hidden + (b + 2) * BLOCK)
                wt[target] = jnp.concatenate([wf[s] for s in source], axis=0).astype(bf16)
                bt[target] = jnp.concatenate([bf[s] for s in source], axis=0)

    x = pair_ref[...].astype(f32).reshape(STEP * k, width)
    normed = normalize(x, gain_ref[...], shift_ref[...])
    gate = sigmoid(dot(normed, gw_ref[...]) + gb_ref[...])
    gate_ref[...] = gate.reshape(STEP, k, width).astype(bf16)
    rows = as_rows(factor(normed, wt[...], bt[...]), k).astype(bf16)
    for b, out in enumerate(outs):
        out[...] = rows[b]


def regroup(pieces, target, matrix):
    many = SIZE // STEP
    for s in range(len(pieces) // many):
        rows = jnp.concatenate([piece() for piece in pieces[s * many : (s + 1) * many]], axis=0)
        moved = dot(matrix, rows).astype(bf16)
        for c in range(BLOCK):
            target[c, s * SIZE : (s + 1) * SIZE, :] = moved[c * SIZE : (c + 1) * SIZE]


def slices(refs):
    tall = STEP * BLOCK
    return [
        functools.partial(lambda ref, at: ref[at : at + tall, :], ref, at)
        for ref in refs
        for at in range(0, ref.shape[0], tall)
    ]


def regroup_right_kernel(rows_ref, out_ref):
    regroup(slices([rows_ref]), out_ref, shuffle(BLOCK, SIZE))


def regroup_left_kernel(*refs):
    regroup(slices(refs[:-1]), refs[-1], shuffle(BLOCK, SIZE))


def product_kernel(right, near, *refs):
    lefts = refs[:-3]
    out_ref, far, held = refs[-3:]
    rows = lefts[0].shape[0] // BLOCK
    host = lax.axis_index(("chan", "quarter"))
    regroup(slices(lefts), far, shuffle(BLOCK, SIZE))
    for c in range(BLOCK):
        left = jnp.concatenate([near[c], far[c]], axis=0)
        held[c] = dot_nt(left, right[c]).astype(bf16)
    back = shuffle(SIZE, BLOCK)
    for s in range(held.shape[1] // SIZE):
        parts = jnp.concatenate([held[c, s * SIZE : (s + 1) * SIZE, :] for c in range(BLOCK)], axis=0)
        moved = dot(back, parts).astype(bf16)
        for i in range(0, SIZE, STEP):
            to, at = divmod(s * SIZE + i, rows)
            out_ref[host ^ to, at * BLOCK : (at + STEP) * BLOCK, :] = moved[
                i * BLOCK : (i + STEP) * BLOCK
            ]


def final_kernel(x_ref, gate_ref, g_ref, s_ref, w_ref, b_ref, out_ref, made, leave):
    hosts, _, j = x_ref.shape
    rows = gate_ref.shape[0]
    width = hosts * BLOCK
    gain, shift = widen(column(g_ref[...]), j), widen(column(s_ref[...]), j)
    stores = []
    for r in range(0, rows, 2):
        pair = x_ref[:, r * BLOCK : (r + 2) * BLOCK].astype(f32)
        for n in range(2):
            x = pair[:, n * BLOCK : (n + 1) * BLOCK].reshape(width, j)
            centered = x - jnp.mean(x, axis=0, keepdims=True)
            variance = jnp.mean(centered * centered, axis=0, keepdims=True)
            normed = centered * lax.rsqrt(variance + epsilon) * gain + shift
            outward = dot(normed.astype(bf16).T, w_ref[...]) + b_ref[...]
            made[r + n] = (gate_ref[r + n].astype(f32) * outward).astype(bf16)
        at = pl.ds(r, 2)
        stores.append(pltpu.make_async_copy(made.at[at], out_ref.at[at], leave.at[r // 2]))
        stores[-1].start()
    for store in stores:
        store.wait()


def whole(shape):
    return pl.BlockSpec(shape, lambda s: (0,) * len(shape))


def cost(flops, size):
    return pl.CostEstimate(flops=flops, bytes_accessed=size, transcendentals=0)


def params(mib=32):
    return pltpu.CompilerParams(vmem_limit_bytes=mib * MIB)


def shards(parts, pair, norm_gain, norm_shift, factor_weight, factor_bias, gate_weight, gate_bias,
           center_gain, center_shift, out_weight, out_bias):
    rows, k, width = pair.shape
    hidden = out_weight.shape[0]
    hosts = hidden // BLOCK
    steps = rows // STEP
    tall = rows * BLOCK
    mine = hosts * rows
    devices = parts * hosts
    in_part = ("chan", "quarter")
    everywhere = ("part",) + in_part
    row = lambda v: v.reshape(1, -1)
    row_block = pl.BlockSpec((STEP, k, width), lambda s: (s, 0, 0))
    work = rows * k * width
    bfloat = lambda *shape: jax.ShapeDtypeStruct(shape, bf16)

    vmem = pl.BlockSpec(memory_space=pltpu.VMEM)
    anywhere = pl.BlockSpec(memory_space=pl.ANY)
    right = pl.pallas_call(
        right_kernel,
        grid=(steps,),
        in_specs=[
            row_block,
            whole((1, width)),
            whole((1, width)),
            pl.BlockSpec((width, 2 * hidden), lambda s: (0, 1)),
            pl.BlockSpec((1, 2 * hidden), lambda s: (0, 1)),
        ],
        out_specs=pl.BlockSpec((parts, hosts, STEP * BLOCK, k), lambda s: (0, 0, s, 0)),
        out_shape=bfloat(parts, hosts, tall, k),
        scratch_shapes=[pltpu.VMEM((2 * hidden, width), bf16), pltpu.VMEM((2 * hidden, LANES), f32)],
        compiler_params=params(60),
        cost_estimate=cost(4 * work * hidden, 6 * work),
        name="right_factor",
    )(pair, row(norm_gain), row(norm_shift), factor_weight, row(factor_bias))
    right = lax.all_to_all(right.reshape(devices, tall, k), everywhere, 0, 0, tiled=True)

    def send(values, b):
        pairs = [(p * hosts + h, p * hosts + (h ^ b)) for p in range(parts) for h in range(hosts)]
        return lax.ppermute(values, everywhere, pairs)

    *lefts, gate = pl.pallas_call(
        left_kernel,
        grid=(steps,),
        in_specs=[
            row_block,
            whole((1, width)),
            whole((1, width)),
            whole((width, 2 * hidden)),
            whole((1, 2 * hidden)),
            whole((width, width)),
            whole((1, width)),
        ],
        out_specs=[pl.BlockSpec((STEP * BLOCK, k), lambda s: (s, 0))] * hosts + [row_block],
        out_shape=[bfloat(tall, k)] * hosts + [bfloat(*pair.shape)],
        scratch_shapes=[
            pltpu.VMEM((2 * hidden, width), f32),
            pltpu.VMEM((2 * hidden, LANES), f32),
            pltpu.VMEM((2 * hidden, width), bf16),
            pltpu.VMEM((2 * hidden, LANES), f32),
        ],
        compiler_params=params(),
        cost_estimate=cost(4 * work * hidden, 6 * work),
        name="left_factor",
    )(
        pair,
        row(norm_gain),
        row(norm_shift),
        factor_weight,
        row(factor_bias),
        gate_weight,
        row(gate_bias),
    )
    lefts = [lefts[0]] + [send(lefts[b], b) for b in reversed(range(1, hosts))][::-1]

    half = hosts // 2
    near = pl.pallas_call(
        regroup_left_kernel,
        in_specs=[vmem] * half,
        out_specs=vmem,
        out_shape=bfloat(BLOCK, mine // 2, k),
        compiler_params=params(),
        cost_estimate=cost(work * BLOCK * SIZE, 2 * work),
        name="regroup_left",
    )(*lefts[:half])

    span = GATHER * rows
    gathers = devices // GATHER
    grouped = pl.BlockSpec((BLOCK, span, k), lambda s: (0, s, 0))
    if gathers == 1:
        limit = params()
        blocks = dict(in_specs=[vmem], out_specs=vmem)
        rest = dict(in_specs=[vmem] * (2 + half), out_specs=vmem)
    else:
        limit = params(60)
        blocks = dict(
            grid=(gathers,),
            in_specs=[pl.BlockSpec((span * BLOCK, k), lambda s: (s, 0))],
            out_specs=grouped,
        )
        rest = dict(
            grid=(gathers,),
            in_specs=[grouped, whole((BLOCK, mine // 2, k))] + [whole((tall, k))] * half,
            out_specs=pl.BlockSpec((hosts, tall, span), lambda s: (0, 0, s)),
        )
    right = pl.pallas_call(
        regroup_right_kernel,
        **blocks,
        out_shape=bfloat(BLOCK, devices * rows, k),
        compiler_params=limit,
        cost_estimate=cost(1 << 37, 4 * devices * tall * k),
        name="regroup_right",
    )(right.reshape(devices * tall, k))
    product = pl.pallas_call(
        product_kernel,
        **rest,
        out_shape=bfloat(hosts, tall, devices * rows),
        scratch_shapes=[
            pltpu.VMEM((BLOCK, mine // 2, k), bf16),
            pltpu.VMEM((BLOCK, mine, span), bf16),
        ],
        compiler_params=limit,
        cost_estimate=cost(2 * BLOCK * mine * mine * k, 6 * BLOCK * mine * k),
        name="products",
    )(right, near, *lefts[half:])
    product = lax.all_to_all(product, in_part, 0, 0, tiled=True)

    return pl.pallas_call(
        final_kernel,
        in_specs=[vmem] * 6,
        out_specs=anywhere,
        out_shape=bfloat(*pair.shape),
        scratch_shapes=[pltpu.VMEM(pair.shape, bf16), pltpu.SemaphoreType.DMA((rows // 2,))],
        compiler_params=params(),
        cost_estimate=cost(2 * work * width, 6 * work),
        name="update",
    )(product, gate, row(center_gain), row(center_shift), out_weight, row(out_bias))


def solution(mesh):
    groups, chan, quarter = (mesh.shape[a] for a in ("groups", "chan", "quarter"))
    near = CHANNELS // BLOCK // quarter
    parts = chan // near
    split = Mesh(
        mesh.devices.reshape(groups, parts, near, quarter), ("groups", "part", "chan", "quarter")
    )
    rows = P(("groups", "part", "chan", "quarter"), None, None)
    return jax.shard_map(
        functools.partial(shards, parts),
        mesh=split,
        in_specs=(rows,) + (P(),) * 10,
        out_specs=rows,
        check_vma=False,
    )
```

```python
import functools

import jax
import jax.numpy as jnp
from jax import lax
from jax.experimental import pallas as pl
from jax.experimental.pallas import tpu as pltpu
from jax.sharding import Mesh
from jax.sharding import PartitionSpec as P

epsilon = 1e-05
CHANNELS = 128
BLOCK = 8
STEP = 4
SIZE = 32
LANES = 128
GATHER = 32
MIB = 1024 * 1024

f32, bf16 = jnp.float32, jnp.bfloat16


def sigmoid(x):
    return 0.5 * jnp.tanh(0.5 * x) + 0.5


def dot(a, b):
    return jnp.dot(a, b, preferred_element_type=f32)


def dot_nt(a, b):
    return lax.dot_general(a, b, (((1,), (1,)), ((), ())), preferred_element_type=f32)


def column(row):
    blocks = [
        jnp.broadcast_to(row[:, k : k + LANES], (LANES, LANES)).T
        for k in range(0, row.shape[1], LANES)
    ]
    return jnp.concatenate(blocks, axis=0)


def widen(col, width):
    return jnp.concatenate([col] * (width // LANES), axis=1)


def shuffle(groups, size):
    n = groups * size
    out = lax.broadcasted_iota(jnp.int32, (n, n), 0)
    row = lax.broadcasted_iota(jnp.int32, (n, n), 1)
    want = (out % size) * groups + out // size
    return jnp.where(want == row, 1.0, 0.0).astype(bf16)


def normalize(x, gain, shift):
    width = x.shape[1]
    ones = jnp.ones((width, width), bf16)
    centered = x.astype(f32) - dot(x, ones) * (1.0 / width)
    square = centered * centered
    high = square.astype(bf16)
    low = (square - high.astype(f32)).astype(bf16)
    variance = (dot(high, ones) + dot(low, ones)) * (1.0 / width)
    return (centered * lax.rsqrt(variance + epsilon) * gain + shift).astype(bf16)


def factor(normed, wt, bias):
    width = wt.shape[0] // 2
    both = dot_nt(wt, normed) + widen(bias, normed.shape[0])
    return sigmoid(both[:width]) * both[width:]


def as_rows(values, k):
    hosts = values.shape[0] // BLOCK
    return jnp.concatenate(
        [values[:, r * k : (r + 1) * k].reshape(hosts, BLOCK, k) for r in range(STEP)], axis=1
    )


def right_kernel(pair_ref, gain_ref, shift_ref, w_ref, b_ref, out_ref, wt, bt):
    @pl.when(pl.program_id(0) == 0)
    def _():
        wt[...] = w_ref[...].astype(f32).T.astype(bf16)
        bt[...] = column(b_ref[...])

    k, width = pair_ref.shape[1:]
    x = pair_ref[...].reshape(STEP * k, width)
    normed = normalize(x, gain_ref[...], shift_ref[...])
    out = as_rows(factor(normed, wt[...], bt[...]), k).astype(bf16)
    for p in range(out_ref.shape[0]):
        out_ref[p] = out


def left_kernel(pair_ref, gain_ref, shift_ref, w_ref, b_ref, gw_ref, gb_ref, *refs):
    wf, bf, wt, bt = refs[-4:]
    gate_ref = refs[-5]
    outs = refs[:-5]
    k, width = pair_ref.shape[1:]
    hidden = w_ref.shape[1] // 2

    @pl.when(pl.program_id(0) == 0)
    def _():
        wf[...] = w_ref[...].astype(f32).T
        bf[...] = column(b_ref[...])
        host = lax.axis_index(("chan", "quarter"))
        for half in range(2):
            for b in range(0, len(outs), 2):
                source = [
                    pl.ds(pl.multiple_of(half * hidden + (host ^ (b + n)) * BLOCK, BLOCK), BLOCK)
                    for n in range(2)
                ]
                target = slice(half * hidden + b * BLOCK, half * hidden + (b + 2) * BLOCK)
                wt[target] = jnp.concatenate([wf[s] for s in source], axis=0).astype(bf16)
                bt[target] = jnp.concatenate([bf[s] for s in source], axis=0)

    x = pair_ref[...].reshape(STEP * k, width)
    normed = normalize(x, gain_ref[...], shift_ref[...])
    gate = sigmoid(dot(normed, gw_ref[...]) + gb_ref[...])
    gate_ref[...] = gate.reshape(STEP, k, width).astype(bf16)
    rows = as_rows(factor(normed, wt[...], bt[...]), k).astype(bf16)
    for b, out in enumerate(outs):
        out[...] = rows[b]


def regroup(pieces, target, matrix):
    many = SIZE // STEP
    for s in range(len(pieces) // many):
        rows = jnp.concatenate([piece() for piece in pieces[s * many : (s + 1) * many]], axis=0)
        moved = dot(matrix, rows).astype(bf16)
        for c in range(BLOCK):
            target[c, s * SIZE : (s + 1) * SIZE, :] = moved[c * SIZE : (c + 1) * SIZE]


def slices(refs):
    tall = STEP * BLOCK
    return [
        functools.partial(lambda ref, at: ref[at : at + tall, :], ref, at)
        for ref in refs
        for at in range(0, ref.shape[0], tall)
    ]


def regroup_right_kernel(rows_ref, out_ref):
    regroup(slices([rows_ref]), out_ref, shuffle(BLOCK, SIZE))


def regroup_left_kernel(*refs):
    regroup(slices(refs[:-1]), refs[-1], shuffle(BLOCK, SIZE))


def product_kernel(right, near, *refs):
    lefts = refs[:-3]
    out_ref, far, held = refs[-3:]
    rows = lefts[0].shape[0] // BLOCK
    host = lax.axis_index(("chan", "quarter"))
    regroup(slices(lefts), far, shuffle(BLOCK, SIZE))
    for c in range(BLOCK):
        left = jnp.concatenate([near[c], far[c]], axis=0)
        held[c] = dot_nt(left, right[c]).astype(bf16)
    back = shuffle(SIZE, BLOCK)
    for s in range(held.shape[1] // SIZE):
        parts = jnp.concatenate([held[c, s * SIZE : (s + 1) * SIZE, :] for c in range(BLOCK)], axis=0)
        moved = dot(back, parts).astype(bf16)
        for i in range(0, SIZE, STEP):
            to, at = divmod(s * SIZE + i, rows)
            out_ref[host ^ to, at * BLOCK : (at + STEP) * BLOCK, :] = moved[
                i * BLOCK : (i + STEP) * BLOCK
            ]


def final_kernel(x_ref, gate_ref, g_ref, s_ref, w_ref, b_ref, out_ref, made, leave):
    hosts, _, j = x_ref.shape
    rows = gate_ref.shape[0]
    width = hosts * BLOCK
    gain, shift = widen(column(g_ref[...]), j), widen(column(s_ref[...]), j)
    stores = []
    for r in range(0, rows, 2):
        pair = x_ref[:, r * BLOCK : (r + 2) * BLOCK].astype(f32)
        for n in range(2):
            x = pair[:, n * BLOCK : (n + 1) * BLOCK].reshape(width, j)
            centered = x - jnp.mean(x, axis=0, keepdims=True)
            variance = jnp.mean(centered * centered, axis=0, keepdims=True)
            normed = centered * lax.rsqrt(variance + epsilon) * gain + shift
            outward = dot(normed.astype(bf16).T, w_ref[...]) + b_ref[...]
            made[r + n] = (gate_ref[r + n].astype(f32) * outward).astype(bf16)
        at = pl.ds(r, 2)
        stores.append(pltpu.make_async_copy(made.at[at], out_ref.at[at], leave.at[r // 2]))
        stores[-1].start()
    for store in stores:
        store.wait()


def whole(shape):
    return pl.BlockSpec(shape, lambda s: (0,) * len(shape))


def cost(flops, size):
    return pl.CostEstimate(flops=flops, bytes_accessed=size, transcendentals=0)


def params(mib=32):
    return pltpu.CompilerParams(vmem_limit_bytes=mib * MIB)


def shards(parts, pair, norm_gain, norm_shift, factor_weight, factor_bias, gate_weight, gate_bias,
           center_gain, center_shift, out_weight, out_bias):
    rows, k, width = pair.shape
    hidden = out_weight.shape[0]
    hosts = hidden // BLOCK
    steps = rows // STEP
    tall = rows * BLOCK
    mine = hosts * rows
    devices = parts * hosts
    in_part = ("chan", "quarter")
    everywhere = ("part",) + in_part
    row = lambda v: v.reshape(1, -1)
    row_block = pl.BlockSpec((STEP, k, width), lambda s: (s, 0, 0))
    work = rows * k * width
    bfloat = lambda *shape: jax.ShapeDtypeStruct(shape, bf16)

    vmem = pl.BlockSpec(memory_space=pltpu.VMEM)
    anywhere = pl.BlockSpec(memory_space=pl.ANY)
    right = pl.pallas_call(
        right_kernel,
        grid=(steps,),
        in_specs=[
            row_block,
            whole((1, width)),
            whole((1, width)),
            pl.BlockSpec((width, 2 * hidden), lambda s: (0, 1)),
            pl.BlockSpec((1, 2 * hidden), lambda s: (0, 1)),
        ],
        out_specs=pl.BlockSpec((parts, hosts, STEP * BLOCK, k), lambda s: (0, 0, s, 0)),
        out_shape=bfloat(parts, hosts, tall, k),
        scratch_shapes=[pltpu.VMEM((2 * hidden, width), bf16), pltpu.VMEM((2 * hidden, LANES), f32)],
        compiler_params=params(60),
        cost_estimate=cost(4 * work * hidden, 6 * work),
        name="right_factor",
    )(pair, row(norm_gain), row(norm_shift), factor_weight, row(factor_bias))
    right = lax.all_to_all(right.reshape(devices, tall, k), everywhere, 0, 0, tiled=True)

    def send(values, b):
        pairs = [(p * hosts + h, p * hosts + (h ^ b)) for p in range(parts) for h in range(hosts)]
        return lax.ppermute(values, everywhere, pairs)

    *lefts, gate = pl.pallas_call(
        left_kernel,
        grid=(steps,),
        in_specs=[
            row_block,
            whole((1, width)),
            whole((1, width)),
            whole((width, 2 * hidden)),
            whole((1, 2 * hidden)),
            whole((width, width)),
            whole((1, width)),
        ],
        out_specs=[pl.BlockSpec((STEP * BLOCK, k), lambda s: (s, 0))] * hosts + [row_block],
        out_shape=[bfloat(tall, k)] * hosts + [bfloat(*pair.shape)],
        scratch_shapes=[
            pltpu.VMEM((2 * hidden, width), f32),
            pltpu.VMEM((2 * hidden, LANES), f32),
            pltpu.VMEM((2 * hidden, width), bf16),
            pltpu.VMEM((2 * hidden, LANES), f32),
        ],
        compiler_params=params(),
        cost_estimate=cost(4 * work * hidden, 6 * work),
        name="left_factor",
    )(
        pair,
        row(norm_gain),
        row(norm_shift),
        factor_weight,
        row(factor_bias),
        gate_weight,
        row(gate_bias),
    )
    lefts = [lefts[0]] + [send(lefts[b], b) for b in reversed(range(1, hosts))][::-1]

    half = hosts // 2
    near = pl.pallas_call(
        regroup_left_kernel,
        in_specs=[vmem] * half,
        out_specs=vmem,
        out_shape=bfloat(BLOCK, mine // 2, k),
        compiler_params=params(),
        cost_estimate=cost(work * BLOCK * SIZE, 2 * work),
        name="regroup_left",
    )(*lefts[:half])

    span = GATHER * rows
    gathers = devices // GATHER
    grouped = pl.BlockSpec((BLOCK, span, k), lambda s: (0, s, 0))
    if gathers == 1:
        limit = params()
        blocks = dict(in_specs=[vmem], out_specs=vmem)
        rest = dict(in_specs=[vmem] * (2 + half), out_specs=vmem)
    else:
        limit = params(60)
        blocks = dict(
            grid=(gathers,),
            in_specs=[pl.BlockSpec((span * BLOCK, k), lambda s: (s, 0))],
            out_specs=grouped,
        )
        rest = dict(
            grid=(gathers,),
            in_specs=[grouped, whole((BLOCK, mine // 2, k))] + [whole((tall, k))] * half,
            out_specs=pl.BlockSpec((hosts, tall, span), lambda s: (0, 0, s)),
        )
    right = pl.pallas_call(
        regroup_right_kernel,
        **blocks,
        out_shape=bfloat(BLOCK, devices * rows, k),
        compiler_params=limit,
        cost_estimate=cost(1 << 37, 4 * devices * tall * k),
        name="regroup_right",
    )(right.reshape(devices * tall, k))
    product = pl.pallas_call(
        product_kernel,
        **rest,
        out_shape=bfloat(hosts, tall, devices * rows),
        scratch_shapes=[
            pltpu.VMEM((BLOCK, mine // 2, k), bf16),
            pltpu.VMEM((BLOCK, mine, span), bf16),
        ],
        compiler_params=limit,
        cost_estimate=cost(2 * BLOCK * mine * mine * k, 6 * BLOCK * mine * k),
        name="products",
    )(right, near, *lefts[half:])
    product = lax.all_to_all(product, in_part, 0, 0, tiled=True)

    return pl.pallas_call(
        final_kernel,
        in_specs=[vmem] * 6,
        out_specs=anywhere,
        out_shape=bfloat(*pair.shape),
        scratch_shapes=[pltpu.VMEM(pair.shape, bf16), pltpu.SemaphoreType.DMA((rows // 2,))],
        compiler_params=params(),
        cost_estimate=cost(2 * work * width, 6 * work),
        name="update",
    )(product, gate, row(center_gain), row(center_shift), out_weight, row(out_bias))


def solution(mesh):
    groups, chan, quarter = (mesh.shape[a] for a in ("groups", "chan", "quarter"))
    near = CHANNELS // BLOCK // quarter
    parts = chan // near
    split = Mesh(
        mesh.devices.reshape(groups, parts, near, quarter), ("groups", "part", "chan", "quarter")
    )
    rows = P(("groups", "part", "chan", "quarter"), None, None)
    return jax.shard_map(
        functools.partial(shards, parts),
        mesh=split,
        in_specs=(rows,) + (P(),) * 10,
        out_specs=rows,
        check_vma=False,
    )
```

```python
import functools

import jax
import jax.numpy as jnp
from jax import lax
from jax.experimental import pallas as pl
from jax.experimental.pallas import tpu as pltpu
from jax.sharding import Mesh
from jax.sharding import PartitionSpec as P

epsilon = 1e-05
CHANNELS = 128
BLOCK = 8
STEP = 4
SIZE = 32
LANES = 128
GATHER = 32
MIB = 1024 * 1024

f32, bf16 = jnp.float32, jnp.bfloat16


def sigmoid(x):
    return 0.5 * jnp.tanh(0.5 * x) + 0.5


def dot(a, b):
    return jnp.dot(a, b, preferred_element_type=f32)


def dot_nt(a, b):
    return lax.dot_general(a, b, (((1,), (1,)), ((), ())), preferred_element_type=f32)


def column(row):
    blocks = [
        jnp.broadcast_to(row[:, k : k + LANES], (LANES, LANES)).T
        for k in range(0, row.shape[1], LANES)
    ]
    return jnp.concatenate(blocks, axis=0)


def widen(col, width):
    return jnp.concatenate([col] * (width // LANES), axis=1)


def shuffle(groups, size):
    n = groups * size
    out = lax.broadcasted_iota(jnp.int32, (n, n), 0)
    row = lax.broadcasted_iota(jnp.int32, (n, n), 1)
    want = (out % size) * groups + out // size
    return jnp.where(want == row, 1.0, 0.0).astype(bf16)


def normalize(x, gain, shift):
    centered = x - jnp.mean(x, axis=1, keepdims=True)
    variance = jnp.mean(centered * centered, axis=1, keepdims=True)
    return (centered * lax.rsqrt(variance + epsilon) * gain + shift).astype(bf16)


def factor(normed, wt, bias):
    width = wt.shape[0] // 2
    both = dot_nt(wt, normed) + widen(bias, normed.shape[0])
    return sigmoid(both[:width]) * both[width:]


def as_rows(values, k):
    hosts = values.shape[0] // BLOCK
    return jnp.concatenate(
        [values[:, r * k : (r + 1) * k].reshape(hosts, BLOCK, k) for r in range(STEP)], axis=1
    )


def right_kernel(pair_ref, gain_ref, shift_ref, w_ref, b_ref, out_ref):
    k, width = pair_ref.shape[1:]
    half = w_ref.shape[1] // 2
    x = pair_ref[...].astype(f32).reshape(STEP * k, width)
    normed = normalize(x, gain_ref[...], shift_ref[...])
    both = dot(normed, w_ref[...]) + b_ref[...]
    values = sigmoid(both[:, :half]) * both[:, half:]
    out = as_rows(values.T, k).astype(bf16)
    for p in range(out_ref.shape[0]):
        out_ref[p] = out


def left_kernel(pair_ref, gain_ref, shift_ref, w_ref, b_ref, gw_ref, gb_ref, *refs):
    wf, bf, wt, bt = refs[-4:]
    gate_ref = refs[-5]
    outs = refs[:-5]
    k, width = pair_ref.shape[1:]
    hidden = w_ref.shape[1] // 2

    @pl.when(pl.program_id(0) == 0)
    def _():
        wf[...] = w_ref[...].astype(f32).T
        bf[...] = column(b_ref[...])
        host = lax.axis_index(("chan", "quarter"))
        for half in range(2):
            for b in range(0, len(outs), 2):
                source = [
                    pl.ds(pl.multiple_of(half * hidden + (host ^ (b + n)) * BLOCK, BLOCK), BLOCK)
                    for n in range(2)
                ]
                target = slice(half * hidden + b * BLOCK, half * hidden + (b + 2) * BLOCK)
                wt[target] = jnp.concatenate([wf[s] for s in source], axis=0).astype(bf16)
                bt[target] = jnp.concatenate([bf[s] for s in source], axis=0)

    x = pair_ref[...].astype(f32).reshape(STEP * k, width)
    normed = normalize(x, gain_ref[...], shift_ref[...])
    gate = sigmoid(dot(normed, gw_ref[...]) + gb_ref[...])
    gate_ref[...] = gate.reshape(STEP, k, width).astype(bf16)
    rows = as_rows(factor(normed, wt[...], bt[...]), k).astype(bf16)
    for b, out in enumerate(outs):
        out[...] = rows[b]


def regroup(pieces, target, matrix):
    many = SIZE // STEP
    for s in range(len(pieces) // many):
        rows = jnp.concatenate([piece() for piece in pieces[s * many : (s + 1) * many]], axis=0)
        moved = dot(matrix, rows).astype(bf16)
        for c in range(BLOCK):
            target[c, s * SIZE : (s + 1) * SIZE, :] = moved[c * SIZE : (c + 1) * SIZE]


def slices(refs):
    tall = STEP * BLOCK
    return [
        functools.partial(lambda ref, at: ref[at : at + tall, :], ref, at)
        for ref in refs
        for at in range(0, ref.shape[0], tall)
    ]


def regroup_right_kernel(rows_ref, out_ref):
    regroup(slices([rows_ref]), out_ref, shuffle(BLOCK, SIZE))


def regroup_left_kernel(*refs):
    regroup(slices(refs[:-1]), refs[-1], shuffle(BLOCK, SIZE))


def product_kernel(right, near, *refs):
    lefts = refs[:-3]
    out_ref, far, held = refs[-3:]
    rows = lefts[0].shape[0] // BLOCK
    host = lax.axis_index(("chan", "quarter"))
    regroup(slices(lefts), far, shuffle(BLOCK, SIZE))
    for c in range(BLOCK):
        left = jnp.concatenate([near[c], far[c]], axis=0)
        held[c] = dot_nt(left, right[c]).astype(bf16)
    back = shuffle(SIZE, BLOCK)
    for s in range(held.shape[1] // SIZE):
        parts = jnp.concatenate([held[c, s * SIZE : (s + 1) * SIZE, :] for c in range(BLOCK)], axis=0)
        moved = dot(back, parts).astype(bf16)
        for i in range(0, SIZE, STEP):
            to, at = divmod(s * SIZE + i, rows)
            out_ref[host ^ to, at * BLOCK : (at + STEP) * BLOCK, :] = moved[
                i * BLOCK : (i + STEP) * BLOCK
            ]


def final_kernel(x_ref, gate_ref, g_ref, s_ref, w_ref, b_ref, out_ref, made, leave):
    hosts, _, j = x_ref.shape
    rows = gate_ref.shape[0]
    width = hosts * BLOCK
    gain, shift = widen(column(g_ref[...]), j), widen(column(s_ref[...]), j)
    stores = []
    for r in range(0, rows, 2):
        pair = x_ref[:, r * BLOCK : (r + 2) * BLOCK].astype(f32)
        for n in range(2):
            x = pair[:, n * BLOCK : (n + 1) * BLOCK].reshape(width, j)
            centered = x - jnp.mean(x, axis=0, keepdims=True)
            variance = jnp.mean(centered * centered, axis=0, keepdims=True)
            normed = centered * lax.rsqrt(variance + epsilon) * gain + shift
            outward = dot(normed.astype(bf16).T, w_ref[...]) + b_ref[...]
            made[r + n] = (gate_ref[r + n].astype(f32) * outward).astype(bf16)
        at = pl.ds(r, 2)
        stores.append(pltpu.make_async_copy(made.at[at], out_ref.at[at], leave.at[r // 2]))
        stores[-1].start()
    for store in stores:
        store.wait()


def whole(shape):
    return pl.BlockSpec(shape, lambda s: (0,) * len(shape))


def cost(flops, size):
    return pl.CostEstimate(flops=flops, bytes_accessed=size, transcendentals=0)


def params(mib=32):
    return pltpu.CompilerParams(vmem_limit_bytes=mib * MIB)


def shards(parts, pair, norm_gain, norm_shift, factor_weight, factor_bias, gate_weight, gate_bias,
           center_gain, center_shift, out_weight, out_bias):
    rows, k, width = pair.shape
    hidden = out_weight.shape[0]
    hosts = hidden // BLOCK
    steps = rows // STEP
    tall = rows * BLOCK
    mine = hosts * rows
    devices = parts * hosts
    in_part = ("chan", "quarter")
    everywhere = ("part",) + in_part
    row = lambda v: v.reshape(1, -1)
    row_block = pl.BlockSpec((STEP, k, width), lambda s: (s, 0, 0))
    work = rows * k * width
    bfloat = lambda *shape: jax.ShapeDtypeStruct(shape, bf16)

    vmem = pl.BlockSpec(memory_space=pltpu.VMEM)
    anywhere = pl.BlockSpec(memory_space=pl.ANY)
    right = pl.pallas_call(
        right_kernel,
        grid=(steps,),
        in_specs=[
            row_block,
            whole((1, width)),
            whole((1, width)),
            pl.BlockSpec((width, 2 * hidden), lambda s: (0, 1)),
            pl.BlockSpec((1, 2 * hidden), lambda s: (0, 1)),
        ],
        out_specs=pl.BlockSpec((parts, hosts, STEP * BLOCK, k), lambda s: (0, 0, s, 0)),
        out_shape=bfloat(parts, hosts, tall, k),
        compiler_params=params(60),
        cost_estimate=cost(4 * work * hidden, 6 * work),
        name="right_factor",
    )(pair, row(norm_gain), row(norm_shift), factor_weight, row(factor_bias))
    right = lax.all_to_all(right.reshape(devices, tall, k), everywhere, 0, 0, tiled=True)

    def send(values, b):
        pairs = [(p * hosts + h, p * hosts + (h ^ b)) for p in range(parts) for h in range(hosts)]
        return lax.ppermute(values, everywhere, pairs)

    *lefts, gate = pl.pallas_call(
        left_kernel,
        grid=(steps,),
        in_specs=[
            row_block,
            whole((1, width)),
            whole((1, width)),
            whole((width, 2 * hidden)),
            whole((1, 2 * hidden)),
            whole((width, width)),
            whole((1, width)),
        ],
        out_specs=[pl.BlockSpec((STEP * BLOCK, k), lambda s: (s, 0))] * hosts + [row_block],
        out_shape=[bfloat(tall, k)] * hosts + [bfloat(*pair.shape)],
        scratch_shapes=[
            pltpu.VMEM((2 * hidden, width), f32),
            pltpu.VMEM((2 * hidden, LANES), f32),
            pltpu.VMEM((2 * hidden, width), bf16),
            pltpu.VMEM((2 * hidden, LANES), f32),
        ],
        compiler_params=params(),
        cost_estimate=cost(4 * work * hidden, 6 * work),
        name="left_factor",
    )(
        pair,
        row(norm_gain),
        row(norm_shift),
        factor_weight,
        row(factor_bias),
        gate_weight,
        row(gate_bias),
    )
    lefts = [lefts[0]] + [send(lefts[b], b) for b in reversed(range(1, hosts))][::-1]

    half = hosts // 2
    near = pl.pallas_call(
        regroup_left_kernel,
        in_specs=[vmem] * half,
        out_specs=vmem,
        out_shape=bfloat(BLOCK, mine // 2, k),
        compiler_params=params(),
        cost_estimate=cost(work * BLOCK * SIZE, 2 * work),
        name="regroup_left",
    )(*lefts[:half])

    span = GATHER * rows
    gathers = devices // GATHER
    grouped = pl.BlockSpec((BLOCK, span, k), lambda s: (0, s, 0))
    if gathers == 1:
        limit = params()
        blocks = dict(in_specs=[vmem], out_specs=vmem)
        rest = dict(in_specs=[vmem] * (2 + half), out_specs=vmem)
    else:
        limit = params(60)
        blocks = dict(
            grid=(gathers,),
            in_specs=[pl.BlockSpec((span * BLOCK, k), lambda s: (s, 0))],
            out_specs=grouped,
        )
        rest = dict(
            grid=(gathers,),
            in_specs=[grouped, whole((BLOCK, mine // 2, k))] + [whole((tall, k))] * half,
            out_specs=pl.BlockSpec((hosts, tall, span), lambda s: (0, 0, s)),
        )
    right = pl.pallas_call(
        regroup_right_kernel,
        **blocks,
        out_shape=bfloat(BLOCK, devices * rows, k),
        compiler_params=limit,
        cost_estimate=cost(1 << 37, 4 * devices * tall * k),
        name="regroup_right",
    )(right.reshape(devices * tall, k))
    product = pl.pallas_call(
        product_kernel,
        **rest,
        out_shape=bfloat(hosts, tall, devices * rows),
        scratch_shapes=[
            pltpu.VMEM((BLOCK, mine // 2, k), bf16),
            pltpu.VMEM((BLOCK, mine, span), bf16),
        ],
        compiler_params=limit,
        cost_estimate=cost(2 * BLOCK * mine * mine * k, 6 * BLOCK * mine * k),
        name="products",
    )(right, near, *lefts[half:])
    product = lax.all_to_all(product, in_part, 0, 0, tiled=True)

    return pl.pallas_call(
        final_kernel,
        in_specs=[vmem] * 6,
        out_specs=anywhere,
        out_shape=bfloat(*pair.shape),
        scratch_shapes=[pltpu.VMEM(pair.shape, bf16), pltpu.SemaphoreType.DMA((rows // 2,))],
        compiler_params=params(),
        cost_estimate=cost(2 * work * width, 6 * work),
        name="update",
    )(product, gate, row(center_gain), row(center_shift), out_weight, row(out_bias))


def solution(mesh):
    groups, chan, quarter = (mesh.shape[a] for a in ("groups", "chan", "quarter"))
    near = CHANNELS // BLOCK // quarter
    parts = chan // near
    split = Mesh(
        mesh.devices.reshape(groups, parts, near, quarter), ("groups", "part", "chan", "quarter")
    )
    rows = P(("groups", "part", "chan", "quarter"), None, None)
    return jax.shard_map(
        functools.partial(shards, parts),
        mesh=split,
        in_specs=(rows,) + (P(),) * 10,
        out_specs=rows,
        check_vma=False,
    )
```

```python
import functools

import jax
import jax.numpy as jnp
from jax import lax
from jax.experimental import pallas as pl
from jax.experimental.pallas import tpu as pltpu
from jax.sharding import Mesh
from jax.sharding import PartitionSpec as P

epsilon = 1e-05
CHANNELS = 128
BLOCK = 8
STEP = 4
SIZE = 32
LANES = 128
GATHER = 32
MIB = 1024 * 1024

f32, bf16 = jnp.float32, jnp.bfloat16


def sigmoid(x):
    return 0.5 * jnp.tanh(0.5 * x) + 0.5


def dot(a, b):
    return jnp.dot(a, b, preferred_element_type=f32)


def dot_nt(a, b):
    return lax.dot_general(a, b, (((1,), (1,)), ((), ())), preferred_element_type=f32)


def column(row):
    blocks = [
        jnp.broadcast_to(row[:, k : k + LANES], (LANES, LANES)).T
        for k in range(0, row.shape[1], LANES)
    ]
    return jnp.concatenate(blocks, axis=0)


def widen(col, width):
    return jnp.concatenate([col] * (width // LANES), axis=1)


def shuffle(groups, size):
    n = groups * size
    out = lax.broadcasted_iota(jnp.int32, (n, n), 0)
    row = lax.broadcasted_iota(jnp.int32, (n, n), 1)
    want = (out % size) * groups + out // size
    return jnp.where(want == row, 1.0, 0.0).astype(bf16)


def normalize(x, gain, shift):
    centered = x - jnp.mean(x, axis=1, keepdims=True)
    variance = jnp.mean(centered * centered, axis=1, keepdims=True)
    return (centered * lax.rsqrt(variance + epsilon) * gain + shift).astype(bf16)


def factor(normed, wt, bias):
    width = wt.shape[0] // 2
    both = dot_nt(wt, normed) + widen(bias, normed.shape[0])
    return sigmoid(both[:width]) * both[width:]


def as_rows(values, k):
    hosts = values.shape[0] // BLOCK
    return jnp.concatenate(
        [values[:, r * k : (r + 1) * k].reshape(hosts, BLOCK, k) for r in range(STEP)], axis=1
    )


def right_kernel(pair_ref, gain_ref, shift_ref, w_ref, b_ref, out_ref):
    k, width = pair_ref.shape[1:]
    half = w_ref.shape[1] // 2
    x = pair_ref[...].astype(f32).reshape(STEP * k, width)
    normed = normalize(x, gain_ref[...], shift_ref[...])
    both = dot(normed, w_ref[...]) + b_ref[...]
    values = sigmoid(both[:, :half]) * both[:, half:]
    out = as_rows(values.T, k).astype(bf16)
    for p in range(out_ref.shape[0]):
        out_ref[p] = out


def left_kernel(pair_ref, gain_ref, shift_ref, w_ref, b_ref, gw_ref, gb_ref, *refs):
    wf, bf, wt, bt = refs[-4:]
    gate_ref = refs[-5]
    outs = refs[:-5]
    k, width = pair_ref.shape[1:]
    hidden = w_ref.shape[1] // 2

    @pl.when(pl.program_id(0) == 0)
    def _():
        wf[...] = w_ref[...].astype(f32).T
        bf[...] = column(b_ref[...])
        host = lax.axis_index(("chan", "quarter"))
        for half in range(2):
            for b in range(0, len(outs), 2):
                source = [
                    pl.ds(pl.multiple_of(half * hidden + (host ^ (b + n)) * BLOCK, BLOCK), BLOCK)
                    for n in range(2)
                ]
                target = slice(half * hidden + b * BLOCK, half * hidden + (b + 2) * BLOCK)
                wt[target] = jnp.concatenate([wf[s] for s in source], axis=0).astype(bf16)
                bt[target] = jnp.concatenate([bf[s] for s in source], axis=0)

    x = pair_ref[...].astype(f32).reshape(STEP * k, width)
    normed = normalize(x, gain_ref[...], shift_ref[...])
    gate = sigmoid(dot(normed, gw_ref[...]) + gb_ref[...])
    gate_ref[...] = gate.reshape(STEP, k, width).astype(bf16)
    rows = as_rows(factor(normed, wt[...], bt[...]), k).astype(bf16)
    for b, out in enumerate(outs):
        out[...] = rows[b]


def regroup(pieces, target, matrix):
    many = SIZE // STEP
    for s in range(len(pieces) // many):
        rows = jnp.concatenate([piece() for piece in pieces[s * many : (s + 1) * many]], axis=0)
        moved = dot(matrix, rows).astype(bf16)
        for c in range(BLOCK):
            target[c, s * SIZE : (s + 1) * SIZE, :] = moved[c * SIZE : (c + 1) * SIZE]


def slices(refs):
    tall = STEP * BLOCK
    return [
        functools.partial(lambda ref, at: ref[at : at + tall, :], ref, at)
        for ref in refs
        for at in range(0, ref.shape[0], tall)
    ]


def regroup_left_kernel(*refs):
    regroup(slices(refs[:-1]), refs[-1], shuffle(BLOCK, SIZE))


def multiply(left, right, held, store):
    for c in range(BLOCK):
        held[c] = dot_nt(left[c], right[c]).astype(bf16)
    back = shuffle(SIZE, BLOCK)
    for s in range(held.shape[1] // SIZE):
        parts = jnp.concatenate([held[c, s * SIZE : (s + 1) * SIZE, :] for c in range(BLOCK)], axis=0)
        moved = dot(back, parts).astype(bf16)
        for i in range(0, SIZE, STEP):
            store(s * SIZE + i, moved[i * BLOCK : (i + STEP) * BLOCK])


def near_kernel(rows_ref, left, out_ref, right, held):
    regroup(slices([rows_ref]), right, shuffle(BLOCK, SIZE))
    rows = left.shape[1] // out_ref.shape[0]

    def store(i, values):
        to, at = divmod(i, rows)
        out_ref[to, at * BLOCK : (at + STEP) * BLOCK, :] = values

    multiply(left, right, held, store)


def far_again_kernel(rows_ref, near_ref, *refs):
    regroup(slices([rows_ref]), refs[-1], shuffle(BLOCK, SIZE))
    far_kernel(refs[-1], near_ref, *refs[:-1])


def far_kernel(right, near_ref, *refs):
    lefts = refs[:-4]
    out_ref, left, held, sems = refs[-4:]
    half = len(lefts)
    rows = lefts[0].shape[0] // BLOCK
    host = lax.axis_index(("chan", "quarter"))
    copies = [
        pltpu.make_async_copy(near_ref.at[b], out_ref.at[host ^ b], sems.at[b]) for b in range(half)
    ]
    for copy in copies:
        copy.start()
    regroup(slices(lefts), left, shuffle(BLOCK, SIZE))

    def store(i, values):
        to, at = divmod(i, rows)
        out_ref[host ^ (half + to), at * BLOCK : (at + STEP) * BLOCK, :] = values

    multiply(left, right, held, store)
    for copy in copies:
        copy.wait()


def final_kernel(x_ref, gate_ref, g_ref, s_ref, w_ref, b_ref, out_ref, made, leave):
    hosts, _, j = x_ref.shape
    rows = gate_ref.shape[0]
    width = hosts * BLOCK
    gain, shift = widen(column(g_ref[...]), j), widen(column(s_ref[...]), j)
    stores = []
    for r in range(0, rows, 2):
        pair = x_ref[:, r * BLOCK : (r + 2) * BLOCK].astype(f32)
        for n in range(2):
            x = pair[:, n * BLOCK : (n + 1) * BLOCK].reshape(width, j)
            centered = x - jnp.mean(x, axis=0, keepdims=True)
            variance = jnp.mean(centered * centered, axis=0, keepdims=True)
            normed = centered * lax.rsqrt(variance + epsilon) * gain + shift
            outward = dot(normed.astype(bf16).T, w_ref[...]) + b_ref[...]
            made[r + n] = (gate_ref[r + n].astype(f32) * outward).astype(bf16)
        at = pl.ds(r, 2)
        stores.append(pltpu.make_async_copy(made.at[at], out_ref.at[at], leave.at[r // 2]))
        stores[-1].start()
    for store in stores:
        store.wait()


def whole(shape):
    return pl.BlockSpec(shape, lambda s: (0,) * len(shape))


def cost(flops, size):
    return pl.CostEstimate(flops=flops, bytes_accessed=size, transcendentals=0)


def params(mib=32):
    return pltpu.CompilerParams(vmem_limit_bytes=mib * MIB)


def shards(parts, pair, norm_gain, norm_shift, factor_weight, factor_bias, gate_weight, gate_bias,
           center_gain, center_shift, out_weight, out_bias):
    rows, k, width = pair.shape
    hidden = out_weight.shape[0]
    hosts = hidden // BLOCK
    steps = rows // STEP
    tall = rows * BLOCK
    mine = hosts * rows
    devices = parts * hosts
    in_part = ("chan", "quarter")
    everywhere = ("part",) + in_part
    row = lambda v: v.reshape(1, -1)
    row_block = pl.BlockSpec((STEP, k, width), lambda s: (s, 0, 0))
    work = rows * k * width
    bfloat = lambda *shape: jax.ShapeDtypeStruct(shape, bf16)

    vmem = pl.BlockSpec(memory_space=pltpu.VMEM)
    anywhere = pl.BlockSpec(memory_space=pl.ANY)
    right = pl.pallas_call(
        right_kernel,
        grid=(steps,),
        in_specs=[
            row_block,
            whole((1, width)),
            whole((1, width)),
            pl.BlockSpec((width, 2 * hidden), lambda s: (0, 1)),
            pl.BlockSpec((1, 2 * hidden), lambda s: (0, 1)),
        ],
        out_specs=pl.BlockSpec((parts, hosts, STEP * BLOCK, k), lambda s: (0, 0, s, 0)),
        out_shape=bfloat(parts, hosts, tall, k),
        compiler_params=params(60),
        cost_estimate=cost(4 * work * hidden, 6 * work),
        name="right_factor",
    )(pair, row(norm_gain), row(norm_shift), factor_weight, row(factor_bias))
    right = lax.all_to_all(right.reshape(devices, tall, k), everywhere, 0, 0, tiled=True)

    def send(values, b):
        pairs = [(p * hosts + h, p * hosts + (h ^ b)) for p in range(parts) for h in range(hosts)]
        return lax.ppermute(values, everywhere, pairs)

    *lefts, gate = pl.pallas_call(
        left_kernel,
        grid=(steps,),
        in_specs=[
            row_block,
            whole((1, width)),
            whole((1, width)),
            whole((width, 2 * hidden)),
            whole((1, 2 * hidden)),
            whole((width, width)),
            whole((1, width)),
        ],
        out_specs=[pl.BlockSpec((STEP * BLOCK, k), lambda s: (s, 0))] * hosts + [row_block],
        out_shape=[bfloat(tall, k)] * hosts + [bfloat(*pair.shape)],
        scratch_shapes=[
            pltpu.VMEM((2 * hidden, width), f32),
            pltpu.VMEM((2 * hidden, LANES), f32),
            pltpu.VMEM((2 * hidden, width), bf16),
            pltpu.VMEM((2 * hidden, LANES), f32),
        ],
        compiler_params=params(),
        cost_estimate=cost(4 * work * hidden, 6 * work),
        name="left_factor",
    )(
        pair,
        row(norm_gain),
        row(norm_shift),
        factor_weight,
        row(factor_bias),
        gate_weight,
        row(gate_bias),
    )
    lefts = [lefts[0]] + [send(lefts[b], b) for b in reversed(range(1, hosts))][::-1]

    half = hosts // 2
    near = pl.pallas_call(
        regroup_left_kernel,
        in_specs=[vmem] * half,
        out_specs=vmem,
        out_shape=bfloat(BLOCK, mine // 2, k),
        compiler_params=params(),
        cost_estimate=cost(work * BLOCK * SIZE, 2 * work),
        name="regroup_left",
    )(*lefts[:half])

    span = GATHER * rows
    gathers = devices // GATHER
    right = right.reshape(devices * tall, k)
    part = bfloat(half, tall, devices * rows)
    spent = BLOCK * mine * mine * k
    held = pltpu.VMEM((BLOCK, mine // 2, span), bf16)
    scratch = [pltpu.VMEM((BLOCK, mine // 2, k), bf16), held, pltpu.SemaphoreType.DMA((half,))]
    if gathers == 1:
        limit = params()
        early = dict(
            in_specs=[vmem] * 2,
            out_specs=[vmem] * 2,
            out_shape=[part, bfloat(BLOCK, devices * rows, k)],
            scratch_shapes=[held],
        )
        rest = dict(in_specs=[vmem] * (2 + half), out_specs=vmem, scratch_shapes=scratch)
    else:
        limit = params(60)
        regrouped = [pltpu.VMEM((BLOCK, span, k), bf16)]
        block = pl.BlockSpec((span * BLOCK, k), lambda s: (s, 0))
        part_block = pl.BlockSpec((half, tall, span), lambda s: (0, 0, s))
        early = dict(
            grid=(gathers,),
            in_specs=[block, whole((BLOCK, mine // 2, k))],
            out_specs=[part_block],
            out_shape=[part],
            scratch_shapes=regrouped + [held],
        )
        rest = dict(
            grid=(gathers,),
            in_specs=[block, part_block] + [whole((tall, k))] * half,
            out_specs=pl.BlockSpec((hosts, tall, span), lambda s: (0, 0, s)),
            scratch_shapes=scratch + regrouped,
        )
    near, *regrouped = pl.pallas_call(
        near_kernel,
        **early,
        compiler_params=limit,
        cost_estimate=cost(1 << 37, 6 * BLOCK * mine * k),
        name="near_products",
    )(right, near)
    product = pl.pallas_call(
        far_kernel if regrouped else far_again_kernel,
        **rest,
        out_shape=bfloat(hosts, tall, devices * rows),
        compiler_params=limit,
        cost_estimate=cost(spent, 6 * BLOCK * mine * k),
        name="far_products",
    )(*regrouped or [right], near, *lefts[half:])
    product = lax.all_to_all(product, in_part, 0, 0, tiled=True)

    return pl.pallas_call(
        final_kernel,
        in_specs=[vmem] * 6,
        out_specs=anywhere,
        out_shape=bfloat(*pair.shape),
        scratch_shapes=[pltpu.VMEM(pair.shape, bf16), pltpu.SemaphoreType.DMA((rows // 2,))],
        compiler_params=params(),
        cost_estimate=cost(2 * work * width, 6 * work),
        name="update",
    )(product, gate, row(center_gain), row(center_shift), out_weight, row(out_bias))


def solution(mesh):
    groups, chan, quarter = (mesh.shape[a] for a in ("groups", "chan", "quarter"))
    near = CHANNELS // BLOCK // quarter
    parts = chan // near
    split = Mesh(
        mesh.devices.reshape(groups, parts, near, quarter), ("groups", "part", "chan", "quarter")
    )
    rows = P(("groups", "part", "chan", "quarter"), None, None)
    return jax.shard_map(
        functools.partial(shards, parts),
        mesh=split,
        in_specs=(rows,) + (P(),) * 10,
        out_specs=rows,
        check_vma=False,
    )
```

```python
import functools

import jax
import jax.numpy as jnp
from jax import lax
from jax.experimental import pallas as pl
from jax.experimental.pallas import tpu as pltpu
from jax.sharding import Mesh
from jax.sharding import PartitionSpec as P

epsilon = 1e-05
CHANNELS = 128
BLOCK = 8
STEP = 4
PAIRED = 2
SIZE = 32
LANES = 128
GATHER = 32
MIB = 1024 * 1024

f32, bf16 = jnp.float32, jnp.bfloat16


def sigmoid(x):
    return 0.5 * jnp.tanh(0.5 * x) + 0.5


def dot(a, b):
    return jnp.dot(a, b, preferred_element_type=f32)


def dot_nt(a, b):
    return lax.dot_general(a, b, (((1,), (1,)), ((), ())), preferred_element_type=f32)


def column(row):
    blocks = [
        jnp.broadcast_to(row[:, k : k + LANES], (LANES, LANES)).T
        for k in range(0, row.shape[1], LANES)
    ]
    return jnp.concatenate(blocks, axis=0)


def widen(col, width):
    return jnp.concatenate([col] * (width // LANES), axis=1)


def shuffle(groups, size):
    n = groups * size
    out = lax.broadcasted_iota(jnp.int32, (n, n), 0)
    row = lax.broadcasted_iota(jnp.int32, (n, n), 1)
    want = (out % size) * groups + out // size
    return jnp.where(want == row, 1.0, 0.0).astype(bf16)


def normalize(x, gain, shift):
    centered = x - jnp.mean(x, axis=1, keepdims=True)
    variance = jnp.mean(centered * centered, axis=1, keepdims=True)
    return (centered * lax.rsqrt(variance + epsilon) * gain + shift).astype(bf16)


def factor(normed, wt, bias):
    width = wt.shape[0] // 2
    both = dot_nt(wt, normed) + widen(bias, normed.shape[0])
    return sigmoid(both[:width]) * both[width:]


def as_rows(values, k, step=STEP):
    hosts = values.shape[0] // BLOCK
    return jnp.concatenate(
        [values[:, r * k : (r + 1) * k].reshape(hosts, BLOCK, k) for r in range(step)], axis=1
    )


def turns_of(rows):
    cuts = [0, PAIRED, *range(PAIRED + STEP, rows - PAIRED + 1, STEP), rows]
    return list(zip(cuts[:-1], (n - m for m, n in zip(cuts[:-1], cuts[1:]))))


def right_kernel(
    pair_ref, gain_ref, shift_ref, w_ref, b_ref, out_ref, pair, gain, shift, w, bias, made,
    arrive, leave, sems,
):
    rows, k, width = pair.shape
    half = w.shape[1]
    turns = turns_of(rows)
    loads = [
        pltpu.make_async_copy(pair_ref.at[pl.ds(r, size)], pair.at[pl.ds(r, size)], arrive.at[n])
        for n, (r, size) in enumerate(turns)
    ]
    small = [
        pltpu.make_async_copy(ref, to, sems.at[n])
        for n, (ref, to) in enumerate(
            [
                (w_ref.at[:, pl.ds(half, half)], w),
                (b_ref.at[:, pl.ds(half, half)], bias),
                (gain_ref, gain),
                (shift_ref, shift),
            ]
        )
    ]
    for copy in loads[:1] + small + loads[1:]:
        copy.start()
    for copy in small:
        copy.wait()
    stores = []
    for n, (r, size) in enumerate(turns):
        loads[n].wait()
        x = pair[r : r + size].astype(f32).reshape(size * k, width)
        normed = normalize(x, gain[...], shift[...])
        at = pl.ds(r * BLOCK, size * BLOCK)
        both = dot(normed, w[...]) + bias[...]
        values = sigmoid(both[:, : half // 2]) * both[:, half // 2 :]
        made[:, at, :] = as_rows(values.T, k, size).astype(bf16)
        for p in range(out_ref.shape[0]):
            stores.append(
                pltpu.make_async_copy(made.at[:, at, :], out_ref.at[p, :, at, :], leave.at[p, n])
            )
            stores[-1].start()
    for store in stores:
        store.wait()


def left_kernel(pair_ref, gain_ref, shift_ref, w_ref, b_ref, gw_ref, gb_ref, *refs):
    wf, bf, wt, bt = refs[-4:]
    gate_ref = refs[-5]
    outs = refs[:-5]
    k, width = pair_ref.shape[1:]
    hidden = w_ref.shape[1] // 2

    @pl.when(pl.program_id(0) == 0)
    def _():
        wf[...] = w_ref[...].astype(f32).T
        bf[...] = column(b_ref[...])
        host = lax.axis_index(("chan", "quarter"))
        for half in range(2):
            for b in range(0, len(outs), 2):
                source = [
                    pl.ds(pl.multiple_of(half * hidden + (host ^ (b + n)) * BLOCK, BLOCK), BLOCK)
                    for n in range(2)
                ]
                target = slice(half * hidden + b * BLOCK, half * hidden + (b + 2) * BLOCK)
                wt[target] = jnp.concatenate([wf[s] for s in source], axis=0).astype(bf16)
                bt[target] = jnp.concatenate([bf[s] for s in source], axis=0)

    x = pair_ref[...].astype(f32).reshape(STEP * k, width)
    normed = normalize(x, gain_ref[...], shift_ref[...])
    gate = sigmoid(dot(normed, gw_ref[...]) + gb_ref[...])
    gate_ref[...] = gate.reshape(STEP, k, width).astype(bf16)
    rows = as_rows(factor(normed, wt[...], bt[...]), k).astype(bf16)
    for b, out in enumerate(outs):
        out[...] = rows[b]


def regroup(pieces, target, matrix):
    many = SIZE // STEP
    for s in range(len(pieces) // many):
        rows = jnp.concatenate([piece() for piece in pieces[s * many : (s + 1) * many]], axis=0)
        moved = dot(matrix, rows).astype(bf16)
        for c in range(BLOCK):
            target[c, s * SIZE : (s + 1) * SIZE, :] = moved[c * SIZE : (c + 1) * SIZE]


def slices(refs):
    tall = STEP * BLOCK
    return [
        functools.partial(lambda ref, at: ref[at : at + tall, :], ref, at)
        for ref in refs
        for at in range(0, ref.shape[0], tall)
    ]


def regroup_right_kernel(rows_ref, out_ref):
    regroup(slices([rows_ref]), out_ref, shuffle(BLOCK, SIZE))


def regroup_left_kernel(*refs):
    regroup(slices(refs[:-1]), refs[-1], shuffle(BLOCK, SIZE))


def product_kernel(right, near, *refs):
    lefts = refs[:-3]
    out_ref, far, held = refs[-3:]
    rows = lefts[0].shape[0] // BLOCK
    host = lax.axis_index(("chan", "quarter"))
    regroup(slices(lefts), far, shuffle(BLOCK, SIZE))
    for c in range(BLOCK):
        left = jnp.concatenate([near[c], far[c]], axis=0)
        held[c] = dot_nt(left, right[c]).astype(bf16)
    back = shuffle(SIZE, BLOCK)
    for s in range(held.shape[1] // SIZE):
        parts = jnp.concatenate([held[c, s * SIZE : (s + 1) * SIZE, :] for c in range(BLOCK)], axis=0)
        moved = dot(back, parts).astype(bf16)
        for i in range(0, SIZE, STEP):
            to, at = divmod(s * SIZE + i, rows)
            out_ref[host ^ to, at * BLOCK : (at + STEP) * BLOCK, :] = moved[
                i * BLOCK : (i + STEP) * BLOCK
            ]


def final_kernel(x_ref, gate_ref, g_ref, s_ref, w_ref, b_ref, out_ref, made, leave):
    hosts, _, j = x_ref.shape
    rows = gate_ref.shape[0]
    width = hosts * BLOCK
    gain, shift = widen(column(g_ref[...]), j), widen(column(s_ref[...]), j)
    stores = []
    for r in range(0, rows, 2):
        pair = x_ref[:, r * BLOCK : (r + 2) * BLOCK].astype(f32)
        for n in range(2):
            x = pair[:, n * BLOCK : (n + 1) * BLOCK].reshape(width, j)
            centered = x - jnp.mean(x, axis=0, keepdims=True)
            variance = jnp.mean(centered * centered, axis=0, keepdims=True)
            normed = centered * lax.rsqrt(variance + epsilon) * gain + shift
            outward = dot(normed.astype(bf16).T, w_ref[...]) + b_ref[...]
            made[r + n] = (gate_ref[r + n].astype(f32) * outward).astype(bf16)
        at = pl.ds(r, 2)
        stores.append(pltpu.make_async_copy(made.at[at], out_ref.at[at], leave.at[r // 2]))
        stores[-1].start()
    for store in stores:
        store.wait()


def whole(shape):
    return pl.BlockSpec(shape, lambda s: (0,) * len(shape))


def cost(flops, size):
    return pl.CostEstimate(flops=flops, bytes_accessed=size, transcendentals=0)


def params(mib=32):
    return pltpu.CompilerParams(vmem_limit_bytes=mib * MIB)


def shards(parts, pair, norm_gain, norm_shift, factor_weight, factor_bias, gate_weight, gate_bias,
           center_gain, center_shift, out_weight, out_bias):
    rows, k, width = pair.shape
    hidden = out_weight.shape[0]
    hosts = hidden // BLOCK
    steps = rows // STEP
    tall = rows * BLOCK
    mine = hosts * rows
    devices = parts * hosts
    in_part = ("chan", "quarter")
    everywhere = ("part",) + in_part
    row = lambda v: v.reshape(1, -1)
    row_block = pl.BlockSpec((STEP, k, width), lambda s: (s, 0, 0))
    work = rows * k * width
    bfloat = lambda *shape: jax.ShapeDtypeStruct(shape, bf16)

    vmem = pl.BlockSpec(memory_space=pltpu.VMEM)
    anywhere = pl.BlockSpec(memory_space=pl.ANY)
    turns = len(turns_of(rows))
    right = pl.pallas_call(
        right_kernel,
        in_specs=[anywhere] * 5,
        out_specs=anywhere,
        out_shape=bfloat(parts, hosts, tall, k),
        scratch_shapes=[
            pltpu.VMEM((rows, k, width), bf16),
            pltpu.VMEM((1, width), f32),
            pltpu.VMEM((1, width), f32),
            pltpu.VMEM((width, 2 * hidden), bf16),
            pltpu.VMEM((1, 2 * hidden), f32),
            pltpu.VMEM((hosts, tall, k), bf16),
            pltpu.SemaphoreType.DMA((turns,)),
            pltpu.SemaphoreType.DMA((parts, turns)),
            pltpu.SemaphoreType.DMA((4,)),
        ],
        compiler_params=params(60),
        cost_estimate=cost(4 * work * hidden, 6 * work),
        name="right_factor",
    )(pair, row(norm_gain), row(norm_shift), factor_weight, row(factor_bias))
    right = lax.all_to_all(right.reshape(devices, tall, k), everywhere, 0, 0, tiled=True)

    def send(values, b):
        pairs = [(p * hosts + h, p * hosts + (h ^ b)) for p in range(parts) for h in range(hosts)]
        return lax.ppermute(values, everywhere, pairs)

    *lefts, gate = pl.pallas_call(
        left_kernel,
        grid=(steps,),
        in_specs=[
            row_block,
            whole((1, width)),
            whole((1, width)),
            whole((width, 2 * hidden)),
            whole((1, 2 * hidden)),
            whole((width, width)),
            whole((1, width)),
        ],
        out_specs=[pl.BlockSpec((STEP * BLOCK, k), lambda s: (s, 0))] * hosts + [row_block],
        out_shape=[bfloat(tall, k)] * hosts + [bfloat(*pair.shape)],
        scratch_shapes=[
            pltpu.VMEM((2 * hidden, width), f32),
            pltpu.VMEM((2 * hidden, LANES), f32),
            pltpu.VMEM((2 * hidden, width), bf16),
            pltpu.VMEM((2 * hidden, LANES), f32),
        ],
        compiler_params=params(),
        cost_estimate=cost(4 * work * hidden, 6 * work),
        name="left_factor",
    )(
        pair,
        row(norm_gain),
        row(norm_shift),
        factor_weight,
        row(factor_bias),
        gate_weight,
        row(gate_bias),
    )
    lefts = [lefts[0]] + [send(lefts[b], b) for b in reversed(range(1, hosts))][::-1]

    half = hosts // 2
    near = pl.pallas_call(
        regroup_left_kernel,
        in_specs=[vmem] * half,
        out_specs=vmem,
        out_shape=bfloat(BLOCK, mine // 2, k),
        compiler_params=params(),
        cost_estimate=cost(work * BLOCK * SIZE, 2 * work),
        name="regroup_left",
    )(*lefts[:half])

    span = GATHER * rows
    gathers = devices // GATHER
    grouped = pl.BlockSpec((BLOCK, span, k), lambda s: (0, s, 0))
    if gathers == 1:
        limit = params()
        blocks = dict(in_specs=[vmem], out_specs=vmem)
        rest = dict(in_specs=[vmem] * (2 + half), out_specs=vmem)
    else:
        limit = params(60)
        blocks = dict(
            grid=(gathers,),
            in_specs=[pl.BlockSpec((span * BLOCK, k), lambda s: (s, 0))],
            out_specs=grouped,
        )
        rest = dict(
            grid=(gathers,),
            in_specs=[grouped, whole((BLOCK, mine // 2, k))] + [whole((tall, k))] * half,
            out_specs=pl.BlockSpec((hosts, tall, span), lambda s: (0, 0, s)),
        )
    right = pl.pallas_call(
        regroup_right_kernel,
        **blocks,
        out_shape=bfloat(BLOCK, devices * rows, k),
        compiler_params=limit,
        cost_estimate=cost(1 << 37, 4 * devices * tall * k),
        name="regroup_right",
    )(right.reshape(devices * tall, k))
    product = pl.pallas_call(
        product_kernel,
        **rest,
        out_shape=bfloat(hosts, tall, devices * rows),
        scratch_shapes=[
            pltpu.VMEM((BLOCK, mine // 2, k), bf16),
            pltpu.VMEM((BLOCK, mine, span), bf16),
        ],
        compiler_params=limit,
        cost_estimate=cost(2 * BLOCK * mine * mine * k, 6 * BLOCK * mine * k),
        name="products",
    )(right, near, *lefts[half:])
    product = lax.all_to_all(product, in_part, 0, 0, tiled=True)

    return pl.pallas_call(
        final_kernel,
        in_specs=[vmem] * 6,
        out_specs=anywhere,
        out_shape=bfloat(*pair.shape),
        scratch_shapes=[pltpu.VMEM(pair.shape, bf16), pltpu.SemaphoreType.DMA((rows // 2,))],
        compiler_params=params(),
        cost_estimate=cost(2 * work * width, 6 * work),
        name="update",
    )(product, gate, row(center_gain), row(center_shift), out_weight, row(out_bias))


def solution(mesh):
    groups, chan, quarter = (mesh.shape[a] for a in ("groups", "chan", "quarter"))
    near = CHANNELS // BLOCK // quarter
    parts = chan // near
    split = Mesh(
        mesh.devices.reshape(groups, parts, near, quarter), ("groups", "part", "chan", "quarter")
    )
    rows = P(("groups", "part", "chan", "quarter"), None, None)
    return jax.shard_map(
        functools.partial(shards, parts),
        mesh=split,
        in_specs=(rows,) + (P(),) * 10,
        out_specs=rows,
        check_vma=False,
    )
```

```python
import functools

import jax
import jax.numpy as jnp
from jax import lax
from jax.experimental import pallas as pl
from jax.experimental.pallas import tpu as pltpu
from jax.sharding import Mesh
from jax.sharding import PartitionSpec as P

epsilon = 1e-05
CHANNELS = 128
BLOCK = 8
STEP = 4
PAIRED = 2
SIZE = 32
LANES = 128
GATHER = 32
MIB = 1024 * 1024

f32, bf16 = jnp.float32, jnp.bfloat16


def sigmoid(x):
    return 0.5 * jnp.tanh(0.5 * x) + 0.5


def dot(a, b):
    return jnp.dot(a, b, preferred_element_type=f32)


def dot_nt(a, b):
    return lax.dot_general(a, b, (((1,), (1,)), ((), ())), preferred_element_type=f32)


def column(row):
    blocks = [
        jnp.broadcast_to(row[:, k : k + LANES], (LANES, LANES)).T
        for k in range(0, row.shape[1], LANES)
    ]
    return jnp.concatenate(blocks, axis=0)


def widen(col, width):
    return jnp.concatenate([col] * (width // LANES), axis=1)


def shuffle(groups, size):
    n = groups * size
    out = lax.broadcasted_iota(jnp.int32, (n, n), 0)
    row = lax.broadcasted_iota(jnp.int32, (n, n), 1)
    want = (out % size) * groups + out // size
    return jnp.where(want == row, 1.0, 0.0).astype(bf16)


def normalize(x, gain, shift):
    centered = x - jnp.mean(x, axis=1, keepdims=True)
    variance = jnp.mean(centered * centered, axis=1, keepdims=True)
    return (centered * lax.rsqrt(variance + epsilon) * gain + shift).astype(bf16)


def factor(normed, wt, bias):
    width = wt.shape[0] // 2
    both = dot_nt(wt, normed) + widen(bias, normed.shape[0])
    return sigmoid(both[:width]) * both[width:]


def as_rows(values, k, step=STEP):
    hosts = values.shape[0] // BLOCK
    return jnp.concatenate(
        [values[:, r * k : (r + 1) * k].reshape(hosts, BLOCK, k) for r in range(step)], axis=1
    )


def right_kernel(pair_ref, gain_ref, shift_ref, w_ref, b_ref, out_ref):
    k, width = pair_ref.shape[1:]
    half = w_ref.shape[1] // 2
    x = pair_ref[...].astype(f32).reshape(PAIRED * k, width)
    normed = normalize(x, gain_ref[...], shift_ref[...])
    both = dot(normed, w_ref[...]) + b_ref[...]
    values = sigmoid(both[:, :half]) * both[:, half:]
    out = as_rows(values.T, k, PAIRED).astype(bf16)
    for p in range(out_ref.shape[0]):
        out_ref[p] = out


def left_kernel(pair_ref, gain_ref, shift_ref, w_ref, b_ref, gw_ref, gb_ref, *refs):
    wf, bf, wt, bt = refs[-4:]
    gate_ref = refs[-5]
    outs = refs[:-5]
    k, width = pair_ref.shape[1:]
    hidden = w_ref.shape[1] // 2

    @pl.when(pl.program_id(0) == 0)
    def _():
        wf[...] = w_ref[...].astype(f32).T
        bf[...] = column(b_ref[...])
        host = lax.axis_index(("chan", "quarter"))
        for half in range(2):
            for b in range(0, len(outs), 2):
                source = [
                    pl.ds(pl.multiple_of(half * hidden + (host ^ (b + n)) * BLOCK, BLOCK), BLOCK)
                    for n in range(2)
                ]
                target = slice(half * hidden + b * BLOCK, half * hidden + (b + 2) * BLOCK)
                wt[target] = jnp.concatenate([wf[s] for s in source], axis=0).astype(bf16)
                bt[target] = jnp.concatenate([bf[s] for s in source], axis=0)

    x = pair_ref[...].astype(f32).reshape(STEP * k, width)
    normed = normalize(x, gain_ref[...], shift_ref[...])
    gate = sigmoid(dot(normed, gw_ref[...]) + gb_ref[...])
    gate_ref[...] = gate.reshape(STEP, k, width).astype(bf16)
    rows = as_rows(factor(normed, wt[...], bt[...]), k).astype(bf16)
    for b, out in enumerate(outs):
        out[...] = rows[b]


def regroup(pieces, target, matrix):
    many = SIZE // STEP
    for s in range(len(pieces) // many):
        rows = jnp.concatenate([piece() for piece in pieces[s * many : (s + 1) * many]], axis=0)
        moved = dot(matrix, rows).astype(bf16)
        for c in range(BLOCK):
            target[c, s * SIZE : (s + 1) * SIZE, :] = moved[c * SIZE : (c + 1) * SIZE]


def slices(refs):
    tall = STEP * BLOCK
    return [
        functools.partial(lambda ref, at: ref[at : at + tall, :], ref, at)
        for ref in refs
        for at in range(0, ref.shape[0], tall)
    ]


def regroup_right_kernel(rows_ref, out_ref):
    regroup(slices([rows_ref]), out_ref, shuffle(BLOCK, SIZE))


def regroup_left_kernel(*refs):
    regroup(slices(refs[:-1]), refs[-1], shuffle(BLOCK, SIZE))


def product_kernel(right, near, *refs):
    lefts = refs[:-3]
    out_ref, far, held = refs[-3:]
    rows = lefts[0].shape[0] // BLOCK
    host = lax.axis_index(("chan", "quarter"))
    regroup(slices(lefts), far, shuffle(BLOCK, SIZE))
    for c in range(BLOCK):
        left = jnp.concatenate([near[c], far[c]], axis=0)
        held[c] = dot_nt(left, right[c]).astype(bf16)
    back = shuffle(SIZE, BLOCK)
    for s in range(held.shape[1] // SIZE):
        parts = jnp.concatenate([held[c, s * SIZE : (s + 1) * SIZE, :] for c in range(BLOCK)], axis=0)
        moved = dot(back, parts).astype(bf16)
        for i in range(0, SIZE, STEP):
            to, at = divmod(s * SIZE + i, rows)
            out_ref[host ^ to, at * BLOCK : (at + STEP) * BLOCK, :] = moved[
                i * BLOCK : (i + STEP) * BLOCK
            ]


def final_kernel(x_ref, gate_ref, g_ref, s_ref, w_ref, b_ref, out_ref, made, leave):
    hosts, _, j = x_ref.shape
    rows = gate_ref.shape[0]
    width = hosts * BLOCK
    gain, shift = widen(column(g_ref[...]), j), widen(column(s_ref[...]), j)
    stores = []
    for r in range(0, rows, 2):
        pair = x_ref[:, r * BLOCK : (r + 2) * BLOCK].astype(f32)
        for n in range(2):
            x = pair[:, n * BLOCK : (n + 1) * BLOCK].reshape(width, j)
            centered = x - jnp.mean(x, axis=0, keepdims=True)
            variance = jnp.mean(centered * centered, axis=0, keepdims=True)
            normed = centered * lax.rsqrt(variance + epsilon) * gain + shift
            outward = dot(normed.astype(bf16).T, w_ref[...]) + b_ref[...]
            made[r + n] = (gate_ref[r + n].astype(f32) * outward).astype(bf16)
        at = pl.ds(r, 2)
        stores.append(pltpu.make_async_copy(made.at[at], out_ref.at[at], leave.at[r // 2]))
        stores[-1].start()
    for store in stores:
        store.wait()


def whole(shape):
    return pl.BlockSpec(shape, lambda s: (0,) * len(shape))


def cost(flops, size):
    return pl.CostEstimate(flops=flops, bytes_accessed=size, transcendentals=0)


def params(mib=32):
    return pltpu.CompilerParams(vmem_limit_bytes=mib * MIB)


def shards(parts, pair, norm_gain, norm_shift, factor_weight, factor_bias, gate_weight, gate_bias,
           center_gain, center_shift, out_weight, out_bias):
    rows, k, width = pair.shape
    hidden = out_weight.shape[0]
    hosts = hidden // BLOCK
    steps = rows // STEP
    tall = rows * BLOCK
    mine = hosts * rows
    devices = parts * hosts
    in_part = ("chan", "quarter")
    everywhere = ("part",) + in_part
    row = lambda v: v.reshape(1, -1)
    row_block = pl.BlockSpec((STEP, k, width), lambda s: (s, 0, 0))
    work = rows * k * width
    bfloat = lambda *shape: jax.ShapeDtypeStruct(shape, bf16)

    vmem = pl.BlockSpec(memory_space=pltpu.VMEM)
    anywhere = pl.BlockSpec(memory_space=pl.ANY)
    right = pl.pallas_call(
        right_kernel,
        grid=(rows // PAIRED,),
        in_specs=[
            pl.BlockSpec((PAIRED, k, width), lambda s: (s, 0, 0)),
            whole((1, width)),
            whole((1, width)),
            pl.BlockSpec((width, 2 * hidden), lambda s: (0, 1)),
            pl.BlockSpec((1, 2 * hidden), lambda s: (0, 1)),
        ],
        out_specs=pl.BlockSpec((parts, hosts, PAIRED * BLOCK, k), lambda s: (0, 0, s, 0)),
        out_shape=bfloat(parts, hosts, tall, k),
        compiler_params=params(60),
        cost_estimate=cost(4 * work * hidden, 6 * work),
        name="right_factor",
    )(pair, row(norm_gain), row(norm_shift), factor_weight, row(factor_bias))
    right = lax.all_to_all(right.reshape(devices, tall, k), everywhere, 0, 0, tiled=True)

    def send(values, b):
        pairs = [(p * hosts + h, p * hosts + (h ^ b)) for p in range(parts) for h in range(hosts)]
        return lax.ppermute(values, everywhere, pairs)

    *lefts, gate = pl.pallas_call(
        left_kernel,
        grid=(steps,),
        in_specs=[
            row_block,
            whole((1, width)),
            whole((1, width)),
            whole((width, 2 * hidden)),
            whole((1, 2 * hidden)),
            whole((width, width)),
            whole((1, width)),
        ],
        out_specs=[pl.BlockSpec((STEP * BLOCK, k), lambda s: (s, 0))] * hosts + [row_block],
        out_shape=[bfloat(tall, k)] * hosts + [bfloat(*pair.shape)],
        scratch_shapes=[
            pltpu.VMEM((2 * hidden, width), f32),
            pltpu.VMEM((2 * hidden, LANES), f32),
            pltpu.VMEM((2 * hidden, width), bf16),
            pltpu.VMEM((2 * hidden, LANES), f32),
        ],
        compiler_params=params(),
        cost_estimate=cost(4 * work * hidden, 6 * work),
        name="left_factor",
    )(
        pair,
        row(norm_gain),
        row(norm_shift),
        factor_weight,
        row(factor_bias),
        gate_weight,
        row(gate_bias),
    )
    lefts = [lefts[0]] + [send(lefts[b], b) for b in reversed(range(1, hosts))][::-1]

    half = hosts // 2
    near = pl.pallas_call(
        regroup_left_kernel,
        in_specs=[vmem] * half,
        out_specs=vmem,
        out_shape=bfloat(BLOCK, mine // 2, k),
        compiler_params=params(),
        cost_estimate=cost(work * BLOCK * SIZE, 2 * work),
        name="regroup_left",
    )(*lefts[:half])

    span = GATHER * rows
    gathers = devices // GATHER
    grouped = pl.BlockSpec((BLOCK, span, k), lambda s: (0, s, 0))
    if gathers == 1:
        limit = params()
        blocks = dict(in_specs=[vmem], out_specs=vmem)
        rest = dict(in_specs=[vmem] * (2 + half), out_specs=vmem)
    else:
        limit = params(60)
        blocks = dict(
            grid=(gathers,),
            in_specs=[pl.BlockSpec((span * BLOCK, k), lambda s: (s, 0))],
            out_specs=grouped,
        )
        rest = dict(
            grid=(gathers,),
            in_specs=[grouped, whole((BLOCK, mine // 2, k))] + [whole((tall, k))] * half,
            out_specs=pl.BlockSpec((hosts, tall, span), lambda s: (0, 0, s)),
        )
    right = pl.pallas_call(
        regroup_right_kernel,
        **blocks,
        out_shape=bfloat(BLOCK, devices * rows, k),
        compiler_params=limit,
        cost_estimate=cost(1 << 37, 4 * devices * tall * k),
        name="regroup_right",
    )(right.reshape(devices * tall, k))
    product = pl.pallas_call(
        product_kernel,
        **rest,
        out_shape=bfloat(hosts, tall, devices * rows),
        scratch_shapes=[
            pltpu.VMEM((BLOCK, mine // 2, k), bf16),
            pltpu.VMEM((BLOCK, mine, span), bf16),
        ],
        compiler_params=limit,
        cost_estimate=cost(2 * BLOCK * mine * mine * k, 6 * BLOCK * mine * k),
        name="products",
    )(right, near, *lefts[half:])
    product = lax.all_to_all(product, in_part, 0, 0, tiled=True)

    return pl.pallas_call(
        final_kernel,
        in_specs=[vmem] * 6,
        out_specs=anywhere,
        out_shape=bfloat(*pair.shape),
        scratch_shapes=[pltpu.VMEM(pair.shape, bf16), pltpu.SemaphoreType.DMA((rows // 2,))],
        compiler_params=params(),
        cost_estimate=cost(2 * work * width, 6 * work),
        name="update",
    )(product, gate, row(center_gain), row(center_shift), out_weight, row(out_bias))


def solution(mesh):
    groups, chan, quarter = (mesh.shape[a] for a in ("groups", "chan", "quarter"))
    near = CHANNELS // BLOCK // quarter
    parts = chan // near
    split = Mesh(
        mesh.devices.reshape(groups, parts, near, quarter), ("groups", "part", "chan", "quarter")
    )
    rows = P(("groups", "part", "chan", "quarter"), None, None)
    return jax.shard_map(
        functools.partial(shards, parts),
        mesh=split,
        in_specs=(rows,) + (P(),) * 10,
        out_specs=rows,
        check_vma=False,
    )
```

```python
import functools

import jax
import jax.numpy as jnp
from jax import lax
from jax.experimental import pallas as pl
from jax.experimental.pallas import tpu as pltpu
from jax.sharding import Mesh
from jax.sharding import PartitionSpec as P

epsilon = 1e-05
CHANNELS = 128
BLOCK = 8
STEP = 4
PAIRED = 6
SIZE = 32
LANES = 128
GATHER = 32
MIB = 1024 * 1024

f32, bf16 = jnp.float32, jnp.bfloat16


def sigmoid(x):
    return 0.5 * jnp.tanh(0.5 * x) + 0.5


def dot(a, b):
    return jnp.dot(a, b, preferred_element_type=f32)


def dot_nt(a, b):
    return lax.dot_general(a, b, (((1,), (1,)), ((), ())), preferred_element_type=f32)


def column(row):
    blocks = [
        jnp.broadcast_to(row[:, k : k + LANES], (LANES, LANES)).T
        for k in range(0, row.shape[1], LANES)
    ]
    return jnp.concatenate(blocks, axis=0)


def widen(col, width):
    return jnp.concatenate([col] * (width // LANES), axis=1)


def shuffle(groups, size):
    n = groups * size
    out = lax.broadcasted_iota(jnp.int32, (n, n), 0)
    row = lax.broadcasted_iota(jnp.int32, (n, n), 1)
    want = (out % size) * groups + out // size
    return jnp.where(want == row, 1.0, 0.0).astype(bf16)


def normalize(x, gain, shift):
    centered = x - jnp.mean(x, axis=1, keepdims=True)
    variance = jnp.mean(centered * centered, axis=1, keepdims=True)
    return (centered * lax.rsqrt(variance + epsilon) * gain + shift).astype(bf16)


def factor(normed, wt, bias):
    width = wt.shape[0] // 2
    both = dot_nt(wt, normed) + widen(bias, normed.shape[0])
    return sigmoid(both[:width]) * both[width:]


def as_rows(values, k, step=STEP):
    hosts = values.shape[0] // BLOCK
    return jnp.concatenate(
        [values[:, r * k : (r + 1) * k].reshape(hosts, BLOCK, k) for r in range(step)], axis=1
    )


def right_kernel(pair_ref, gain_ref, shift_ref, w_ref, b_ref, out_ref):
    k, width = pair_ref.shape[1:]
    half = w_ref.shape[1] // 2
    x = pair_ref[...].astype(f32).reshape(PAIRED * k, width)
    normed = normalize(x, gain_ref[...], shift_ref[...])
    both = dot(normed, w_ref[...]) + b_ref[...]
    values = sigmoid(both[:, :half]) * both[:, half:]
    out = as_rows(values.T, k, PAIRED).astype(bf16)
    for p in range(out_ref.shape[0]):
        out_ref[p] = out


def left_kernel(pair_ref, gain_ref, shift_ref, w_ref, b_ref, gw_ref, gb_ref, *refs):
    wf, bf, wt, bt = refs[-4:]
    gate_ref = refs[-5]
    outs = refs[:-5]
    k, width = pair_ref.shape[1:]
    hidden = w_ref.shape[1] // 2

    @pl.when(pl.program_id(0) == 0)
    def _():
        wf[...] = w_ref[...].astype(f32).T
        bf[...] = column(b_ref[...])
        host = lax.axis_index(("chan", "quarter"))
        for half in range(2):
            for b in range(0, len(outs), 2):
                source = [
                    pl.ds(pl.multiple_of(half * hidden + (host ^ (b + n)) * BLOCK, BLOCK), BLOCK)
                    for n in range(2)
                ]
                target = slice(half * hidden + b * BLOCK, half * hidden + (b + 2) * BLOCK)
                wt[target] = jnp.concatenate([wf[s] for s in source], axis=0).astype(bf16)
                bt[target] = jnp.concatenate([bf[s] for s in source], axis=0)

    x = pair_ref[...].astype(f32).reshape(STEP * k, width)
    normed = normalize(x, gain_ref[...], shift_ref[...])
    gate = sigmoid(dot(normed, gw_ref[...]) + gb_ref[...])
    gate_ref[...] = gate.reshape(STEP, k, width).astype(bf16)
    rows = as_rows(factor(normed, wt[...], bt[...]), k).astype(bf16)
    for b, out in enumerate(outs):
        out[...] = rows[b]


def regroup(pieces, target, matrix):
    many = SIZE // STEP
    for s in range(len(pieces) // many):
        rows = jnp.concatenate([piece() for piece in pieces[s * many : (s + 1) * many]], axis=0)
        moved = dot(matrix, rows).astype(bf16)
        for c in range(BLOCK):
            target[c, s * SIZE : (s + 1) * SIZE, :] = moved[c * SIZE : (c + 1) * SIZE]


def slices(refs):
    tall = STEP * BLOCK
    return [
        functools.partial(lambda ref, at: ref[at : at + tall, :], ref, at)
        for ref in refs
        for at in range(0, ref.shape[0], tall)
    ]


def regroup_right_kernel(rows_ref, out_ref):
    regroup(slices([rows_ref]), out_ref, shuffle(BLOCK, SIZE))


def regroup_left_kernel(*refs):
    regroup(slices(refs[:-1]), refs[-1], shuffle(BLOCK, SIZE))


def product_kernel(right, near, *refs):
    lefts = refs[:-3]
    out_ref, far, held = refs[-3:]
    rows = lefts[0].shape[0] // BLOCK
    host = lax.axis_index(("chan", "quarter"))
    regroup(slices(lefts), far, shuffle(BLOCK, SIZE))
    for c in range(BLOCK):
        left = jnp.concatenate([near[c], far[c]], axis=0)
        held[c] = dot_nt(left, right[c]).astype(bf16)
    back = shuffle(SIZE, BLOCK)
    for s in range(held.shape[1] // SIZE):
        parts = jnp.concatenate([held[c, s * SIZE : (s + 1) * SIZE, :] for c in range(BLOCK)], axis=0)
        moved = dot(back, parts).astype(bf16)
        for i in range(0, SIZE, STEP):
            to, at = divmod(s * SIZE + i, rows)
            out_ref[host ^ to, at * BLOCK : (at + STEP) * BLOCK, :] = moved[
                i * BLOCK : (i + STEP) * BLOCK
            ]


def final_kernel(x_ref, gate_ref, g_ref, s_ref, w_ref, b_ref, out_ref, made, leave):
    hosts, _, j = x_ref.shape
    rows = gate_ref.shape[0]
    width = hosts * BLOCK
    gain, shift = widen(column(g_ref[...]), j), widen(column(s_ref[...]), j)
    stores = []
    for r in range(0, rows, 2):
        pair = x_ref[:, r * BLOCK : (r + 2) * BLOCK].astype(f32)
        for n in range(2):
            x = pair[:, n * BLOCK : (n + 1) * BLOCK].reshape(width, j)
            centered = x - jnp.mean(x, axis=0, keepdims=True)
            variance = jnp.mean(centered * centered, axis=0, keepdims=True)
            normed = centered * lax.rsqrt(variance + epsilon) * gain + shift
            outward = dot(normed.astype(bf16).T, w_ref[...]) + b_ref[...]
            made[r + n] = (gate_ref[r + n].astype(f32) * outward).astype(bf16)
        at = pl.ds(r, 2)
        stores.append(pltpu.make_async_copy(made.at[at], out_ref.at[at], leave.at[r // 2]))
        stores[-1].start()
    for store in stores:
        store.wait()


def whole(shape):
    return pl.BlockSpec(shape, lambda s: (0,) * len(shape))


def cost(flops, size):
    return pl.CostEstimate(flops=flops, bytes_accessed=size, transcendentals=0)


def params(mib=32):
    return pltpu.CompilerParams(vmem_limit_bytes=mib * MIB)


def shards(parts, pair, norm_gain, norm_shift, factor_weight, factor_bias, gate_weight, gate_bias,
           center_gain, center_shift, out_weight, out_bias):
    rows, k, width = pair.shape
    hidden = out_weight.shape[0]
    hosts = hidden // BLOCK
    steps = rows // STEP
    tall = rows * BLOCK
    mine = hosts * rows
    devices = parts * hosts
    in_part = ("chan", "quarter")
    everywhere = ("part",) + in_part
    row = lambda v: v.reshape(1, -1)
    row_block = pl.BlockSpec((STEP, k, width), lambda s: (s, 0, 0))
    work = rows * k * width
    bfloat = lambda *shape: jax.ShapeDtypeStruct(shape, bf16)

    vmem = pl.BlockSpec(memory_space=pltpu.VMEM)
    anywhere = pl.BlockSpec(memory_space=pl.ANY)
    right = pl.pallas_call(
        right_kernel,
        grid=(rows // PAIRED,),
        in_specs=[
            pl.BlockSpec((PAIRED, k, width), lambda s: (s, 0, 0)),
            whole((1, width)),
            whole((1, width)),
            pl.BlockSpec((width, 2 * hidden), lambda s: (0, 1)),
            pl.BlockSpec((1, 2 * hidden), lambda s: (0, 1)),
        ],
        out_specs=pl.BlockSpec((parts, hosts, PAIRED * BLOCK, k), lambda s: (0, 0, s, 0)),
        out_shape=bfloat(parts, hosts, tall, k),
        compiler_params=params(60),
        cost_estimate=cost(4 * work * hidden, 6 * work),
        name="right_factor",
    )(pair, row(norm_gain), row(norm_shift), factor_weight, row(factor_bias))
    right = lax.all_to_all(right.reshape(devices, tall, k), everywhere, 0, 0, tiled=True)

    def send(values, b):
        pairs = [(p * hosts + h, p * hosts + (h ^ b)) for p in range(parts) for h in range(hosts)]
        return lax.ppermute(values, everywhere, pairs)

    *lefts, gate = pl.pallas_call(
        left_kernel,
        grid=(steps,),
        in_specs=[
            row_block,
            whole((1, width)),
            whole((1, width)),
            whole((width, 2 * hidden)),
            whole((1, 2 * hidden)),
            whole((width, width)),
            whole((1, width)),
        ],
        out_specs=[pl.BlockSpec((STEP * BLOCK, k), lambda s: (s, 0))] * hosts + [row_block],
        out_shape=[bfloat(tall, k)] * hosts + [bfloat(*pair.shape)],
        scratch_shapes=[
            pltpu.VMEM((2 * hidden, width), f32),
            pltpu.VMEM((2 * hidden, LANES), f32),
            pltpu.VMEM((2 * hidden, width), bf16),
            pltpu.VMEM((2 * hidden, LANES), f32),
        ],
        compiler_params=params(),
        cost_estimate=cost(4 * work * hidden, 6 * work),
        name="left_factor",
    )(
        pair,
        row(norm_gain),
        row(norm_shift),
        factor_weight,
        row(factor_bias),
        gate_weight,
        row(gate_bias),
    )
    lefts = [lefts[0]] + [send(lefts[b], b) for b in reversed(range(1, hosts))][::-1]

    half = hosts // 2
    near = pl.pallas_call(
        regroup_left_kernel,
        in_specs=[vmem] * half,
        out_specs=vmem,
        out_shape=bfloat(BLOCK, mine // 2, k),
        compiler_params=params(),
        cost_estimate=cost(work * BLOCK * SIZE, 2 * work),
        name="regroup_left",
    )(*lefts[:half])

    span = GATHER * rows
    gathers = devices // GATHER
    grouped = pl.BlockSpec((BLOCK, span, k), lambda s: (0, s, 0))
    if gathers == 1:
        limit = params()
        blocks = dict(in_specs=[vmem], out_specs=vmem)
        rest = dict(in_specs=[vmem] * (2 + half), out_specs=vmem)
    else:
        limit = params(60)
        blocks = dict(
            grid=(gathers,),
            in_specs=[pl.BlockSpec((span * BLOCK, k), lambda s: (s, 0))],
            out_specs=grouped,
        )
        rest = dict(
            grid=(gathers,),
            in_specs=[grouped, whole((BLOCK, mine // 2, k))] + [whole((tall, k))] * half,
            out_specs=pl.BlockSpec((hosts, tall, span), lambda s: (0, 0, s)),
        )
    right = pl.pallas_call(
        regroup_right_kernel,
        **blocks,
        out_shape=bfloat(BLOCK, devices * rows, k),
        compiler_params=limit,
        cost_estimate=cost(1 << 37, 4 * devices * tall * k),
        name="regroup_right",
    )(right.reshape(devices * tall, k))
    product = pl.pallas_call(
        product_kernel,
        **rest,
        out_shape=bfloat(hosts, tall, devices * rows),
        scratch_shapes=[
            pltpu.VMEM((BLOCK, mine // 2, k), bf16),
            pltpu.VMEM((BLOCK, mine, span), bf16),
        ],
        compiler_params=limit,
        cost_estimate=cost(2 * BLOCK * mine * mine * k, 6 * BLOCK * mine * k),
        name="products",
    )(right, near, *lefts[half:])
    product = lax.all_to_all(product, in_part, 0, 0, tiled=True)

    return pl.pallas_call(
        final_kernel,
        in_specs=[vmem] * 6,
        out_specs=anywhere,
        out_shape=bfloat(*pair.shape),
        scratch_shapes=[pltpu.VMEM(pair.shape, bf16), pltpu.SemaphoreType.DMA((rows // 2,))],
        compiler_params=params(),
        cost_estimate=cost(2 * work * width, 6 * work),
        name="update",
    )(product, gate, row(center_gain), row(center_shift), out_weight, row(out_bias))


def solution(mesh):
    groups, chan, quarter = (mesh.shape[a] for a in ("groups", "chan", "quarter"))
    near = CHANNELS // BLOCK // quarter
    parts = chan // near
    split = Mesh(
        mesh.devices.reshape(groups, parts, near, quarter), ("groups", "part", "chan", "quarter")
    )
    rows = P(("groups", "part", "chan", "quarter"), None, None)
    return jax.shard_map(
        functools.partial(shards, parts),
        mesh=split,
        in_specs=(rows,) + (P(),) * 10,
        out_specs=rows,
        check_vma=False,
    )
```
